32 devices in a mesh: dp: 8 (over y, x, core), head: 4 (over z).
Axes of the slice: x: 2, y: 2, z: 4, core: 2. Of those that a mesh axis runs over, the one named last changes fastest.
Arguments:
- series: bfloat16 [32768, 512], P(('dp', 'head')), may hold values from -6 to 6
- target: float32 [32768, 512], P(('dp', 'head')), may hold values from -6 to 6
- valid: int32 [32768], P(('dp', 'head')), may hold values from 0 to 1
- window_id: int32 [256, 128], P(('dp', 'head')), may hold values from 0 to 3, never falling along the last dimension, each value on 1 to 48 neighbouring positions
- mode_index: int32 [8, 64], P('head'), may hold values from 0 to 64, as said below
- query_weight: float32 [512, 512], P(None, 'head'), may hold values from -0.25 to 0.25
- query_first: float32 [512, 512], P(None, 'head'), may hold values from -4.7683716e-06 to 4.7683716e-06
- query_second: float32 [512, 512], P(None, 'head'), may hold values from 5.867866e-14 to 2.3471465e-13
- out_weight: float32 [512, 512], P('head'), may hold values from -0.25 to 0.25
- out_first: float32 [512, 512], P('head'), may hold values from -4.7683716e-06 to 4.7683716e-06
- out_second: float32 [512, 512], P('head'), may hold values from 5.867866e-14 to 2.3471465e-13
- mode_weight: float32 [2, 8, 64, 4096], P(None, 'head'), may hold values from -0.36 to 0.36
- mode_first: float32 [2, 8, 64, 4096], P(None, 'head'), may hold values from -4.7683716e-06 to 4.7683716e-06
- mode_second: float32 [2, 8, 64, 4096], P(None, 'head'), may hold values from 5.867866e-14 to 2.3471465e-13
- up_weight: float32 [512, 2048], P(None, 'head'), may hold values from -0.25 to 0.25
- up_first: float32 [512, 2048], P(None, 'head'), may hold values from -4.7683716e-06 to 4.7683716e-06
- up_second: float32 [512, 2048], P(None, 'head'), may hold values from 5.867866e-14 to 2.3471465e-13
- down_weight: float32 [2048, 512], P('head'), may hold values from -0.125 to 0.125
- down_first: float32 [2048, 512], P('head'), may hold values from -4.7683716e-06 to 4.7683716e-06
- down_second: float32 [2048, 512], P('head'), may hold values from 5.867866e-14 to 2.3471465e-13
- bias_pair: float32 [2, 512], replicated, may hold values from -3 to 3
- bias_first: float32 [2, 512], replicated, may hold values from -4.7683716e-06 to 4.7683716e-06
- bias_second: float32 [2, 512], replicated, may hold values from 5.867866e-14 to 2.3471465e-13
- decomp_params: float32 [2, 2, 5], replicated, may hold values from -3 to 3
- decomp_first: float32 [2, 2, 5], replicated, may hold values from -4.7683716e-06 to 4.7683716e-06
- decomp_second: float32 [2, 2, 5], replicated, may hold values from 5.867866e-14 to 2.3471465e-13
Outputs:
- loss_sum: float32 [], replicated
- valid_count: float32 [], replicated
- grad_norm: float32 [], replicated
- query_weight_new: float32 [512, 512], P(None, 'head')
- query_first_new: float32 [512, 512], P(None, 'head')
- query_second_new: float32 [512, 512], P(None, 'head')
- out_weight_new: float32 [512, 512], P('head')
- out_first_new: float32 [512, 512], P('head')
- out_second_new: float32 [512, 512], P('head')
- mode_weight_new: float32 [2, 8, 64, 4096], P(None, 'head')
- mode_first_new: float32 [2, 8, 64, 4096], P(None, 'head')
- mode_second_new: float32 [2, 8, 64, 4096], P(None, 'head')
- up_weight_new: float32 [512, 2048], P(None, 'head')
- up_first_new: float32 [512, 2048], P(None, 'head')
- up_second_new: float32 [512, 2048], P(None, 'head')
- down_weight_new: float32 [2048, 512], P('head')
- down_first_new: float32 [2048, 512], P('head')
- down_second_new: float32 [2048, 512], P('head')
- bias_pair_new: float32 [2, 512], replicated
- bias_first_new: float32 [2, 512], replicated
- bias_second_new: float32 [2, 512], replicated
- decomp_params_new: float32 [2, 2, 5], replicated
- decomp_first_new: float32 [2, 2, 5], replicated
- decomp_second_new: float32 [2, 2, 5], replicated
The draws below stay inside these ranges and needn't reach their ends.
Inputs may be any that keep to these rules, and one draw needn't show every extreme that they name: `mode_index`: each head's list names 64 different frequencies. `window_id`: along a context the window numbers never fall; every window holds 1 to 48 steps.
All inputs are finite; a program needn't handle non-finite values.
Results may differ from the reference program's by a relative error of at most 0.0022.
Values may be sent and summed in bfloat16 or wider, within the bound.
No kernel may reach another device: no remote copies, remote signals or barrier semaphores. Data moves between devices by JAX's collectives and lax.ppermute only.
A program may use at most 256 MiB of HBM per device.

```python
import math
import jax
import jax.numpy as jnp
import numpy as np
from jax import lax

D = 512
FF = 2048
HEADS = 8
HEAD_DIM = 64
MODES = 64
SEQ_LEN = 128
KERNELS = 5
WINDOWS = 4
CTX_DEV = 32
MICRO = 2
STEP = 10
CONTEXTS = 256
ROWS = 32768
PARAMS = 6816788


def draw_valid(key, part):
    key = jax.random.fold_in(key, 7)
    ticket = jax.random.randint(key, (ROWS,), 0, 1000)
    limit = 250 + 500 * jnp.arange(ROWS, dtype=jnp.int32) // ROWS
    return (ticket < limit).astype(jnp.int32)


def draw_mode_index(key, part):
    key = jax.random.fold_in(key, 5)
    keys = jax.random.split(key, HEADS)
    picks = jax.vmap(lambda single: jax.random.permutation(single, SEQ_LEN // 2 + 1)[:MODES])(keys)
    return picks.astype(jnp.int32)


def steps_of(own_key, dims, cuts, smallest, high):
    loudness = 1.0
    for dim, parts in cuts:
        heights = jax.random.uniform(jax.random.fold_in(jax.random.fold_in(own_key, 6), dim), (parts,), jnp.float32, smallest / len(cuts), high / len(cuts))
        loudness = loudness * jnp.repeat(jnp.exp(heights), dims[dim] // parts).reshape((-1,) + (1,) * (len(dims) - 1 - dim))
    return loudness


def profile(count, total, bound, slope):
    portions = [(1 << 20) // math.isqrt(standing ** slope) + 1 for standing in range(2, count + 1)]
    surplus, given = total - bound - (count - 1), [1] * (count - 1)
    while surplus > 0:
        candidates = [i for i in range(count - 1) if given[i] < bound]
        pool, left = sum([portions[i] for i in candidates]), surplus
        for i in candidates:
            extra = min(bound - given[i], max(1, left * portions[i] // pool), surplus)
            given[i] = given[i] + extra
            surplus = surplus - extra
    return np.array([bound] + given)


def ragged_sizes(stream_key, number_of, total, bound, lean):
    if number_of == 2:
        one = jax.random.randint(stream_key, (), max(1, total - bound), min(bound, total - 1) + 1)
        return jnp.stack([one, total - one])
    sizes = jnp.asarray(profile(number_of, total, bound, lean), jnp.int32)
    twos = (number_of - 1) // 2
    source_of, receiver = sizes[1:1 + 2 * twos:2], sizes[2:2 + 2 * twos:2]
    room = jnp.minimum(source_of - 1, bound - receiver)
    moved = jax.random.randint(jax.random.fold_in(stream_key, 1), (twos,), 0, 1 << 20) % (room + 1)
    sizes = sizes.at[1:1 + 2 * twos:2].set(source_of - moved).at[2:2 + 2 * twos:2].set(receiver + moved)
    return sizes[jax.random.permutation(jax.random.fold_in(stream_key, 2), number_of)]


def normal_values(own_key, extent, spread, most, cuts=(), held_as=jnp.bfloat16):
    entries = spread * jax.random.normal(own_key, extent, jnp.float32)
    if cuts:
        entries = entries * steps_of(own_key, extent, cuts, -0.22, 0.18)
    return jnp.clip(entries, -most, most).astype(held_as)


def setup_inputs(seed: int = 0) -> dict:
    arg_keys = jax.random.split(jax.random.key(seed), 27)
    return {
        "series": normal_values(arg_keys[0], (ROWS, D), 1.0, 6.0, ((0, 32),)),
        "target": normal_values(arg_keys[1], (ROWS, D), 1.0, 6.0, ((0, 32),), jnp.float32),
        "valid": draw_valid(jax.random.fold_in(arg_keys[26], 71), 0),
        "window_id": jax.vmap(lambda own: jnp.searchsorted(jnp.cumsum(ragged_sizes(own, WINDOWS, SEQ_LEN, 3 * SEQ_LEN // 8, 1)), jnp.arange(SEQ_LEN), side="right"))(jax.random.split(arg_keys[3], CONTEXTS)).reshape((CONTEXTS, SEQ_LEN)).astype(jnp.int32),
        "mode_index": draw_mode_index(jax.random.fold_in(arg_keys[26], 71), 0),
        "query_weight": normal_values(arg_keys[5], (D, D), D ** -0.5, 0.25, ((1, 4),), jnp.float32),
        "query_first": normal_values(arg_keys[6], (D, D), (0.0022 / PARAMS ** 0.5), 4.76837158203125e-06, ((1, 4),), jnp.float32),
        "query_second": jnp.clip(jnp.exp(math.log(2.3471464572280554e-13) - 1.3862944 * jax.random.uniform(arg_keys[7], (D, D), jnp.float32) ** steps_of(arg_keys[7], (D, D), ((1, 4),), -0.2, 0.2)), 5.867866143070138e-14, 2.3471464572280554e-13),
        "out_weight": normal_values(arg_keys[8], (D, D), D ** -0.5, 0.25, ((0, 4),), jnp.float32),
        "out_first": normal_values(arg_keys[9], (D, D), (0.0022 / PARAMS ** 0.5), 4.76837158203125e-06, ((0, 4),), jnp.float32),
        "out_second": jnp.clip(jnp.exp(math.log(2.3471464572280554e-13) - 1.3862944 * jax.random.uniform(arg_keys[10], (D, D), jnp.float32) ** steps_of(arg_keys[10], (D, D), ((0, 4),), -0.2, 0.2)), 5.867866143070138e-14, 2.3471464572280554e-13),
        "mode_weight": normal_values(arg_keys[11], (2, HEADS, HEAD_DIM, HEAD_DIM * MODES), 0.06, 0.36, ((1, 4),), jnp.float32),
        "mode_first": normal_values(arg_keys[12], (2, HEADS, HEAD_DIM, HEAD_DIM * MODES), (0.0022 / PARAMS ** 0.5), 4.76837158203125e-06, ((1, 4),), jnp.float32),
        "mode_second": jnp.clip(jnp.exp(math.log(2.3471464572280554e-13) - 1.3862944 * jax.random.uniform(arg_keys[13], (2, HEADS, HEAD_DIM, HEAD_DIM * MODES), jnp.float32) ** steps_of(arg_keys[13], (2, HEADS, HEAD_DIM, HEAD_DIM * MODES), ((1, 4),), -0.2, 0.2)), 5.867866143070138e-14, 2.3471464572280554e-13),
        "up_weight": normal_values(arg_keys[14], (D, FF), D ** -0.5, 0.25, ((1, 4),), jnp.float32),
        "up_first": normal_values(arg_keys[15], (D, FF), (0.0022 / PARAMS ** 0.5), 4.76837158203125e-06, ((1, 4),), jnp.float32),
        "up_second": jnp.clip(jnp.exp(math.log(2.3471464572280554e-13) - 1.3862944 * jax.random.uniform(arg_keys[16], (D, FF), jnp.float32) ** steps_of(arg_keys[16], (D, FF), ((1, 4),), -0.2, 0.2)), 5.867866143070138e-14, 2.3471464572280554e-13),
        "down_weight": normal_values(arg_keys[17], (FF, D), FF ** -0.5, 0.125, ((0, 4),), jnp.float32),
        "down_first": normal_values(arg_keys[18], (FF, D), (0.0022 / PARAMS ** 0.5), 4.76837158203125e-06, ((0, 4),), jnp.float32),
        "down_second": jnp.clip(jnp.exp(math.log(2.3471464572280554e-13) - 1.3862944 * jax.random.uniform(arg_keys[19], (FF, D), jnp.float32) ** steps_of(arg_keys[19], (FF, D), ((0, 4),), -0.2, 0.2)), 5.867866143070138e-14, 2.3471464572280554e-13),
        "bias_pair": normal_values(arg_keys[20], (2, D), 0.5, 3.0, (), jnp.float32),
        "bias_first": normal_values(arg_keys[21], (2, D), (0.0022 / PARAMS ** 0.5), 4.76837158203125e-06, (), jnp.float32),
        "bias_second": jnp.clip(jnp.exp(jax.random.uniform(arg_keys[22], (2, D), jnp.float32, math.log(5.867866143070138e-14), math.log(2.3471464572280554e-13))), 5.867866143070138e-14, 2.3471464572280554e-13),
        "decomp_params": normal_values(arg_keys[23], (2, 2, KERNELS), 1.0, 3.0, (), jnp.float32),
        "decomp_first": normal_values(arg_keys[24], (2, 2, KERNELS), (0.0022 / PARAMS ** 0.5), 4.76837158203125e-06, (), jnp.float32),
        "decomp_second": jnp.clip(jnp.exp(jax.random.uniform(arg_keys[25], (2, 2, KERNELS), jnp.float32, math.log(5.867866143070138e-14), math.log(2.3471464572280554e-13))), 5.867866143070138e-14, 2.3471464572280554e-13),
    }


HIGHEST_PRECISION = lax.Precision.HIGHEST
KERNEL_WIDTHS = (7, 12, 14, 24, 48)
BETA_ONE = 0.9
BETA_TWO = 0.999
LEARN_RATE = 0.05
EPSILON = 1e-08
DECAY = 0.01
CLIP_NORM = 0.02

@jax.custom_vjp
def low(v):
    return lax.optimization_barrier(v.astype(jnp.bfloat16)).astype(jnp.float32)

@jax.custom_vjp
def low_back(v):
    return v

def low_keep(v):
    return (low(v), None)

def low_pass(kept, grad):
    return (grad,)

def back_keep(v):
    return (v, None)

def back_low(kept, grad):
    return (low(grad),)
low.defvjp(low_keep, low_pass)
low_back.defvjp(back_keep, back_low)

def window_averages(window_rows):
    length = window_rows.shape[1]
    earlier = (window_rows[:, None, :] < window_rows[:, :, None]).astype(jnp.int32)
    first = lax.optimization_barrier(jnp.sum(earlier, axis=2)).astype(jnp.int32)[:, :, None]
    upto = (window_rows[:, None, :] <= window_rows[:, :, None]).astype(jnp.int32)
    last = (lax.optimization_barrier(jnp.sum(upto, axis=2)).astype(jnp.int32) - 1)[:, :, None]
    row_steps = jnp.arange(length, dtype=jnp.int32)[None, :, None]
    columns = jnp.arange(length, dtype=jnp.int32)[None, None, :]
    matrices = []
    for kernel_width in KERNEL_WIDTHS:
        lead_pad = kernel_width - 1 - (kernel_width - 1) // 2
        matrix = jnp.zeros((window_rows.shape[0], length, length), jnp.float32)
        for offset in range(kernel_width):
            position = jnp.minimum(jnp.maximum(row_steps - lead_pad + offset, first), last)
            matrix = matrix + (position == columns).astype(jnp.float32)
        matrices.append(matrix / kernel_width)
    return jnp.stack(matrices, axis=1)

def forward_tables(mode_index, length):
    steps_t = jnp.arange(length, dtype=jnp.int32)
    phase_index = mode_index[:, :, None] * steps_t[None, None, :] % length
    angles = phase_index.astype(jnp.float32) * (2.0 * math.pi / length)
    return (jnp.cos(angles), jnp.sin(angles))

def inverse_tables(count_modes, length):
    steps_t = jnp.arange(length, dtype=jnp.int32)[:, None]
    orders = jnp.arange(count_modes, dtype=jnp.int32)[None, :]
    angles = (steps_t * orders % length).astype(jnp.float32) * (2.0 * math.pi / length)
    weights = jnp.where(orders == 0, 1.0, 2.0).astype(jnp.float32) / length
    return (jnp.cos(angles) * weights, jnp.sin(angles) * weights)

def spectral(queries, mode_weights, cos_fwd, sin_fwd, cos_inv, sin_inv):
    heads = cos_fwd.shape[0]
    count_modes = cos_fwd.shape[1]
    length = cos_fwd.shape[2]
    contexts = queries.shape[0] // length
    shaped = queries.reshape(contexts, length, heads, -1)
    width = shaped.shape[3]
    merged = mode_weights.reshape(2, heads, width, -1, count_modes)
    real_in = jnp.einsum('hmt,bthe->bhme', cos_fwd, shaped, precision=HIGHEST_PRECISION)
    imag_in = -jnp.einsum('hmt,bthe->bhme', sin_fwd, shaped, precision=HIGHEST_PRECISION)
    w_real = merged[0]
    w_imag = merged[1]
    real_out = jnp.einsum('bhme,heom->bhmo', real_in, w_real, precision=HIGHEST_PRECISION) - jnp.einsum('bhme,heom->bhmo', imag_in, w_imag, precision=HIGHEST_PRECISION)
    imag_out = jnp.einsum('bhme,heom->bhmo', real_in, w_imag, precision=HIGHEST_PRECISION) + jnp.einsum('bhme,heom->bhmo', imag_in, w_real, precision=HIGHEST_PRECISION)
    result = jnp.einsum('tm,bhmo->btho', cos_inv, real_out, precision=HIGHEST_PRECISION) - jnp.einsum('tm,bhmo->btho', sin_inv, imag_out, precision=HIGHEST_PRECISION)
    return result.reshape(queries.shape[0], -1)

def decompose(values, decomp_row, averages):
    length = averages.shape[2]
    contexts = values.shape[0] // length
    shaped = values.reshape(contexts, length, values.shape[1])
    averaged = jnp.einsum('bkts,bsf->kbtf', averages, shaped, precision=HIGHEST_PRECISION)
    logits = shaped[None] * decomp_row[0][:, None, None, None] + decomp_row[1][:, None, None, None]
    shares = jax.nn.softmax(logits, axis=0)
    trend_part = lax.optimization_barrier(jnp.sum(shares * averaged, axis=0)).reshape(values.shape)
    return (values - trend_part, trend_part)

def block_loss(params, inputs, target_rows, valid_rows, window_rows, tables):
    query_weight, out_weight, mode_weight, up_weight, down_weight, bias_pair, decomp_params = params
    averages = window_averages(window_rows)
    queries = low_back(jnp.dot(inputs, low(query_weight), precision=HIGHEST_PRECISION) + bias_pair[0])
    spectrum = low(spectral(queries, mode_weight, *tables))
    attention = low_back(jnp.dot(spectrum, low(out_weight), precision=HIGHEST_PRECISION)) + bias_pair[1]
    season_one, trend_one = decompose(inputs + attention, decomp_params[0], averages)
    hidden = low_back(jnp.dot(low(season_one), low(up_weight), precision=HIGHEST_PRECISION))
    active = low(jax.nn.gelu(hidden, approximate=False))
    feed_out = low_back(jnp.dot(active, low(down_weight), precision=HIGHEST_PRECISION))
    trend_two = decompose(season_one + feed_out, decomp_params[1], averages)[1]
    misfit = trend_one + trend_two - target_rows
    return jnp.sum(valid_rows[:, None] * misfit * misfit)

def adam_step(weight, gradient, moment_one, second):
    moment_one = BETA_ONE * moment_one + (1.0 - BETA_ONE) * gradient
    second = BETA_TWO * second + (1.0 - BETA_TWO) * gradient * gradient
    first_hat = moment_one / (1.0 - BETA_ONE ** STEP)
    second_hat = second / (1.0 - BETA_TWO ** STEP)
    weight = weight - LEARN_RATE * (first_hat / (jnp.sqrt(second_hat) + EPSILON) + DECAY * weight)
    return (weight, moment_one, second)

def reference(series, target, valid, window_id, mode_index, query_weight, query_first, query_second, out_weight, out_first, out_second, mode_weight, mode_first, mode_second, up_weight, up_first, up_second, down_weight, down_first, down_second, bias_pair, bias_first, bias_second, decomp_params, decomp_first, decomp_second):
    tables = forward_tables(mode_index, SEQ_LEN) + inverse_tables(MODES, SEQ_LEN)
    ctx_block = CTX_DEV // MICRO
    rows_block = ctx_block * SEQ_LEN
    blocks = ROWS // rows_block
    items = (series.astype(jnp.float32).reshape(blocks, rows_block, D), target.reshape(blocks, rows_block, D), valid.astype(jnp.float32).reshape(blocks, rows_block), window_id.reshape(blocks, ctx_block, SEQ_LEN))
    weights = (query_weight, out_weight, mode_weight, up_weight, down_weight, bias_pair, decomp_params)

    def total_loss(params):
        block_fn = jax.checkpoint(lambda inner, block_item: block_loss(inner, block_item[0], block_item[1], block_item[2], block_item[3], tables))

        def scan_step(running, block_item):
            return (running + block_fn(params, block_item), None)
        return lax.scan(scan_step, jnp.zeros((), jnp.float32), items)[0]
    loss_sum, pullback = jax.vjp(total_loss, weights)
    gradients = pullback(jnp.ones((), jnp.float32))[0]
    valid_count = jnp.sum(valid.astype(jnp.float32))
    gradients = tuple((gradient / valid_count for gradient in gradients))
    grad_norm = jnp.sqrt(sum((jnp.sum(gradient * gradient) for gradient in gradients)))
    factor = jnp.minimum(1.0, CLIP_NORM / (grad_norm + 1e-06))
    firsts = (query_first, out_first, mode_first, up_first, down_first, bias_first, decomp_first)
    seconds = (query_second, out_second, mode_second, up_second, down_second, bias_second, decomp_second)
    news = [adam_step(weights[index], gradients[index] * factor, firsts[index], seconds[index]) for index in range(7)]
    return (loss_sum, valid_count, grad_norm, news[0][0], news[0][1], news[0][2], news[1][0], news[1][1], news[1][2], news[2][0], news[2][1], news[2][2], news[3][0], news[3][1], news[3][2], news[4][0], news[4][1], news[4][2], news[5][0], news[5][1], news[5][2], news[6][0], news[6][1], news[6][2])
```

```python
from functools import partial
import math

import jax
import jax.numpy as jnp
from jax import lax
from jax.experimental import pallas as pl
from jax.experimental.pallas import tpu as pltpu
from jax.sharding import PartitionSpec as P

MODES = 64
SEQ_LEN = 128
HEAD_DIM = 64
STEP = 10
KERNEL_WIDTHS = (7, 12, 14, 24, 48)
KERNELS = len(KERNEL_WIDTHS)
BETA_ONE = 0.9
BETA_TWO = 0.999
LEARN_RATE = 0.05
EPSILON = 1e-08
DECAY = 0.01
CLIP_NORM = 0.02
LOG2E = math.log2(math.e)
LANES = 128
BF = jnp.bfloat16
F32 = jnp.float32
MIB = 1 << 20

ERF_P = 0.3275911
ERF_A = (0.254829592, -0.284496736, 1.421413741, -1.453152027, 1.061405429)


def dot(a, b, ca=1, cb=0):
    return lax.dot_general(a, b, (((ca,), (cb,)), ((), ())), preferred_element_type=F32)


def query_kernel(x_ref, w_ref, b_ref, q_ref):
    heads, _, width = w_ref.shape
    x = x_ref[...]
    for h in range(heads):
        q_ref[h] = (dot(x, w_ref[h]) + b_ref[h]).astype(BF)


def query_call(x, w_all, bias_row):
    rows, d = x.shape
    heads, _, width = w_all.shape
    step = min(256, rows)
    return pl.pallas_call(
        query_kernel,
        grid=(rows // step,),
        in_specs=[
            pl.BlockSpec((step, d), lambda i: (i, 0)),
            pl.BlockSpec((heads, d, width), lambda i: (0, 0, 0)),
            pl.BlockSpec((heads, 1, width), lambda i: (0, 0, 0)),
        ],
        out_specs=pl.BlockSpec((heads, step, width), lambda i: (0, i, 0)),
        out_shape=jax.ShapeDtypeStruct((heads, rows, width), BF),
        compiler_params=pltpu.CompilerParams(vmem_limit_bytes=24 * MIB),
        name="queries",
    )(x, w_all, bias_row.reshape(heads, 1, width))


def lane_low(rows):
    return lax.broadcasted_iota(jnp.int32, (rows, LANES), 1) < HEAD_DIM


def mix_block(wc_ref, m):
    low = lane_low(HEAD_DIM)
    zero = jnp.zeros((HEAD_DIM, LANES), F32)

    def spread(part):
        part = part.astype(F32)
        return jnp.concatenate([jnp.where(low, part, zero), jnp.where(low, zero, part)], axis=0)

    real = spread(wc_ref[m, 0])
    imag = spread(wc_ref[m, 1])
    top = jnp.concatenate([real, imag], axis=1)
    bottom = jnp.concatenate([-imag, real], axis=1)
    return jnp.concatenate([top, bottom], axis=0).astype(BF)


def pair_width(contexts):
    return 2 if contexts % 2 == 0 else 1


def spectrum_kernel(q_ref, wc_ref, tf_ref, ti_ref, spec_ref, xs_ref, x_scr, y_scr):
    contexts = q_ref.shape[0]
    pair = pair_width(contexts)
    low = lane_low(SEQ_LEN)

    def forward(p, _):
        cols = jnp.concatenate([q_ref[p * pair + k] for k in range(pair)], axis=1)
        res = dot(tf_ref[...], jnp.concatenate([cols, cols], axis=0))
        for k in range(pair):
            part = res[:, k * LANES : (k + 1) * LANES]
            x_scr[pl.ds(pl.multiple_of((p * pair + k) * SEQ_LEN, SEQ_LEN), SEQ_LEN), :] = jnp.where(
                low, part[:SEQ_LEN], part[SEQ_LEN:]
            )
        return 0

    lax.fori_loop(0, contexts // pair, forward, 0)

    def mix(m, _):
        xr = x_scr[pl.ds(m, contexts, stride=SEQ_LEN), :].astype(BF)
        xi = x_scr[pl.ds(MODES + m, contexts, stride=SEQ_LEN), :].astype(BF)
        xs_ref[m] = jnp.concatenate([xr, xi], axis=0)
        y = dot(jnp.concatenate([xr, xi], axis=1), mix_block(wc_ref, m))
        y_scr[pl.ds(m, contexts, stride=SEQ_LEN), :] = y[:, :LANES]
        y_scr[pl.ds(MODES + m, contexts, stride=SEQ_LEN), :] = y[:, LANES:]
        return 0

    lax.fori_loop(0, MODES, mix, 0, unroll=4)

    def inverse(p, _):
        parts = [
            y_scr[pl.ds(pl.multiple_of((p * pair + k) * SEQ_LEN, SEQ_LEN), SEQ_LEN), :].astype(BF)
            for k in range(pair)
        ]
        cols = jnp.concatenate(parts, axis=1)
        res = dot(ti_ref[...], jnp.concatenate([cols, cols], axis=0)).astype(BF)
        for k in range(pair):
            spec_ref[p * pair + k] = res[:, k * LANES : (k + 1) * LANES]
        return 0

    lax.fori_loop(0, contexts // pair, inverse, 0)


def spectrum_call(q, wc, tf, ti):
    contexts = q.shape[0]
    return pl.pallas_call(
        spectrum_kernel,
        out_shape=(
            jax.ShapeDtypeStruct((contexts, SEQ_LEN, LANES), BF),
            jax.ShapeDtypeStruct((MODES, 2 * contexts, LANES), BF),
        ),
        scratch_shapes=[
            pltpu.VMEM((contexts * SEQ_LEN, LANES), F32),
            pltpu.VMEM((contexts * SEQ_LEN, LANES), F32),
        ],
        compiler_params=pltpu.CompilerParams(vmem_limit_bytes=32 * MIB),
        name="spectrum",
    )(q, wc, tf, ti)


def mode_grad_kernel(me_ref, ds_ref, xs_ref, tit_ref, dy_ref, send_ref, keep_ref, y_scr, dw_scr, sems):
    contexts = ds_ref.shape[0]
    pair = pair_width(contexts)
    pieces = dw_scr.shape[0]
    depth = HEAD_DIM // pieces
    low = lane_low(HEAD_DIM)
    me = me_ref[0]

    def forward(p, _):
        cols = jnp.concatenate([ds_ref[p * pair + k] for k in range(pair)], axis=1)
        res = dot(tit_ref[...], jnp.concatenate([cols, cols], axis=0))
        for k in range(pair):
            y_scr[pl.ds(pl.multiple_of((p * pair + k) * SEQ_LEN, SEQ_LEN), SEQ_LEN), :] = res[
                :, k * LANES : (k + 1) * LANES
            ]
        return 0

    lax.fori_loop(0, contexts // pair, forward, 0)

    def mix(m, _):
        yr = y_scr[pl.ds(m, contexts, stride=SEQ_LEN), :]
        yi = y_scr[pl.ds(MODES + m, contexts, stride=SEQ_LEN), :]
        dy_ref[m] = jnp.concatenate([yr, yi], axis=1).astype(BF)
        right = jnp.concatenate(
            [jnp.concatenate([yr, yi], axis=0), jnp.concatenate([yi, -yr], axis=0)], axis=1
        ).astype(BF)
        dw = dot(xs_ref[m], right, 0, 0)
        for c in range(2):
            half = dw[:, c * LANES : (c + 1) * LANES]
            part = jnp.where(low, half[:HEAD_DIM], half[HEAD_DIM:])
            for d in range(pieces):
                dw_scr[me ^ d, m, c] = part[d * depth : (d + 1) * depth]
        return 0

    lax.fori_loop(0, MODES, mix, 0, unroll=4)
    copies = []
    for j in range(pieces):
        target = (send_ref if j % 2 else keep_ref).at[j // 2]
        copies.append(pltpu.make_async_copy(dw_scr.at[j], target, sems.at[j]))
        copies[-1].start()
    for copy in copies:
        copy.wait()


def mode_grad_call(me, ds, xs, tit, pieces):
    contexts = ds.shape[0]
    half = jax.ShapeDtypeStruct((pieces // 2, MODES, 2, HEAD_DIM // pieces, LANES), F32)
    whole = pl.BlockSpec(memory_space=pltpu.VMEM)
    anywhere = pl.BlockSpec(memory_space=pl.ANY)
    return pl.pallas_call(
        mode_grad_kernel,
        in_specs=[pl.BlockSpec(memory_space=pltpu.SMEM), whole, whole, whole],
        out_specs=(whole, anywhere, anywhere),
        out_shape=(jax.ShapeDtypeStruct((MODES, contexts, 2 * LANES), BF), half, half),
        scratch_shapes=[
            pltpu.VMEM((contexts * SEQ_LEN, LANES), F32),
            pltpu.VMEM((pieces,) + half.shape[1:], F32),
            pltpu.SemaphoreType.DMA((pieces,)),
        ],
        compiler_params=pltpu.CompilerParams(vmem_limit_bytes=40 * MIB),
        name="mode_grads",
    )(me, ds, xs, tit)


def query_grad_kernel(dy_ref, wc_ref, tft_ref, dq_ref, bias_ref, x_scr):
    contexts = dq_ref.shape[0]
    pair = pair_width(contexts)
    low = lane_low(SEQ_LEN)
    zero = jnp.zeros((SEQ_LEN, LANES), F32)

    def mix(m, _):
        dx = dot(dy_ref[m], mix_block(wc_ref, m), 1, 1)
        x_scr[pl.ds(m, contexts, stride=SEQ_LEN), :] = dx[:, :LANES]
        x_scr[pl.ds(MODES + m, contexts, stride=SEQ_LEN), :] = dx[:, LANES:]
        return 0

    lax.fori_loop(0, MODES, mix, 0, unroll=4)
    bias_ref[...] = jnp.zeros_like(bias_ref)

    def inverse(p, _):
        parts = []
        for k in range(pair):
            one = x_scr[pl.ds(pl.multiple_of((p * pair + k) * SEQ_LEN, SEQ_LEN), SEQ_LEN), :]
            parts.append(
                jnp.concatenate([jnp.where(low, one, zero), jnp.where(low, zero, one)], axis=0)
            )
        cols = jnp.concatenate(parts, axis=1).astype(BF)
        res = dot(tft_ref[...], jnp.concatenate([cols, cols], axis=0)).astype(BF)
        total = jnp.zeros((8, LANES), F32)
        for k in range(pair):
            one = res[:, k * LANES : (k + 1) * LANES]
            dq_ref[p * pair + k] = one
            total = total + jnp.sum(one.astype(F32).reshape(SEQ_LEN // 8, 8, LANES), axis=0)
        bias_ref[...] += total
        return 0

    lax.fori_loop(0, contexts // pair, inverse, 0)


def query_grad_call(dy, wc, tft):
    contexts = dy.shape[1]
    return pl.pallas_call(
        query_grad_kernel,
        out_shape=(
            jax.ShapeDtypeStruct((contexts, SEQ_LEN, LANES), BF),
            jax.ShapeDtypeStruct((8, LANES), F32),
        ),
        scratch_shapes=[pltpu.VMEM((contexts * SEQ_LEN, LANES), F32)],
        compiler_params=pltpu.CompilerParams(vmem_limit_bytes=32 * MIB),
        name="query_grads",
    )(dy, wc, tft)


SUM_SLOPE = (0, 10)
SUM_OFFSET = (5, 15)
SUM_LOSS = 20
SUM_BIAS = 21
SUM_ROWS = 24


def window_counts(first, last, rows, cols, width):
    lead = width - 1 - (width - 1) // 2
    reach = cols - rows + (lead + 1)
    here = jnp.where(cols < first, 0, jnp.where(cols >= last, width, jnp.clip(reach, 0, width)))
    before = jnp.where(
        cols <= first, 0, jnp.where(cols > last, width, jnp.clip(reach - 1, 0, width))
    )
    return (here - before).astype(F32)


def window_edges(starts, rows):
    s1, s2, s3 = starts
    first = jnp.where(rows >= s3, s3, jnp.where(rows >= s2, s2, jnp.where(rows >= s1, s1, 0)))
    last = jnp.where(
        rows < s1, s1 - 1, jnp.where(rows < s2, s2 - 1, jnp.where(rows < s3, s3 - 1, SEQ_LEN - 1))
    )
    return first, last


def fold(v):
    return jnp.sum(v.reshape(v.shape[0] // 8, 8, v.shape[1]), axis=0)


def local_kernel(
    starts_ref,
    prm_ref,
    me_ref,
    x_ref,
    spec_ref,
    tgt_ref,
    val_ref,
    up_ref,
    down_ref,
    out_ref,
    bias_ref,
    dspec_ref,
    sums_ref,
    up_send,
    up_keep,
    down_send,
    down_keep,
    out_send,
    out_keep,
    u_scr,
    trend_scr,
    season_scr,
    low_scr,
    av1_scr,
    share_scr,
    av2_scr,
    da_scr,
    part_scr,
    g_scr,
    act_scr,
    slope_scr,
    a_scr,
    at_scr,
    gup,
    gdown,
    gout,
    sems,
    *,
    chunk,
):
    step = pl.program_id(0)
    rows, d = x_ref.shape
    nctx = rows // SEQ_LEN
    heads, _, hidden_width = up_ref.shape
    out_width = out_ref.shape[1]
    groups = d // LANES
    loops = SEQ_LEN // chunk

    @pl.when(step == 0)
    def _():
        sums_ref[...] = jnp.zeros_like(sums_ref)
        gup[...] = jnp.zeros_like(gup)
        gdown[...] = jnp.zeros_like(gdown)
        gout[...] = jnp.zeros_like(gout)

    row_ids = lax.broadcasted_iota(jnp.int32, (SEQ_LEN, SEQ_LEN), 0)
    col_ids = lax.broadcasted_iota(jnp.int32, (SEQ_LEN, SEQ_LEN), 1)
    for c in range(nctx):
        ctx = step * nctx + c
        starts = [starts_ref[ctx, k] for k in range(1, 4)]
        first, last = window_edges(starts, row_ids)
        first_t, last_t = window_edges(starts, col_ids)
        for w, width in enumerate(KERNEL_WIDTHS):
            counts = window_counts(first, last, row_ids, col_ids, width).astype(BF)
            a_scr[c, w * SEQ_LEN : (w + 1) * SEQ_LEN, :SEQ_LEN] = counts
            a_scr[c, w * SEQ_LEN : (w + 1) * SEQ_LEN, SEQ_LEN:] = counts
            at_scr[c, :, w * SEQ_LEN : (w + 1) * SEQ_LEN] = window_counts(
                first_t, last_t, col_ids, row_ids, width
            ).astype(BF)

    def averages(c, u, av):
        high = u.astype(BF)
        rest = (u - high.astype(F32)).astype(BF)
        av[c] = dot(a_scr[c], jnp.concatenate([high, rest], axis=0))

    spec = jnp.concatenate([spec_ref[h] for h in range(heads)], axis=1)
    out_all = jnp.concatenate([out_ref[h] for h in range(heads)], axis=0)
    pre = x_ref[...].astype(F32) + (dot(spec, out_all) + bias_ref[...])
    u_scr[...] = pre
    for c in range(nctx):
        averages(c, pre[c * SEQ_LEN : (c + 1) * SEQ_LEN], av1_scr)

    def shares_of(u, avs, layer):
        logits = [
            u * (prm_ref[layer, 0, w] * LOG2E) + prm_ref[layer, 1, w] * LOG2E
            for w in range(KERNELS)
        ]
        top = logits[0]
        for v in logits[1:]:
            top = jnp.maximum(top, v)
        powers = [jnp.exp2(v - top) for v in logits]
        total = powers[0]
        for v in powers[1:]:
            total = total + v
        scale = 1.0 / total
        shares = [v * scale for v in powers]
        trend = shares[0] * avs[0]
        for s, a in zip(shares[1:], avs[1:]):
            trend = trend + s * a
        return shares, trend

    def read_averages(av, c, row, lanes):
        return [
            av[c, pl.ds(w * SEQ_LEN + row, chunk), lanes] * (1.0 / width)
            for w, width in enumerate(KERNEL_WIDTHS)
        ]

    def pull(shares, avs, trend, grad, u, layer, base, c, row, lanes, sums):
        rest = base
        slopes, offsets = [], []
        for w, width in enumerate(KERNEL_WIDTHS):
            d_avg = shares[w] * grad
            da_scr[c, pl.ds(w * SEQ_LEN + row, chunk), lanes] = (d_avg * (1.0 / width)).astype(BF)
            d_logit = d_avg * (avs[w] - trend)
            rest = rest + d_logit * prm_ref[layer, 0, w]
            slopes.append(sums[w] + fold(d_logit * u))
            offsets.append(sums[KERNELS + w] + fold(d_logit))
        return rest, slopes + offsets

    for c in range(nctx):
        for g in range(groups):
            lanes = slice(g * LANES, (g + 1) * LANES)

            def first_pass(r, _, c=c, lanes=lanes):
                row = pl.multiple_of(r * chunk, chunk)
                at = pl.ds(c * SEQ_LEN + row, chunk)
                u = u_scr[at, lanes]
                avs = read_averages(av1_scr, c, row, lanes)
                shares, trend = shares_of(u, avs, 0)
                for w in range(KERNELS):
                    share_scr[c, pl.ds(w * SEQ_LEN + row, chunk), lanes] = shares[w]
                season = u - trend
                trend_scr[at, lanes] = trend
                season_scr[at, lanes] = season
                low_scr[at, lanes] = season.astype(BF)
                return 0

            lax.fori_loop(0, loops, first_pass, 0)

    season_low = low_scr[...]
    feed = jnp.zeros((rows, d), F32)
    for h in range(heads):
        hid = dot(season_low, up_ref[h])
        z = jnp.abs(hid) * (2.0**-0.5)
        t = 1.0 / (1.0 + ERF_P * z)
        e = jnp.exp2(hid * hid * (-0.5 * LOG2E))
        poly = ERF_A[4]
        for coef in ERF_A[3::-1]:
            poly = poly * t + coef
        tail = (0.5 * t) * poly * e
        phi = jnp.where(hid < 0, tail, 1.0 - tail)
        active = (hid * phi).astype(BF)
        slope_scr[h] = phi + hid * e * ((2.0 * math.pi) ** -0.5)
        act_scr[h] = active
        feed = feed + dot(active, down_ref[h])

    pre = season_scr[...] + feed
    g_scr[...] = pre
    for c in range(nctx):
        averages(c, pre[c * SEQ_LEN : (c + 1) * SEQ_LEN], av2_scr)

    for c in range(nctx):
        for g in range(groups):
            lanes = slice(g * LANES, (g + 1) * LANES)

            def second_pass(r, sums, c=c, lanes=lanes):
                row = pl.multiple_of(r * chunk, chunk)
                at = pl.ds(c * SEQ_LEN + row, chunk)
                u = g_scr[at, lanes]
                avs = read_averages(av2_scr, c, row, lanes)
                shares, trend = shares_of(u, avs, 1)
                misfit = trend_scr[at, lanes] + trend - tgt_ref[at, lanes]
                weighted = val_ref[at, :] * misfit
                grad = 2.0 * weighted
                rest, new = pull(
                    shares, avs, trend, grad, u, 1, jnp.zeros_like(u), c, row, lanes, sums
                )
                part_scr[at, lanes] = rest
                g_scr[at, lanes] = grad
                return tuple(new) + (sums[2 * KERNELS] + fold(weighted * misfit),)

            zeros = tuple(jnp.zeros((8, LANES), F32) for _ in range(2 * KERNELS + 1))
            sums = lax.fori_loop(0, loops, second_pass, zeros)
            for k in range(KERNELS):
                sums_ref[SUM_SLOPE[1] + k, :, lanes] += sums[k]
                sums_ref[SUM_OFFSET[1] + k, :, lanes] += sums[KERNELS + k]
            sums_ref[SUM_LOSS, :, lanes] += sums[2 * KERNELS]

    for c in range(nctx):
        at = slice(c * SEQ_LEN, (c + 1) * SEQ_LEN)
        part_scr[at, :] += dot(at_scr[c], da_scr[c])

    d_pre = part_scr[...]
    d_feed = d_pre.astype(BF)
    back = d_pre
    for h in range(heads):
        d_hid = (dot(d_feed, down_ref[h], 1, 1) * slope_scr[h]).astype(BF)
        back = back + dot(d_hid, up_ref[h], 1, 1)
        gup[h] += dot(season_low, d_hid, 0, 0)
        gdown[h] += dot(act_scr[h], d_feed, 0, 0)
    season_scr[...] = back

    for c in range(nctx):
        for g in range(groups):
            lanes = slice(g * LANES, (g + 1) * LANES)

            def third_pass(r, sums, c=c, lanes=lanes):
                row = pl.multiple_of(r * chunk, chunk)
                at = pl.ds(c * SEQ_LEN + row, chunk)
                u = u_scr[at, lanes]
                avs = read_averages(av1_scr, c, row, lanes)
                shares = [
                    share_scr[c, pl.ds(w * SEQ_LEN + row, chunk), lanes] for w in range(KERNELS)
                ]
                d_season = season_scr[at, lanes]
                rest, new = pull(
                    shares,
                    avs,
                    trend_scr[at, lanes],
                    g_scr[at, lanes] - d_season,
                    u,
                    0,
                    d_season,
                    c,
                    row,
                    lanes,
                    sums,
                )
                part_scr[at, lanes] = rest
                return tuple(new)

            zeros = tuple(jnp.zeros((8, LANES), F32) for _ in range(2 * KERNELS))
            sums = lax.fori_loop(0, loops, third_pass, zeros)
            for k in range(KERNELS):
                sums_ref[SUM_SLOPE[0] + k, :, lanes] += sums[k]
                sums_ref[SUM_OFFSET[0] + k, :, lanes] += sums[KERNELS + k]

    for c in range(nctx):
        at = slice(c * SEQ_LEN, (c + 1) * SEQ_LEN)
        part_scr[at, :] += dot(at_scr[c], da_scr[c])

    d_pre = part_scr[...]
    sums_ref[SUM_BIAS] += fold(d_pre)
    d_attn = d_pre.astype(BF)
    d_spec = dot(d_attn, out_all, 1, 1).astype(BF)
    pieces = gout.shape[1]
    depth = out_width // pieces
    g_out = dot(spec, d_attn, 0, 0)
    for h in range(heads):
        dspec_ref[h] = d_spec[:, h * out_width : (h + 1) * out_width]
        for p in range(pieces):
            start = h * out_width + p * depth
            gout[h, p] += g_out[start : start + depth]

    @pl.when(step == pl.num_programs(0) - 1)
    def _():
        me = me_ref[0]
        copies = []
        for j in range(pieces):
            piece = me ^ j
            for k, (grad, send, keep) in enumerate(
                ((gup, up_send, up_keep), (gdown, down_send, down_keep))
            ):
                size = grad.shape[1] // pieces
                source = grad.at[:, pl.ds(pl.multiple_of(piece * size, size), size), :]
                target = (send if j % 2 else keep).at[j // 2]
                copies.append(pltpu.make_async_copy(source, target, sems.at[k, j]))
            target = (out_send if j % 2 else out_keep).at[j // 2]
            copies.append(pltpu.make_async_copy(gout.at[:, piece], target, sems.at[2, j]))
        for copy in copies:
            copy.start()
        for copy in copies:
            copy.wait()


def local_call(starts, prm, me, x, spec, target, valid, up, down, out, bias, pieces):
    rows_all, d = x.shape
    heads, _, hidden = up.shape
    width = out.shape[1]
    nctx = 2 if rows_all % (2 * SEQ_LEN) == 0 else 1
    rows = nctx * SEQ_LEN
    smem = pl.BlockSpec(memory_space=pltpu.SMEM)
    whole = pl.BlockSpec(memory_space=pltpu.VMEM)
    anywhere = pl.BlockSpec(memory_space=pl.ANY)
    halves = [
        jax.ShapeDtypeStruct((pieces // 2, heads, d // pieces, hidden), F32),
        jax.ShapeDtypeStruct((pieces // 2, heads, hidden // pieces, d), F32),
        jax.ShapeDtypeStruct((pieces // 2, heads, width // pieces, d), F32),
    ]
    return pl.pallas_call(
        partial(local_kernel, chunk=16),
        grid=(rows_all // rows,),
        in_specs=[
            smem,
            smem,
            smem,
            pl.BlockSpec((rows, d), lambda i: (i, 0)),
            pl.BlockSpec((heads, rows, width), lambda i: (0, i, 0)),
            pl.BlockSpec((rows, d), lambda i: (i, 0)),
            pl.BlockSpec((rows, 1), lambda i: (i, 0)),
            whole,
            whole,
            whole,
            whole,
        ],
        out_specs=[
            pl.BlockSpec((heads, rows, width), lambda i: (0, i, 0)),
            pl.BlockSpec((SUM_ROWS, 8, d), lambda i: (0, 0, 0)),
        ]
        + [anywhere] * 6,
        out_shape=[
            jax.ShapeDtypeStruct((heads, rows_all, width), BF),
            jax.ShapeDtypeStruct((SUM_ROWS, 8, d), F32),
        ]
        + [h for h in halves for _ in range(2)],
        scratch_shapes=[
            pltpu.VMEM((rows, d), F32),
            pltpu.VMEM((rows, d), F32),
            pltpu.VMEM((rows, d), F32),
            pltpu.VMEM((rows, d), BF),
            pltpu.VMEM((nctx, KERNELS * SEQ_LEN, d), F32),
            pltpu.VMEM((nctx, KERNELS * SEQ_LEN, d), F32),
            pltpu.VMEM((nctx, KERNELS * SEQ_LEN, d), F32),
            pltpu.VMEM((nctx, KERNELS * SEQ_LEN, d), BF),
            pltpu.VMEM((rows, d), F32),
            pltpu.VMEM((rows, d), F32),
            pltpu.VMEM((heads, rows, hidden), BF),
            pltpu.VMEM((heads, rows, hidden), F32),
            pltpu.VMEM((nctx, KERNELS * SEQ_LEN, 2 * SEQ_LEN), BF),
            pltpu.VMEM((nctx, SEQ_LEN, KERNELS * SEQ_LEN), BF),
            pltpu.VMEM((heads, d, hidden), F32),
            pltpu.VMEM((heads, hidden, d), F32),
            pltpu.VMEM((heads, pieces, width // pieces, d), F32),
            pltpu.SemaphoreType.DMA((3, pieces)),
        ],
        compiler_params=pltpu.CompilerParams(vmem_limit_bytes=56 * MIB),
        name="local_layer",
    )(starts, prm, me, x, spec, target, valid, up, down, out, bias)


def adam_kernel(me_ref, scale_ref, *refs):
    scale = scale_ref[0]
    count = len(refs) // 7
    for k in range(count):
        grad, weight, first, second = refs[4 * k : 4 * k + 4]
        outs = refs[4 * count + 3 * k : 4 * count + 3 * k + 3]
        g = grad[...] * scale
        m = BETA_ONE * first[...] + (1.0 - BETA_ONE) * g
        v = BETA_TWO * second[...] + (1.0 - BETA_TWO) * g * g
        first_hat = m * (1.0 / (1.0 - BETA_ONE**STEP))
        second_hat = v * (1.0 / (1.0 - BETA_TWO**STEP))
        w = weight[...]
        outs[0][...] = w - LEARN_RATE * (first_hat / (jnp.sqrt(second_hat) + EPSILON) + DECAY * w)
        outs[1][...] = m
        outs[2][...] = v


def adam_call(me, scale, items):
    pieces = items[0][0].shape[0]
    operands, specs, out_specs, out_shapes = [], [], [], []
    for grad, *states in items:
        block = (1,) + grad.shape[1:]
        zeros = (0,) * (grad.ndim - 1)
        specs.append(pl.BlockSpec(block, lambda i, me_ref, z=zeros: (i ^ me_ref[0],) + z))
        operands.append(grad)
        for state, axis in states:
            shape = state.shape
            state_block = shape[:axis] + (1,) + shape[axis + 1 :]
            spec = pl.BlockSpec(
                state_block,
                lambda i, me_ref, a=axis, n=len(shape): (0,) * a + (i,) + (0,) * (n - a - 1),
            )
            specs.append(spec)
            operands.append(state)
            out_specs.append(spec)
            out_shapes.append(jax.ShapeDtypeStruct(shape, F32))
    return pl.pallas_call(
        adam_body_for(items),
        grid_spec=pltpu.PrefetchScalarGridSpec(
            num_scalar_prefetch=1,
            grid=(pieces,),
            in_specs=[pl.BlockSpec(memory_space=pltpu.SMEM)] + specs,
            out_specs=out_specs,
        ),
        out_shape=out_shapes,
        compiler_params=pltpu.CompilerParams(vmem_limit_bytes=48 * MIB),
        name="adam",
    )(me, scale, *operands)


def adam_body_for(items):
    def body(me_ref, scale_ref, *refs):
        count = len(refs) // 7
        views = []
        for k in range(count):
            grad = refs[4 * k]
            axis = items[k][1][1]
            views.append(grad.at[0])
            for ref in refs[4 * k + 1 : 4 * k + 4]:
                views.append(ref.at[(slice(None),) * axis + (0,)])
        outs = []
        for k in range(count):
            axis = items[k][1][1]
            for ref in refs[4 * count + 3 * k : 4 * count + 3 * k + 3]:
                outs.append(ref.at[(slice(None),) * axis + (0,)])
        adam_kernel(me_ref, scale_ref, *views, *outs)

    return body


def adam_step(weight, gradient, moment_one, second):
    moment_one = BETA_ONE * moment_one + (1.0 - BETA_ONE) * gradient
    second = BETA_TWO * second + (1.0 - BETA_TWO) * gradient * gradient
    first_hat = moment_one / (1.0 - BETA_ONE**STEP)
    second_hat = second / (1.0 - BETA_TWO**STEP)
    weight = weight - LEARN_RATE * (first_hat / (jnp.sqrt(second_hat) + EPSILON) + DECAY * weight)
    return (weight, moment_one, second)


def swap(value, axis, size, bit):
    return lax.ppermute(value, axis, [(i, i ^ (1 << bit)) for i in range(size)])


def reduce_pieces(send, keep, size, order):
    bits = size.bit_length() - 1
    piece = keep.shape[1:]
    now = keep + swap(send, "dp", size, 0)
    now = now.reshape((2,) * (bits - 1) + piece)
    left = list(range(bits - 1, 0, -1))
    for bit in order:
        at = left.index(bit)
        away = lax.index_in_dim(now, 1, at, keepdims=False)
        stay = lax.index_in_dim(now, 0, at, keepdims=False)
        now = stay + swap(away, "dp", size, bit)
        left.remove(bit)
    return now


def gather_pieces(piece, size, order):
    have = []
    now = piece
    for bit in order:
        at = len([b for b in have if b > bit])
        now = jnp.stack([now, swap(now, "dp", size, bit)], axis=at)
        have = sorted(have + [bit], reverse=True)
    return now.reshape((size,) + piece.shape)


def sum_everywhere(value, sizes):
    for axis, size in sizes:
        for bit in range(size.bit_length() - 1):
            value = value + swap(value, axis, size, bit)
    return value


def split_low(table):
    high = lax.reduce_precision(table, 8, 7)
    return high.astype(BF), (table - high).astype(BF)


def spectral_tables(mode_index):
    heads = mode_index.shape[0]
    steps = jnp.arange(SEQ_LEN, dtype=jnp.int32)
    angles = (mode_index[:, :, None] * steps % SEQ_LEN).astype(F32) * (2.0 * math.pi / SEQ_LEN)
    ahead = jnp.concatenate([jnp.cos(angles), -jnp.sin(angles)], axis=1)
    if heads == 1:
        ahead = jnp.concatenate([ahead, jnp.zeros_like(ahead)], axis=0)
    ahead = ahead.reshape(2 * SEQ_LEN, SEQ_LEN)
    orders = jnp.arange(MODES, dtype=jnp.int32)
    angles = (steps[:, None] * orders % SEQ_LEN).astype(F32) * (2.0 * math.pi / SEQ_LEN)
    weights = jnp.where(orders == 0, 1.0, 2.0).astype(F32) / SEQ_LEN
    back = jnp.concatenate([jnp.cos(angles) * weights, -jnp.sin(angles) * weights], axis=1)
    return tuple(
        jnp.concatenate(split_low(t), axis=1) for t in (ahead, back, back.T, ahead.T)
    )


def on_device(
    sizes,
    series,
    target,
    valid,
    window_id,
    mode_index,
    query_weight,
    query_first,
    query_second,
    out_weight,
    out_first,
    out_second,
    mode_weight,
    mode_first,
    mode_second,
    up_weight,
    up_first,
    up_second,
    down_weight,
    down_first,
    down_second,
    bias_pair,
    bias_first,
    bias_second,
    decomp_params,
    decomp_first,
    decomp_second,
):
    ndp, nhead = sizes
    bits = ndp.bit_length() - 1
    order_a = list(range(1, bits))
    order_b = order_a[::-1]
    dp = lax.axis_index("dp")
    head = lax.axis_index("head")
    me = dp.astype(jnp.int32).reshape(1)
    rows, d = series.shape
    own_heads = mode_index.shape[0]
    width = query_weight.shape[1]
    hidden = up_weight.shape[1]

    query_all = lax.all_gather(query_weight.astype(BF), "head")
    packed = jnp.concatenate(
        [w.astype(BF).reshape(-1, d) for w in (up_weight, down_weight, out_weight)], axis=0
    )
    part = packed.shape[0] // ndp
    packed = lax.dynamic_slice_in_dim(packed, dp * part, part, 0)
    packed = lax.all_gather(lax.all_gather(packed, "head"), "dp")
    packed = packed.transpose(1, 0, 2, 3).reshape(nhead, -1, d)
    up_all = packed[:, :hidden].reshape(nhead, d, hidden)
    down_all = packed[:, hidden : 2 * hidden]
    out_all = packed[:, 2 * hidden :]

    tf, ti, tit, tft = spectral_tables(mode_index)
    wc = mode_weight.astype(BF).reshape(2, own_heads, HEAD_DIM, HEAD_DIM, MODES)
    wc = wc.transpose(4, 0, 2, 1, 3).reshape(MODES, 2, HEAD_DIM, own_heads * HEAD_DIM)

    def wide(v):
        pad = LANES - v.shape[-1]
        return jnp.pad(v, [(0, 0)] * (v.ndim - 1) + [(0, pad)]) if pad else v

    wc = wide(wc)

    def exchange(v):
        return lax.all_to_all(v, "head", 0, 0, tiled=True)

    queries = exchange(query_call(series, query_all, bias_pair[0]))
    queries = wide(queries.reshape(-1, SEQ_LEN, width))
    spectrum, modes_in = spectrum_call(queries, wc, tf, ti)
    spectrum = exchange(spectrum[:, :, :width].reshape(nhead, rows, width))

    series_late, spectrum = lax.optimization_barrier((series, spectrum))
    neighbours = [series] + [
        lax.ppermute(series_late, "head", [(i, (i + r) % nhead) for i in range(nhead)])
        for r in range(1, nhead)
    ]

    starts = jnp.sum(window_id[:, None, :] < jnp.arange(5)[None, :, None], axis=2).astype(jnp.int32)
    valid_float = valid.astype(F32)
    local = local_call(
        starts,
        decomp_params,
        me,
        series,
        spectrum,
        target,
        valid_float[:, None],
        up_all,
        down_all,
        out_all,
        bias_pair[1:],
        ndp,
    )
    d_spectrum, sums, up_send, up_keep, down_send, down_keep, out_send, out_keep = local

    d_spectrum = wide(exchange(d_spectrum).reshape(-1, SEQ_LEN, width))
    d_modes, mode_send, mode_keep = mode_grad_call(me, d_spectrum, modes_in, tit, ndp)
    d_queries, bias_part = query_grad_call(d_modes, wc, tft)
    d_queries = d_queries[:, :, :width].reshape(nhead, rows, width)
    d_query = sum(
        dot(x, lax.dynamic_index_in_dim(d_queries, lax.rem(head + nhead - r, nhead), 0, False), 0, 0)
        for r, x in enumerate(neighbours)
    )

    sums = jnp.sum(sums, axis=1)
    bias_zero = lax.dynamic_update_slice_in_dim(
        jnp.zeros((d,), F32), jnp.sum(bias_part, axis=0)[:width], head * width, 0
    )
    small = jnp.concatenate(
        [bias_zero, sums[SUM_BIAS], jnp.sum(sums[:SUM_BIAS], axis=1), jnp.sum(valid_float)[None]]
    )
    small = jnp.pad(small, (0, -small.shape[0] % LANES)).reshape(-1, LANES)
    everyone = (("dp", ndp), ("head", nhead))
    small = sum_everywhere(small, everyone).reshape(-1)
    loss_sum = small[2 * d + SUM_LOSS]
    valid_count = small[2 * d + SUM_BIAS]
    bias_grad = small[: 2 * d].reshape(2, d) / valid_count
    flat = small[2 * d : 2 * d + 4 * KERNELS]
    decomp_grad = flat.reshape(2, 2, KERNELS) / valid_count

    up_piece = jnp.sum(exchange(reduce_pieces(up_send, up_keep, ndp, order_a)), axis=0)
    down_piece = jnp.sum(exchange(reduce_pieces(down_send, down_keep, ndp, order_b)), axis=0)
    out_piece = jnp.sum(exchange(reduce_pieces(out_send, out_keep, ndp, order_a)), axis=0)
    query_piece = jnp.sum(
        lax.all_to_all(d_query.reshape(ndp, d // ndp, width), "dp", 0, 0, tiled=True), axis=0
    )
    half = MODES // 2
    mode_piece = jnp.concatenate(
        [
            reduce_pieces(mode_send[:, :half], mode_keep[:, :half], ndp, order_a),
            reduce_pieces(mode_send[:, half:], mode_keep[:, half:], ndp, order_b),
        ],
        axis=0,
    )
    depth = HEAD_DIM // ndp
    mode_piece = mode_piece.reshape(MODES, 2, depth, 2, HEAD_DIM).transpose(1, 3, 2, 4, 0)
    mode_piece = mode_piece.reshape(2, 2, depth, HEAD_DIM * MODES)[:, :own_heads]

    pieces = (query_piece, out_piece, mode_piece, up_piece, down_piece)
    squares = sum(jnp.sum(p * p) for p in pieces)
    squares = sum_everywhere(jnp.broadcast_to(squares, (8, LANES)), everyone)[0, 0]
    inverse = 1.0 / valid_count
    grad_norm = jnp.sqrt(
        squares * inverse * inverse
        + jnp.sum(bias_grad * bias_grad)
        + jnp.sum(decomp_grad * decomp_grad)
    )
    factor = jnp.minimum(1.0, CLIP_NORM / (grad_norm + 1e-06))

    down_order = list(range(bits - 1, -1, -1))
    up_order = order_a[:] + [0]
    query_g = gather_pieces(query_piece, ndp, down_order)
    out_g = gather_pieces(out_piece, ndp, down_order)
    up_g = gather_pieces(up_piece, ndp, down_order)
    down_g = gather_pieces(down_piece, ndp, up_order)
    mode_g = jnp.concatenate(
        [
            gather_pieces(mode_piece[:1], ndp, down_order),
            gather_pieces(mode_piece[1:], ndp, up_order),
        ],
        axis=1,
    )

    def cut(arrays, axis):
        return [
            (a.reshape(a.shape[:axis] + (ndp, a.shape[axis] // ndp) + a.shape[axis + 1 :]), axis)
            for a in arrays
        ]

    states = (
        (query_weight, query_first, query_second),
        (out_weight, out_first, out_second),
        (mode_weight, mode_first, mode_second),
        (up_weight, up_first, up_second),
        (down_weight, down_first, down_second),
    )
    axes = (0, 0, 2, 0, 0)
    items = [
        (g, *cut(s, a)) for g, s, a in zip((query_g, out_g, mode_g, up_g, down_g), states, axes)
    ]
    news = adam_call(me, (factor * inverse).reshape(1), items)
    news = [n.reshape(states[k // 3][0].shape) for k, n in enumerate(news)]
    news += adam_step(bias_pair, bias_grad * factor, bias_first, bias_second)
    news += adam_step(decomp_params, decomp_grad * factor, decomp_first, decomp_second)
    return (loss_sum, valid_count, grad_norm, *news)


def solution(mesh):
    rows = P(("dp", "head"), None)
    down = P("head", None)
    across = P(None, "head")
    modes = P(None, "head", None, None)
    weights = (across,) * 3 + (down,) * 3 + (modes,) * 3 + (across,) * 3 + (down,) * 3 + (P(),) * 6
    sizes = (mesh.shape["dp"], mesh.shape["head"])
    return jax.shard_map(
        partial(on_device, sizes),
        mesh=mesh,
        in_specs=(rows, rows, P(("dp", "head")), rows, down) + weights,
        out_specs=(P(), P(), P()) + weights,
        check_vma=False,
    )
```

```python
from functools import partial
import math

import jax
import jax.numpy as jnp
from jax import lax
from jax.experimental import pallas as pl
from jax.experimental.pallas import tpu as pltpu
from jax.sharding import PartitionSpec as P

MODES = 64
SEQ_LEN = 128
HEAD_DIM = 64
STEP = 10
KERNEL_WIDTHS = (7, 12, 14, 24, 48)
KERNELS = len(KERNEL_WIDTHS)
BETA_ONE = 0.9
BETA_TWO = 0.999
LEARN_RATE = 0.05
EPSILON = 1e-08
DECAY = 0.01
CLIP_NORM = 0.02
LOG2E = math.log2(math.e)
LANES = 128
BF = jnp.bfloat16
F32 = jnp.float32
MIB = 1 << 20

ERF_P = 0.3275911
ERF_A = (0.254829592, -0.284496736, 1.421413741, -1.453152027, 1.061405429)


def dot(a, b, ca=1, cb=0):
    return lax.dot_general(a, b, (((ca,), (cb,)), ((), ())), preferred_element_type=F32)


def cost(microseconds, moved):
    return pl.CostEstimate(
        flops=int(microseconds * 1.1e9), bytes_accessed=int(moved), transcendentals=0
    )


def query_kernel(head_ref, x_ref, b_ref, *refs):
    heads = len(refs) // 2
    x = x_ref[...]
    for r in range(heads):
        bias = b_ref[lax.rem(head_ref[0] + r, heads)]
        refs[heads + r][...] = (dot(x, refs[r][...]) + bias).astype(BF)


def query_call(head, x, bias_row, weights):
    rows, d = x.shape
    heads = len(weights)
    width = weights[0].shape[1]
    step = min(256, rows)
    return pl.pallas_call(
        query_kernel,
        grid=(rows // step,),
        in_specs=[
            pl.BlockSpec(memory_space=pltpu.SMEM),
            pl.BlockSpec((step, d), lambda i: (i, 0)),
            pl.BlockSpec((heads, 1, width), lambda i: (0, 0, 0)),
        ]
        + [pl.BlockSpec((d, width), lambda i: (0, 0)) for _ in weights],
        out_specs=[pl.BlockSpec((step, width), lambda i: (i, 0)) for _ in weights],
        out_shape=[jax.ShapeDtypeStruct((rows, width), BF) for _ in weights],
        compiler_params=pltpu.CompilerParams(vmem_limit_bytes=24 * MIB),
        cost_estimate=cost(2.5, 3e6),
        name="queries",
    )(head, x, bias_row.reshape(heads, 1, width), *weights)


def lane_low(rows):
    return lax.broadcasted_iota(jnp.int32, (rows, LANES), 1) < HEAD_DIM


def mix_blocks(wt_ref, m, count):
    low = lane_low(HEAD_DIM)
    zero = jnp.zeros((HEAD_DIM, LANES), F32)
    left = [
        wt_ref[pl.ds(c * HEAD_DIM * MODES + m, HEAD_DIM, stride=MODES), :] for c in range(2)
    ]
    blocks = []
    for _ in range(count):
        terms = [v.astype(BF).astype(F32) for v in left]
        left = [v - t for v, t in zip(left, terms)]
        real, imag = (
            jnp.concatenate([jnp.where(low, t, zero), jnp.where(low, zero, t)], axis=0)
            for t in terms
        )
        top = jnp.concatenate([real, -imag], axis=1)
        bottom = jnp.concatenate([imag, real], axis=1)
        blocks.append(jnp.concatenate([top, bottom], axis=0).astype(BF))
    return blocks


def pair_width(contexts):
    return 2 if contexts % 2 == 0 else 1


def spectrum_kernel(wt_ref, tf_ref, ti_ref, *refs):
    owners = (len(refs) - 3) // 3
    q_refs, spec_refs = refs[:owners], refs[owners : 3 * owners]
    xs_ref, x_scr, y_scr = refs[3 * owners :]
    run, width = q_refs[0].shape[0], q_refs[0].shape[2]
    half = run // 2
    contexts = owners * run
    pair = pair_width(half)
    low = lane_low(SEQ_LEN)

    for r in range(owners):

        def forward(p, _, r=r):
            cols = jnp.concatenate([q_refs[r][p * pair + k] for k in range(pair)], axis=1)
            res = dot(tf_ref[...], jnp.concatenate([cols, cols], axis=0))
            for k in range(pair):
                part = res[:, k * LANES : (k + 1) * LANES]
                row = (r * run + p * pair + k) * SEQ_LEN
                x_scr[pl.ds(pl.multiple_of(row, SEQ_LEN), SEQ_LEN), :] = jnp.where(
                    low, part[:SEQ_LEN], part[SEQ_LEN:]
                )
            return 0

        lax.fori_loop(0, run // pair, forward, 0)

    def mix(m, _):
        xr = x_scr[pl.ds(m, contexts, stride=SEQ_LEN), :].astype(BF)
        xi = x_scr[pl.ds(MODES + m, contexts, stride=SEQ_LEN), :].astype(BF)
        xs_ref[m] = jnp.concatenate([xr, xi], axis=0)
        x = jnp.concatenate([xr, xi], axis=1)
        main, rest = mix_blocks(wt_ref, m, 2)
        y = dot(x, main, 1, 1) + dot(x, rest, 1, 1)
        y_scr[pl.ds(m, contexts, stride=SEQ_LEN), :] = y[:, :LANES]
        y_scr[pl.ds(MODES + m, contexts, stride=SEQ_LEN), :] = y[:, LANES:]
        return 0

    lax.fori_loop(0, MODES, mix, 0, unroll=4)

    for r in range(owners):
        for number in range(2):
            target = spec_refs[number * owners + r]

            def inverse(p, _, r=r, number=number, target=target):
                parts = []
                for k in range(pair):
                    row = (r * run + number * half + p * pair + k) * SEQ_LEN
                    parts.append(y_scr[pl.ds(pl.multiple_of(row, SEQ_LEN), SEQ_LEN), :])
                cols = jnp.concatenate(parts, axis=1)
                main = cols.astype(BF)
                rest = (cols - main.astype(F32)).astype(BF)
                res = dot(ti_ref[...], jnp.concatenate([main, main, rest], axis=0)).astype(BF)
                for k in range(pair):
                    target[p * pair + k] = res[:, k * LANES : (k + 1) * LANES]
                return 0

            lax.fori_loop(0, half // pair, inverse, 0)


def spectrum_call(queries, wt, tf, ti):
    owners = len(queries)
    run = queries[0].shape[0]
    contexts = owners * run
    out = jax.ShapeDtypeStruct((run // 2, SEQ_LEN, LANES), BF)
    res = pl.pallas_call(
        spectrum_kernel,
        out_shape=[out] * (2 * owners)
        + [jax.ShapeDtypeStruct((MODES, 2 * contexts, LANES), BF)],
        scratch_shapes=[
            pltpu.VMEM((contexts * SEQ_LEN, LANES), F32),
            pltpu.VMEM((contexts * SEQ_LEN, LANES), F32),
        ],
        compiler_params=pltpu.CompilerParams(vmem_limit_bytes=32 * MIB),
        cost_estimate=cost(15, 7e6),
        name="spectrum",
    )(wt, tf, ti, *queries)
    return res[:owners], res[owners : 2 * owners], res[2 * owners]


def query_grad_kernel(wt_ref, tit_ref, tft_ref, *refs):
    owners = (len(refs) - 4) // 3
    d_refs, dq_refs = refs[: 2 * owners], refs[2 * owners : 3 * owners]
    dy_ref, bias_ref, y_scr, x_scr = refs[3 * owners :]
    half = d_refs[0].shape[0]
    run = 2 * half
    contexts = owners * run
    pair = pair_width(half)
    low = lane_low(SEQ_LEN)
    zero = jnp.zeros((SEQ_LEN, LANES), F32)

    for number in range(2):
        for r in range(owners):
            source = d_refs[number * owners + r]

            def forward(p, _, number=number, r=r, source=source):
                cols = jnp.concatenate([source[p * pair + k] for k in range(pair)], axis=1)
                res = dot(tit_ref[...], jnp.concatenate([cols, cols], axis=0))
                for k in range(pair):
                    row = (r * run + number * half + p * pair + k) * SEQ_LEN
                    y_scr[pl.ds(pl.multiple_of(row, SEQ_LEN), SEQ_LEN), :] = res[
                        :, k * LANES : (k + 1) * LANES
                    ]
                return 0

            lax.fori_loop(0, half // pair, forward, 0)

    def mix(m, _):
        yr = y_scr[pl.ds(m, contexts, stride=SEQ_LEN), :].astype(BF)
        yi = y_scr[pl.ds(MODES + m, contexts, stride=SEQ_LEN), :].astype(BF)
        dy = jnp.concatenate([yr, yi], axis=1)
        dy_ref[m] = dy
        dx = dot(dy, mix_blocks(wt_ref, m, 1)[0])
        x_scr[pl.ds(m, contexts, stride=SEQ_LEN), :] = dx[:, :LANES]
        x_scr[pl.ds(MODES + m, contexts, stride=SEQ_LEN), :] = dx[:, LANES:]
        return 0

    lax.fori_loop(0, MODES, mix, 0, unroll=4)
    bias_ref[...] = jnp.zeros_like(bias_ref)

    for r in range(owners):

        def inverse(p, _, r=r):
            parts = []
            for k in range(pair):
                row = (r * run + p * pair + k) * SEQ_LEN
                one = x_scr[pl.ds(pl.multiple_of(row, SEQ_LEN), SEQ_LEN), :]
                parts.append(
                    jnp.concatenate([jnp.where(low, one, zero), jnp.where(low, zero, one)], axis=0)
                )
            cols = jnp.concatenate(parts, axis=1).astype(BF)
            res = dot(tft_ref[...], jnp.concatenate([cols, cols], axis=0)).astype(BF)
            total = jnp.zeros((8, LANES), F32)
            for k in range(pair):
                one = res[:, k * LANES : (k + 1) * LANES]
                dq_refs[r][p * pair + k] = one
                total = total + jnp.sum(one.astype(F32).reshape(SEQ_LEN // 8, 8, LANES), axis=0)
            bias_ref[...] += total
            return 0

        lax.fori_loop(0, run // pair, inverse, 0)


def query_grad_call(first, second, wt, tit, tft, waits):
    owners = len(first)
    run = 2 * first[0].shape[0]
    contexts = owners * run
    whole = pl.BlockSpec(memory_space=pltpu.VMEM)

    def body(*refs):
        at = 3 + 2 * owners
        query_grad_kernel(*refs[:at], *refs[at + len(waits) :])

    res = pl.pallas_call(
        body,
        in_specs=[whole] * (3 + 2 * owners) + [pl.BlockSpec(memory_space=pl.ANY)] * len(waits),
        out_shape=[jax.ShapeDtypeStruct((run, SEQ_LEN, LANES), BF)] * owners
        + [
            jax.ShapeDtypeStruct((MODES, contexts, 2 * LANES), BF),
            jax.ShapeDtypeStruct((8, LANES), F32),
        ],
        scratch_shapes=[
            pltpu.VMEM((contexts * SEQ_LEN, LANES), F32),
            pltpu.VMEM((contexts * SEQ_LEN, LANES), F32),
        ],
        compiler_params=pltpu.CompilerParams(vmem_limit_bytes=32 * MIB),
        cost_estimate=cost(11, 7e6),
        name="query_grads",
    )(wt, tit, tft, *first, *second, *waits)
    return res[:owners], res[owners], res[owners + 1]


def mode_grad_kernel(me_ref, dy_ref, xs_ref, *refs):
    outs = refs[:4]
    dw_scr, sems = refs[4:]
    pieces, depth = 2 * outs[0].shape[0], outs[0].shape[1]
    total = HEAD_DIM * MODES
    low = lane_low(HEAD_DIM)
    me = me_ref[0]

    def mix(m, _):
        dy = dy_ref[m]
        yr, yi = dy[:, :LANES], dy[:, LANES:]
        right = jnp.concatenate(
            [jnp.concatenate([yr, yi], axis=0), jnp.concatenate([yi, -yr], axis=0)], axis=1
        )
        dw = dot(right, xs_ref[m], 0, 0)
        for c in range(2):
            first = 2 * c * HEAD_DIM
            part = jnp.where(
                low, dw[first : first + HEAD_DIM], dw[first + HEAD_DIM : first + 2 * HEAD_DIM]
            )
            dw_scr[pl.ds(c * total + m, HEAD_DIM, stride=MODES), :] = part
        return 0

    lax.fori_loop(0, MODES, mix, 0, unroll=4)
    copies = []
    for j in range(pieces):
        for c in range(2):
            start = pl.multiple_of(c * total + (me ^ j) * depth, depth)
            copies.append(
                pltpu.make_async_copy(
                    dw_scr.at[pl.ds(start, depth), :],
                    outs[2 * c + (j + 1) % 2].at[j // 2],
                    sems.at[c, j],
                )
            )
    for copy in copies:
        copy.start()
    for copy in copies:
        copy.wait()


def mode_grad_call(me, dy, xs, pieces):
    part = jax.ShapeDtypeStruct((pieces // 2, HEAD_DIM * MODES // pieces, LANES), F32)
    whole = pl.BlockSpec(memory_space=pltpu.VMEM)
    return pl.pallas_call(
        mode_grad_kernel,
        in_specs=[pl.BlockSpec(memory_space=pltpu.SMEM)] + [whole] * 2,
        out_specs=[pl.BlockSpec(memory_space=pl.ANY)] * 4,
        out_shape=[part] * 4,
        scratch_shapes=[
            pltpu.VMEM((2 * HEAD_DIM * MODES, LANES), F32),
            pltpu.SemaphoreType.DMA((2, pieces)),
        ],
        compiler_params=pltpu.CompilerParams(vmem_limit_bytes=40 * MIB),
        cost_estimate=cost(9, 8e6),
        name="mode_grads",
    )(me, dy, xs)


SUM_SLOPE = (0, 10)
SUM_OFFSET = (5, 15)
SUM_LOSS = 20
SUM_BIAS = 21
SUM_ROWS = 24


def window_counts(first, last, rows, cols, width):
    lead = width - 1 - (width - 1) // 2
    reach = cols - rows + (lead + 1)
    here = jnp.where(cols < first, 0, jnp.where(cols >= last, width, jnp.clip(reach, 0, width)))
    before = jnp.where(
        cols <= first, 0, jnp.where(cols > last, width, jnp.clip(reach - 1, 0, width))
    )
    return (here - before).astype(F32)


def window_edges(starts, rows):
    s1, s2, s3 = starts
    first = jnp.where(rows >= s3, s3, jnp.where(rows >= s2, s2, jnp.where(rows >= s1, s1, 0)))
    last = jnp.where(
        rows < s1, s1 - 1, jnp.where(rows < s2, s2 - 1, jnp.where(rows < s3, s3 - 1, SEQ_LEN - 1))
    )
    return first, last


def fold(v):
    return jnp.sum(v.reshape(v.shape[0] // 8, 8, v.shape[1]), axis=0)


def local_kernel(*refs, chunk, hidden_width, heads, waits):
    refs = list(refs)

    def take(n):
        taken = refs[:n]
        del refs[:n]
        return taken

    starts_ref, prm_ref, me_ref, x_ref, tgt_ref, val_ref, bias_ref = take(7)
    spec_refs = take(heads)
    packed_refs = take(4)
    take(waits)
    dspec_refs = take(heads)
    act_ref, dhid_ref, low_ref, dfeed_ref, spec_out, dattn_ref, sums_ref = take(7)
    (
        u_scr,
        trend_scr,
        season_scr,
        av1_scr,
        share_scr,
        av2_scr,
        da_scr,
        part_scr,
        g_scr,
        slope_scr,
        a_scr,
        at_scr,
        weights,
        weight_sems,
    ) = refs
    step = pl.program_id(0)
    rows, d = x_ref.shape
    nctx = rows // SEQ_LEN
    out_width = dspec_refs[0].shape[1]
    up_rows = slice(0, hidden_width)
    down_rows = slice(hidden_width, 2 * hidden_width)
    out_rows = slice(2 * hidden_width, 2 * hidden_width + out_width)
    groups = d // LANES
    loops = SEQ_LEN // chunk

    @pl.when(step == 0)
    def _():
        count, shared, part, _ = packed_refs[0].shape
        copies = []
        for number, ref in enumerate(packed_refs):
            group, bit = number // 2, number % 2
            for k in range(count):
                for r in range(shared):
                    row = pl.multiple_of((me_ref[0] ^ (2 * k + bit)) * part, part)
                    copies.append(
                        pltpu.make_async_copy(
                            ref.at[k, r],
                            weights.at[(heads - group * shared - r) % heads, pl.ds(row, part), :],
                            weight_sems.at[number, k * shared + r],
                        )
                    )
        for copy in copies:
            copy.start()
        sums_ref[...] = jnp.zeros_like(sums_ref)
        for copy in copies:
            copy.wait()

    row_ids = lax.broadcasted_iota(jnp.int32, (SEQ_LEN, SEQ_LEN), 0)
    col_ids = lax.broadcasted_iota(jnp.int32, (SEQ_LEN, SEQ_LEN), 1)
    for c in range(nctx):
        starts = [starts_ref[step * nctx + c, k] for k in range(1, 4)]
        first, last = window_edges(starts, row_ids)
        first_t, last_t = window_edges(starts, col_ids)
        for w, width in enumerate(KERNEL_WIDTHS):
            counts = window_counts(first, last, row_ids, col_ids, width).astype(BF)
            a_scr[c, w * SEQ_LEN : (w + 1) * SEQ_LEN, :SEQ_LEN] = counts
            a_scr[c, w * SEQ_LEN : (w + 1) * SEQ_LEN, SEQ_LEN:] = counts
            at_scr[c, :, w * SEQ_LEN : (w + 1) * SEQ_LEN] = window_counts(
                first_t, last_t, col_ids, row_ids, width
            ).astype(BF)

    def averages(c, u, av):
        high = u.astype(BF)
        rest = (u - high.astype(F32)).astype(BF)
        av[c] = dot(a_scr[c], jnp.concatenate([high, rest], axis=0))

    spec = jnp.concatenate([ref[...] for ref in spec_refs], axis=1)
    for h in range(heads):
        spec_out[h] = spec_refs[h][...]
    out_all = jnp.concatenate([weights[h, out_rows] for h in range(heads)], axis=0)
    pre = x_ref[...].astype(F32) + (dot(spec, out_all) + bias_ref[...])
    u_scr[...] = pre
    for c in range(nctx):
        averages(c, pre[c * SEQ_LEN : (c + 1) * SEQ_LEN], av1_scr)

    def shares_of(u, avs, layer):
        logits = [
            u * (prm_ref[layer, 0, w] * LOG2E) + prm_ref[layer, 1, w] * LOG2E
            for w in range(KERNELS)
        ]
        top = logits[0]
        for v in logits[1:]:
            top = jnp.maximum(top, v)
        powers = [jnp.exp2(v - top) for v in logits]
        total = powers[0]
        for v in powers[1:]:
            total = total + v
        scale = 1.0 / total
        shares = [v * scale for v in powers]
        trend = shares[0] * avs[0]
        for s, a in zip(shares[1:], avs[1:]):
            trend = trend + s * a
        return shares, trend

    def read_averages(av, c, row, lanes):
        return [
            av[c, pl.ds(w * SEQ_LEN + row, chunk), lanes] * (1.0 / width)
            for w, width in enumerate(KERNEL_WIDTHS)
        ]

    def pull(shares, avs, trend, grad, u, layer, base, c, row, lanes, sums):
        rest = base
        slopes, offsets = [], []
        for w, width in enumerate(KERNEL_WIDTHS):
            d_avg = shares[w] * grad
            da_scr[c, pl.ds(w * SEQ_LEN + row, chunk), lanes] = (d_avg * (1.0 / width)).astype(BF)
            d_logit = d_avg * (avs[w] - trend)
            rest = rest + d_logit * prm_ref[layer, 0, w]
            slopes.append(sums[w] + fold(d_logit * u))
            offsets.append(sums[KERNELS + w] + fold(d_logit))
        return rest, slopes + offsets

    for c in range(nctx):
        for g in range(groups):
            lanes = slice(g * LANES, (g + 1) * LANES)

            def first_pass(r, _, c=c, lanes=lanes):
                row = pl.multiple_of(r * chunk, chunk)
                at = pl.ds(c * SEQ_LEN + row, chunk)
                u = u_scr[at, lanes]
                avs = read_averages(av1_scr, c, row, lanes)
                shares, trend = shares_of(u, avs, 0)
                for w in range(KERNELS):
                    share_scr[c, pl.ds(w * SEQ_LEN + row, chunk), lanes] = shares[w]
                season = u - trend
                trend_scr[at, lanes] = trend
                season_scr[at, lanes] = season
                low_ref[at, lanes] = season.astype(BF)
                return 0

            lax.fori_loop(0, loops, first_pass, 0)

    season_low = low_ref[...]
    feed = jnp.zeros((rows, d), F32)
    for h in range(heads):
        hid = dot(season_low, weights[h, up_rows], 1, 1)
        z = jnp.abs(hid) * (2.0**-0.5)
        t = 1.0 / (1.0 + ERF_P * z)
        e = jnp.exp2(hid * hid * (-0.5 * LOG2E))
        poly = ERF_A[4]
        for coef in ERF_A[3::-1]:
            poly = poly * t + coef
        tail = (0.5 * t) * poly * e
        phi = jnp.where(hid < 0, tail, 1.0 - tail)
        active = (hid * phi).astype(BF)
        slope_scr[h] = phi + hid * e * ((2.0 * math.pi) ** -0.5)
        act_ref[h] = active
        feed = feed + dot(active, weights[h, down_rows])

    pre = season_scr[...] + feed
    g_scr[...] = pre
    for c in range(nctx):
        averages(c, pre[c * SEQ_LEN : (c + 1) * SEQ_LEN], av2_scr)

    for c in range(nctx):
        for g in range(groups):
            lanes = slice(g * LANES, (g + 1) * LANES)

            def second_pass(r, sums, c=c, lanes=lanes):
                row = pl.multiple_of(r * chunk, chunk)
                at = pl.ds(c * SEQ_LEN + row, chunk)
                u = g_scr[at, lanes]
                avs = read_averages(av2_scr, c, row, lanes)
                shares, trend = shares_of(u, avs, 1)
                misfit = trend_scr[at, lanes] + trend - tgt_ref[at, lanes]
                weighted = val_ref[at, :] * misfit
                grad = 2.0 * weighted
                rest, new = pull(
                    shares, avs, trend, grad, u, 1, jnp.zeros_like(u), c, row, lanes, sums
                )
                part_scr[at, lanes] = rest
                g_scr[at, lanes] = grad
                return tuple(new) + (sums[2 * KERNELS] + fold(weighted * misfit),)

            zeros = tuple(jnp.zeros((8, LANES), F32) for _ in range(2 * KERNELS + 1))
            sums = lax.fori_loop(0, loops, second_pass, zeros)
            for k in range(KERNELS):
                sums_ref[SUM_SLOPE[1] + k, :, lanes] += sums[k]
                sums_ref[SUM_OFFSET[1] + k, :, lanes] += sums[KERNELS + k]
            sums_ref[SUM_LOSS, :, lanes] += sums[2 * KERNELS]

    for c in range(nctx):
        at = slice(c * SEQ_LEN, (c + 1) * SEQ_LEN)
        part_scr[at, :] += dot(at_scr[c], da_scr[c])

    d_pre = part_scr[...]
    d_feed = d_pre.astype(BF)
    dfeed_ref[...] = d_feed
    back = d_pre
    for h in range(heads):
        d_hid = (dot(d_feed, weights[h, down_rows], 1, 1) * slope_scr[h]).astype(BF)
        back = back + dot(d_hid, weights[h, up_rows])
        dhid_ref[h] = d_hid
    season_scr[...] = back

    for c in range(nctx):
        for g in range(groups):
            lanes = slice(g * LANES, (g + 1) * LANES)

            def third_pass(r, sums, c=c, lanes=lanes):
                row = pl.multiple_of(r * chunk, chunk)
                at = pl.ds(c * SEQ_LEN + row, chunk)
                u = u_scr[at, lanes]
                avs = read_averages(av1_scr, c, row, lanes)
                shares = [
                    share_scr[c, pl.ds(w * SEQ_LEN + row, chunk), lanes] for w in range(KERNELS)
                ]
                d_season = season_scr[at, lanes]
                rest, new = pull(
                    shares,
                    avs,
                    trend_scr[at, lanes],
                    g_scr[at, lanes] - d_season,
                    u,
                    0,
                    d_season,
                    c,
                    row,
                    lanes,
                    sums,
                )
                part_scr[at, lanes] = rest
                return tuple(new)

            zeros = tuple(jnp.zeros((8, LANES), F32) for _ in range(2 * KERNELS))
            sums = lax.fori_loop(0, loops, third_pass, zeros)
            for k in range(KERNELS):
                sums_ref[SUM_SLOPE[0] + k, :, lanes] += sums[k]
                sums_ref[SUM_OFFSET[0] + k, :, lanes] += sums[KERNELS + k]

    for c in range(nctx):
        at = slice(c * SEQ_LEN, (c + 1) * SEQ_LEN)
        part_scr[at, :] += dot(at_scr[c], da_scr[c])

    d_pre = part_scr[...]
    sums_ref[SUM_BIAS] += fold(d_pre)
    d_attn = d_pre.astype(BF)
    dattn_ref[...] = d_attn
    d_spec = dot(d_attn, out_all, 1, 1).astype(BF)
    for h in range(heads):
        dspec_refs[h][...] = d_spec[:, h * out_width : (h + 1) * out_width]


def up8(n):
    return -(-n // 8) * 8


def local_call(number, spec, waits, starts, prm, me, x, target, valid, bias, packed, hidden):
    rows_half = x.shape[0] // 2
    d = x.shape[1]
    heads = len(spec)
    width = spec[0].shape[1]
    nctx = 2 if rows_half % (2 * SEQ_LEN) == 0 else 1
    rows = nctx * SEQ_LEN
    steps = rows_half // rows
    smem = pl.BlockSpec(memory_space=pltpu.SMEM)
    whole = pl.BlockSpec(memory_space=pltpu.VMEM)
    anywhere = pl.BlockSpec(memory_space=pl.ANY)
    averages = (nctx, KERNELS * SEQ_LEN, d)
    count, shared, part, _ = packed[0].shape

    def row_block(columns, half=0):
        return pl.BlockSpec((rows, columns), lambda i: (half * steps + i, 0))

    def head_block(columns):
        return pl.BlockSpec((heads, rows, columns), lambda i: (0, i, 0))

    ctx_half = starts.shape[0] // 2
    res = pl.pallas_call(
        partial(local_kernel, chunk=16, hidden_width=hidden, heads=heads, waits=len(waits)),
        grid=(steps,),
        in_specs=[smem] * 3
        + [row_block(d, number), row_block(d, number), row_block(1, number), whole]
        + [row_block(width)] * heads
        + [anywhere] * (len(packed) + len(waits)),
        out_specs=[row_block(width)] * heads
        + [head_block(hidden), head_block(hidden), row_block(d), row_block(d)]
        + [head_block(width), row_block(d)]
        + [pl.BlockSpec((SUM_ROWS, 8, d), lambda i: (0, 0, 0))],
        out_shape=[jax.ShapeDtypeStruct((rows_half, width), BF)] * heads
        + [jax.ShapeDtypeStruct((heads, rows_half, hidden), BF)] * 2
        + [jax.ShapeDtypeStruct((rows_half, d), BF)] * 2
        + [
            jax.ShapeDtypeStruct((heads, rows_half, width), BF),
            jax.ShapeDtypeStruct((rows_half, d), BF),
            jax.ShapeDtypeStruct((SUM_ROWS, 8, d), F32),
        ],
        scratch_shapes=[
            pltpu.VMEM((rows, d), F32),
            pltpu.VMEM((rows, d), F32),
            pltpu.VMEM((rows, d), F32),
            pltpu.VMEM(averages, F32),
            pltpu.VMEM(averages, F32),
            pltpu.VMEM(averages, F32),
            pltpu.VMEM(averages, BF),
            pltpu.VMEM((rows, d), F32),
            pltpu.VMEM((rows, d), F32),
            pltpu.VMEM((heads, rows, hidden), F32),
            pltpu.VMEM((nctx, KERNELS * SEQ_LEN, 2 * SEQ_LEN), BF),
            pltpu.VMEM((nctx, SEQ_LEN, KERNELS * SEQ_LEN), BF),
            pltpu.VMEM((heads, len(packed) * count // 2 * part, d), BF),
            pltpu.SemaphoreType.DMA((len(packed), count * shared)),
        ],
        compiler_params=pltpu.CompilerParams(vmem_limit_bytes=56 * MIB),
        cost_estimate=cost(38, 24e6),
        name="local_layer",
    )(
        starts[number * ctx_half : (number + 1) * ctx_half],
        prm,
        me,
        x,
        target,
        valid,
        bias,
        *spec,
        *packed,
        *waits,
    )
    return res[:heads], res[heads:-1], res[-1]


def outer_kernel(me_ref, *refs, halves, outs, waits):
    count = len(halves)
    scratch = refs[-1]
    ins = refs[: 2 * sum(halves)]
    targets = refs[2 * sum(halves) + waits : -1]
    for k in range(count):
        total = None
        for n in range(halves[k]):
            left, right = ins[2 * (sum(halves[:k]) + n) : 2 * (sum(halves[:k]) + n) + 2]
            left = left[0] if len(left.shape) == 3 else left[...]
            right = right[0] if len(right.shape) == 3 else right[...]
            term = dot(left, right, 0, 0)
            total = term if total is None else total + term
        where, offset = outs[k]
        send, keep = targets[2 * where : 2 * where + 2]
        pieces = 2 * send.shape[0]
        size = total.shape[0] // pieces
        lanes = slice(0, total.shape[1])
        if size % 8 == 0:
            scratch[: total.shape[0], lanes] = total
            for j in range(pieces):
                row = pl.multiple_of((me_ref[0] ^ j) * size, size)
                (send if j % 2 else keep)[j // 2, 0, offset : offset + size, :] = scratch[
                    pl.ds(row, size), lanes
                ]
        else:
            scratch[: total.shape[0], lanes] = total
            for j in range(pieces):
                (send if j % 2 else keep)[j // 2, 0, offset:, :] = jnp.zeros(
                    (send.shape[2] - offset, total.shape[1]), F32
                )
                for i in range(size):
                    (send if j % 2 else keep)[j // 2, 0, offset + i : offset + i + 1, :] = scratch[
                        pl.ds((me_ref[0] ^ j) * size + i, 1), lanes
                    ]


def outer_call(me, products, shapes, outs, pieces, name, waits=()):
    heads = next(a.shape[0] for p in products for pair in p for a in pair if a.ndim == 3)
    operands = [a for p in products for pair in p for a in pair]

    def spec(a):
        if a.ndim == 3:
            return pl.BlockSpec((1,) + a.shape[1:], lambda h: (h, 0, 0))
        return pl.BlockSpec(a.shape, lambda h: (0, 0))

    out_specs = [
        pl.BlockSpec((pieces // 2, 1) + shape, lambda h: (0, h, 0, 0))
        for shape in shapes
        for _ in range(2)
    ]
    rows = max(pair[0].shape[-1] for p in products for pair in p)
    columns = max(pair[1].shape[-1] for p in products for pair in p)
    return pl.pallas_call(
        partial(outer_kernel, halves=[len(p) for p in products], outs=outs, waits=len(waits)),
        grid=(heads,),
        in_specs=[pl.BlockSpec(memory_space=pltpu.SMEM)]
        + [spec(a) for a in operands]
        + [pl.BlockSpec(memory_space=pl.ANY)] * len(waits),
        out_specs=out_specs,
        out_shape=[
            jax.ShapeDtypeStruct((pieces // 2, heads) + shape, F32)
            for shape in shapes
            for _ in range(2)
        ],
        scratch_shapes=[pltpu.VMEM((rows, columns), F32)],
        compiler_params=pltpu.CompilerParams(vmem_limit_bytes=48 * MIB),
        cost_estimate=cost(8, 20e6),
        name=name,
    )(me, *operands, *waits)


def adam_values(weight, gradient, first, second):
    m = BETA_ONE * first + (1.0 - BETA_ONE) * gradient
    v = BETA_TWO * second + (1.0 - BETA_TWO) * gradient * gradient
    first_hat = m * (1.0 / (1.0 - BETA_ONE**STEP))
    second_hat = v * (1.0 / (1.0 - BETA_TWO**STEP))
    return (
        weight - LEARN_RATE * (first_hat / (jnp.sqrt(second_hat) + EPSILON) + DECAY * weight),
        m,
        v,
    )


def adam_kernel(me_ref, scale_ref, *refs, views, leads, grads):
    scale = scale_ref[0]
    count = len(views)
    pairs = refs[: 2 * grads]
    states = refs[2 * grads : 2 * grads + 3 * count]
    outs = refs[2 * grads + 3 * count : 2 * grads + 6 * count]
    chosen = refs[2 * grads + 6 * count :]
    other = (pl.program_id(0) ^ me_ref[0]) & 1

    @pl.when(other == 0)
    def _():
        for k in range(grads):
            chosen[k][...] = pairs[2 * k][0]

    @pl.when(other == 1)
    def _():
        for k in range(grads):
            chosen[k][...] = pairs[2 * k + 1][0]

    for k, parts in enumerate(views):
        lead = leads[k]
        for which, source, place in parts:
            ins = [r.at[lead][place] for r in states[3 * k : 3 * k + 3]]
            g = chosen[which][source] * scale
            new = adam_values(ins[0], g, ins[1], ins[2])
            for r, value in zip(outs[3 * k : 3 * k + 3], new):
                r.at[lead][place] = value


def adam_call(me, scale, grads, views, states, axes):
    pieces = 2 * grads[0][0].shape[0]
    specs, out_specs, operands, shapes, leads = [], [], [], [], []
    for pair in grads:
        zeros = (0,) * (pair[0].ndim - 1)
        for grad in pair:
            specs.append(
                pl.BlockSpec(
                    (1,) + grad.shape[1:],
                    lambda i, me_ref, z=zeros: (lax.div(i ^ me_ref[0], 2),) + z,
                )
            )
            operands.append(grad)
    for group, axis in zip(states, axes):
        shape = group[0].shape
        size = shape[axis] // pieces
        direct = size % (LANES if axis == len(shape) - 1 else 8) == 0
        if not direct:
            shape = shape[:axis] + (pieces, size) + shape[axis + 1 :]
        block = shape[:axis] + (size if direct else 1,) + shape[axis + 1 :]
        leads.append((slice(None),) * axis + ((slice(None),) if direct else (0,)))
        for state in group:
            spec = pl.BlockSpec(
                block,
                lambda i, me_ref, a=axis, n=len(shape): (0,) * a + (i,) + (0,) * (n - a - 1),
            )
            specs.append(spec)
            out_specs.append(spec)
            operands.append(state.reshape(shape))
            shapes.append(jax.ShapeDtypeStruct(shape, F32))
    news = pl.pallas_call(
        partial(adam_kernel, views=views, leads=leads, grads=len(grads)),
        grid_spec=pltpu.PrefetchScalarGridSpec(
            num_scalar_prefetch=1,
            grid=(pieces,),
            in_specs=[pl.BlockSpec(memory_space=pltpu.SMEM)] + specs,
            out_specs=out_specs,
            scratch_shapes=[pltpu.VMEM(pair[0].shape[1:], F32) for pair in grads],
        ),
        out_shape=shapes,
        compiler_params=pltpu.CompilerParams(vmem_limit_bytes=48 * MIB),
        cost_estimate=cost(15, 48e6),
        name="adam",
    )(me, scale, *operands)
    return [n.reshape(states[k // 3][0].shape) for k, n in enumerate(news)]


def swap(value, axis, size, bit):
    return lax.ppermute(value, axis, [(i, i ^ (1 << bit)) for i in range(size)])


def split_add(items):
    specs, operands, shapes, out_specs = [], [], [], []
    half = items[0][0].shape[0] // 2
    heads = items[0][0].shape[1]
    for kept, got, lowest in items:
        block = (1, 1) + kept.shape[2:]
        away = (lambda i, h: (2 * i + 1, h, 0, 0)) if lowest else (lambda i, h: (half + i, h, 0, 0))
        stay = (lambda i, h: (2 * i, h, 0, 0)) if lowest else (lambda i, h: (i, h, 0, 0))
        for index in (away, stay):
            specs += [pl.BlockSpec(block, index)] * 2
            operands += [kept, got]
            out_specs.append(pl.BlockSpec(block, lambda i, h: (i, h, 0, 0)))
            shapes.append(jax.ShapeDtypeStruct((half,) + kept.shape[1:], F32))

    def body(*refs):
        outs = refs[len(operands) :]
        for k, out in enumerate(outs):
            out[...] = refs[2 * k][...] + refs[2 * k + 1][...]

    res = pl.pallas_call(
        body,
        grid=(half, heads),
        in_specs=specs,
        out_specs=out_specs,
        out_shape=shapes,
        compiler_params=pltpu.CompilerParams(vmem_limit_bytes=24 * MIB),
        cost_estimate=cost(3, 12e6),
        name="split_add",
    )(*operands)
    return [(res[2 * k], res[2 * k + 1]) for k in range(len(items))]


class Reduction:
    def __init__(self, pairs, orders, size):
        self.size = size
        self.orders = [list(order) for order in orders]
        self.lowest = [order == sorted(order) for order in orders]
        self.kept = [keep for _, keep in pairs]
        self.got = [swap(send, "dp", size, 0) for send, _ in pairs]

    def split(self):
        items = list(zip(self.kept, self.got, self.lowest))
        pairs = split_add(items)
        self.kept = [keep for _, keep in pairs]
        self.got = [
            swap(send, "dp", self.size, order.pop(0))
            for (send, _), order in zip(pairs, self.orders)
        ]

    def rest(self):
        while self.orders[0]:
            self.split()
        return [keep[0] + got[0] for keep, got in zip(self.kept, self.got)]


def gather_pieces(piece, size, order):
    have = []
    now = piece
    for bit in order:
        at = len([b for b in have if b > bit])
        now = jnp.stack([now, swap(now, "dp", size, bit)], axis=at)
        have = sorted(have + [bit], reverse=True)
    now = now.reshape((size // 2,) + piece.shape)
    return now, swap(now, "dp", size, 0)


def sum_everywhere(value, sizes):
    for axis, size in sizes:
        for bit in range(size.bit_length() - 1):
            value = value + swap(value, axis, size, bit)
    return value


def split_low(table):
    high = lax.reduce_precision(table, 8, 7)
    return high.astype(BF), (table - high).astype(BF)


def spectral_tables(mode_index):
    heads = mode_index.shape[0]
    steps = jnp.arange(SEQ_LEN, dtype=jnp.int32)
    angles = (mode_index[:, :, None] * steps % SEQ_LEN).astype(F32) * (2.0 * math.pi / SEQ_LEN)
    ahead = jnp.concatenate([jnp.cos(angles), -jnp.sin(angles)], axis=1)
    if heads == 1:
        ahead = jnp.concatenate([ahead, jnp.zeros_like(ahead)], axis=0)
    ahead = ahead.reshape(2 * SEQ_LEN, SEQ_LEN)
    orders = jnp.arange(MODES, dtype=jnp.int32)
    angles = (steps[:, None] * orders % SEQ_LEN).astype(F32) * (2.0 * math.pi / SEQ_LEN)
    weights = jnp.where(orders == 0, 1.0, 2.0).astype(F32) / SEQ_LEN
    back = jnp.concatenate([jnp.cos(angles) * weights, -jnp.sin(angles) * weights], axis=1)
    tables = [jnp.concatenate(split_low(t), axis=1) for t in (ahead, back, back.T, ahead.T)]
    tables[1] = jnp.concatenate([tables[1], tables[1][:, :SEQ_LEN]], axis=1)
    return tables


def on_device(
    sizes,
    series,
    target,
    valid,
    window_id,
    mode_index,
    query_weight,
    query_first,
    query_second,
    out_weight,
    out_first,
    out_second,
    mode_weight,
    mode_first,
    mode_second,
    up_weight,
    up_first,
    up_second,
    down_weight,
    down_first,
    down_second,
    bias_pair,
    bias_first,
    bias_second,
    decomp_params,
    decomp_first,
    decomp_second,
):
    ndp, nhead = sizes
    bits = ndp.bit_length() - 1
    order_a = list(range(1, bits))
    order_b = order_a[::-1]
    dp = lax.axis_index("dp")
    head = lax.axis_index("head")
    me = dp.astype(jnp.int32).reshape(1)
    rows, d = series.shape
    own_heads = mode_index.shape[0]
    width = query_weight.shape[1]
    hidden = up_weight.shape[1]

    everyone = (("dp", ndp), ("head", nhead))
    place = jnp.concatenate([me, head.astype(jnp.int32).reshape(1)])

    def shift(v, r):
        return lax.ppermute(v, "head", [(i, (i + r) % nhead) for i in range(nhead)])

    def exchange(v):
        return lax.all_to_all(v, "head", 0, 0, tiled=True)

    def wide(v):
        pad = LANES - v.shape[-1]
        return jnp.pad(v, [(0, 0)] * (v.ndim - 1) + [(0, pad)]) if pad else v

    query_low = query_weight.astype(BF)
    query_parts = [query_low] + [shift(query_low, r) for r in range(1, nhead)]
    packed = jnp.concatenate(
        [w.astype(BF) for w in (up_weight.T, down_weight, out_weight)], axis=0
    )
    part = -(-packed.shape[0] // (16 * ndp)) * 16
    packed = jnp.pad(packed, ((0, part * ndp - packed.shape[0]), (0, 0)))
    packed = lax.dynamic_slice_in_dim(packed, dp * part, part, 0)
    packed = [packed] + [shift(packed, r) for r in range(1, nhead)]

    tf, ti, tit, tft = spectral_tables(mode_index)
    wt = mode_weight.reshape(2, own_heads * HEAD_DIM, HEAD_DIM * MODES).transpose(0, 2, 1)
    wt = wide(wt).reshape(2 * HEAD_DIM * MODES, LANES)

    def rows_of(v):
        return v[:, :, :width].reshape(-1, width)

    def contexts_of(v):
        return wide(v.reshape(-1, SEQ_LEN, width))

    def send(parts, way=1):
        return [parts[0]] + [shift(parts[r], way * r) for r in range(1, nhead)]

    query_parts = [query_parts[-r % nhead] for r in range(nhead)]
    queries = query_call(place[1:], series, bias_pair[0], query_parts)
    queries = send(queries)
    *packed, queries[0] = lax.optimization_barrier((*packed, queries[0]))
    packed = [jnp.stack(packed[: nhead // 2]), jnp.stack(packed[nhead // 2 :])]
    packed = gather_pieces(packed[0], ndp, order_a) + gather_pieces(packed[1], ndp, order_b)
    first, second, modes_in = spectrum_call([contexts_of(q) for q in queries], wt, tf, ti)
    first = send([rows_of(v) for v in first], -1)
    second = send([rows_of(v) for v in second], -1)

    starts = jnp.sum(window_id[:, None, :] < jnp.arange(5)[None, :, None], axis=2).astype(jnp.int32)
    valid_float = valid.astype(F32)
    half_call = partial(
        local_call,
        starts=starts,
        prm=decomp_params,
        me=me,
        x=series,
        target=target,
        valid=valid_float[:, None],
        bias=bias_pair[1:],
        packed=packed,
        hidden=hidden,
    )
    d_first, kept_first, sums_first = half_call(0, first, [])
    d_first = send(d_first)
    d_second, kept_second, sums = half_call(1, second, [])
    d_second = send(d_second)
    sums = jnp.sum(sums + sums_first, axis=1)

    hidden_part, out_part = hidden // ndp, width // ndp
    both_halves = list(zip(kept_first, kept_second))
    active, d_hidden, season, d_feed, spectrum, d_attention = both_halves
    layer = outer_call(
        me,
        [
            list(zip(season, d_hidden)),
            list(zip(active, d_feed)),
            list(zip(spectrum, d_attention)),
        ],
        [(d // ndp, hidden), (hidden_part + up8(out_part), d)],
        [(0, 0), (1, 0), (1, hidden_part)],
        ndp,
        "layer_grads",
        d_first[1:],
    )
    layer = Reduction([layer[:2], layer[2:]], [order_a, order_b], ndp)
    layer.split()

    d_queries, d_modes, bias_part = query_grad_call(
        [contexts_of(v) for v in d_first],
        [contexts_of(v) for v in d_second],
        wt,
        tit,
        tft,
        layer.kept,
    )
    d_queries = send([rows_of(v) for v in d_queries], -1)
    mode_parts = mode_grad_call(me, d_modes, modes_in, ndp)
    mode_parts = [m.reshape(ndp // 2, nhead, -1, LANES) for m in mode_parts]
    modes = Reduction([mode_parts[:2], mode_parts[2:]], [order_a, order_b], ndp)
    query = outer_call(
        me,
        [[(series, jnp.stack(d_queries))]],
        [(d // ndp, width)],
        [(0, 0)],
        ndp,
        "query_weight_grads",
    )
    query = Reduction([query], [order_a], ndp)

    def over_heads(v):
        return sum(send([v[r] for r in range(nhead)]))

    up_piece, down_piece = [over_heads(v) for v in layer.rest()]
    down_piece = down_piece[: hidden_part + out_part]
    (query_piece,) = [over_heads(v) for v in query.rest()]
    lanes = HEAD_DIM * MODES // ndp
    mode_pieces = [v.reshape(lanes, LANES).T[: own_heads * HEAD_DIM] for v in modes.rest()]

    bias_zero = lax.dynamic_update_slice_in_dim(
        jnp.zeros((d,), F32), jnp.sum(bias_part, axis=0)[:width], head * width, 0
    )
    squares = sum(jnp.sum(p * p) for p in (query_piece, *mode_pieces, up_piece, down_piece))
    small = jnp.concatenate(
        [
            bias_zero,
            sums[SUM_BIAS],
            jnp.sum(sums[:SUM_BIAS], axis=1),
            jnp.stack([jnp.sum(valid_float), squares]),
        ]
    )
    small = jnp.pad(small, (0, -small.shape[0] % LANES)).reshape(-1, LANES)
    small = sum_everywhere(small, everyone).reshape(-1)
    loss_sum = small[2 * d + SUM_LOSS]
    valid_count = small[2 * d + SUM_LOSS + 1]
    inverse = 1.0 / valid_count
    bias_grad = small[: 2 * d].reshape(2, d) * inverse
    decomp_grad = small[2 * d : 2 * d + 4 * KERNELS].reshape(2, 2, KERNELS) * inverse
    grad_norm = jnp.sqrt(
        small[2 * d + SUM_LOSS + 2] * inverse * inverse
        + jnp.sum(bias_grad * bias_grad)
        + jnp.sum(decomp_grad * decomp_grad)
    )
    factor = jnp.minimum(1.0, CLIP_NORM / (grad_norm + 1e-06))

    everything = slice(None)

    def band(start, stop):
        return (slice(start, stop), everything)

    both = (everything, everything)
    if lanes == d and hidden == d and out_part % 8 == 0:
        ways = d // width
        per = d // ndp // ways
        query_flat = query_piece.reshape(ways, per, width).transpose(1, 0, 2).reshape(per, d)
        two = jnp.concatenate([down_piece, query_flat], axis=0)
        grads = [
            gather_pieces(mode_pieces[0], ndp, order_b),
            gather_pieces(mode_pieces[1], ndp, order_a),
            gather_pieces(up_piece, ndp, order_b),
            gather_pieces(two, ndp, order_a),
        ]
        out_end = hidden_part + out_part
        views = [
            [
                (
                    3,
                    (slice(out_end, out_end + per), slice(n * width, (n + 1) * width)),
                    band(n * per, (n + 1) * per),
                )
                for n in range(ways)
            ],
            [(3, band(hidden_part, out_end), both)],
            [
                (c, band(h * HEAD_DIM, (h + 1) * HEAD_DIM), (c, h) + both)
                for c in range(2)
                for h in range(own_heads)
            ],
            [(2, both, both)],
            [(3, band(0, hidden_part), both)],
        ]
    else:
        pieces = (
            query_piece,
            down_piece[hidden_part:],
            up_piece,
            down_piece[:hidden_part],
            *mode_pieces,
        )
        grads = [gather_pieces(p, ndp, order_b) for p in pieces]
        views = [[(k, both, both)] for k in (0, 1, 4, 2, 3)]
        views[2] = [
            (4 + c, band(h * HEAD_DIM, (h + 1) * HEAD_DIM), (c, h) + both)
            for c in range(2)
            for h in range(own_heads)
        ]

    states = (
        (query_weight, query_first, query_second),
        (out_weight, out_first, out_second),
        (mode_weight, mode_first, mode_second),
        (up_weight, up_first, up_second),
        (down_weight, down_first, down_second),
    )
    news = adam_call(me, (factor * inverse).reshape(1), grads, views, states, (0, 0, 3, 0, 0))
    news += adam_values(bias_pair, bias_grad * factor, bias_first, bias_second)
    news += adam_values(decomp_params, decomp_grad * factor, decomp_first, decomp_second)
    return (loss_sum, valid_count, grad_norm, *news)


def solution(mesh):
    rows = P(("dp", "head"), None)
    down = P("head", None)
    across = P(None, "head")
    modes = P(None, "head", None, None)
    weights = (across,) * 3 + (down,) * 3 + (modes,) * 3 + (across,) * 3 + (down,) * 3 + (P(),) * 6
    sizes = (mesh.shape["dp"], mesh.shape["head"])
    return jax.shard_map(
        partial(on_device, sizes),
        mesh=mesh,
        in_specs=(rows, rows, P(("dp", "head")), rows, down) + weights,
        out_specs=(P(), P(), P()) + weights,
        check_vma=False,
    )
```

```python
from functools import partial
import math

import jax
import jax.numpy as jnp
from jax import lax
from jax.experimental import pallas as pl
from jax.experimental.pallas import tpu as pltpu
from jax.sharding import PartitionSpec as P

MODES = 64
SEQ_LEN = 128
HEAD_DIM = 64
STEP = 10
KERNEL_WIDTHS = (7, 12, 14, 24, 48)
KERNELS = len(KERNEL_WIDTHS)
BETA_ONE = 0.9
BETA_TWO = 0.999
LEARN_RATE = 0.05
EPSILON = 1e-08
DECAY = 0.01
CLIP_NORM = 0.02
LOG2E = math.log2(math.e)
LANES = 128
BF = jnp.bfloat16
F32 = jnp.float32
MIB = 1 << 20

ERF_P = 0.3275911
ERF_A = (0.254829592, -0.284496736, 1.421413741, -1.453152027, 1.061405429)


def dot(a, b, ca=1, cb=0):
    return lax.dot_general(a, b, (((ca,), (cb,)), ((), ())), preferred_element_type=F32)


def cost(microseconds, moved):
    return pl.CostEstimate(
        flops=int(microseconds * 1.1e9), bytes_accessed=int(moved), transcendentals=0
    )


def query_kernel(head_ref, x_ref, b_ref, *refs):
    heads = len(refs) // 2
    x = x_ref[...]
    for r in range(heads):
        bias = b_ref[lax.rem(head_ref[0] + r, heads)]
        refs[heads + r][...] = (dot(x, refs[r][...]) + bias).astype(BF)


def query_call(head, x, bias_row, weights):
    rows, d = x.shape
    heads = len(weights)
    width = weights[0].shape[1]
    step = min(256, rows)
    return pl.pallas_call(
        query_kernel,
        grid=(rows // step,),
        in_specs=[
            pl.BlockSpec(memory_space=pltpu.SMEM),
            pl.BlockSpec((step, d), lambda i: (i, 0)),
            pl.BlockSpec((heads, 1, width), lambda i: (0, 0, 0)),
        ]
        + [pl.BlockSpec((d, width), lambda i: (0, 0)) for _ in weights],
        out_specs=[pl.BlockSpec((step, width), lambda i: (i, 0)) for _ in weights],
        out_shape=[jax.ShapeDtypeStruct((rows, width), BF) for _ in weights],
        compiler_params=pltpu.CompilerParams(vmem_limit_bytes=24 * MIB),
        cost_estimate=cost(2.5, 3e6),
        name="queries",
    )(head, x, bias_row.reshape(heads, 1, width), *weights)


def lane_low(rows):
    return lax.broadcasted_iota(jnp.int32, (rows, LANES), 1) < HEAD_DIM


def mix_blocks(wt_ref, m, count):
    low = lane_low(HEAD_DIM)
    zero = jnp.zeros((HEAD_DIM, LANES), F32)
    left = [
        wt_ref[pl.ds(c * HEAD_DIM * MODES + m, HEAD_DIM, stride=MODES), :] for c in range(2)
    ]
    blocks = []
    for _ in range(count):
        terms = [v.astype(BF).astype(F32) for v in left]
        left = [v - t for v, t in zip(left, terms)]
        real, imag = (
            jnp.concatenate([jnp.where(low, t, zero), jnp.where(low, zero, t)], axis=0)
            for t in terms
        )
        top = jnp.concatenate([real, -imag], axis=1)
        bottom = jnp.concatenate([imag, real], axis=1)
        blocks.append(jnp.concatenate([top, bottom], axis=0).astype(BF))
    return blocks


def pair_width(contexts):
    return 2 if contexts % 2 == 0 else 1


def spectrum_kernel(wt_ref, tf_ref, ti_ref, *refs):
    owners = (len(refs) - 3) // 3
    q_refs, spec_refs = refs[:owners], refs[owners : 3 * owners]
    xs_ref, x_scr, y_scr = refs[3 * owners :]
    run, width = q_refs[0].shape[0], q_refs[0].shape[2]
    half = run // 2
    contexts = owners * run
    pair = pair_width(half)
    low = lane_low(SEQ_LEN)

    for r in range(owners):

        def forward(p, _, r=r):
            cols = jnp.concatenate([q_refs[r][p * pair + k] for k in range(pair)], axis=1)
            res = dot(tf_ref[...], jnp.concatenate([cols, cols], axis=0))
            for k in range(pair):
                part = res[:, k * LANES : (k + 1) * LANES]
                row = (r * run + p * pair + k) * SEQ_LEN
                x_scr[pl.ds(pl.multiple_of(row, SEQ_LEN), SEQ_LEN), :] = jnp.where(
                    low, part[:SEQ_LEN], part[SEQ_LEN:]
                )
            return 0

        lax.fori_loop(0, run // pair, forward, 0)

    def mix(m, _):
        xr = x_scr[pl.ds(m, contexts, stride=SEQ_LEN), :].astype(BF)
        xi = x_scr[pl.ds(MODES + m, contexts, stride=SEQ_LEN), :].astype(BF)
        xs_ref[m] = jnp.concatenate([xr, xi], axis=0)
        x = jnp.concatenate([xr, xi], axis=1)
        main, rest = mix_blocks(wt_ref, m, 2)
        y = dot(x, main, 1, 1) + dot(x, rest, 1, 1)
        y_scr[pl.ds(m, contexts, stride=SEQ_LEN), :] = y[:, :LANES]
        y_scr[pl.ds(MODES + m, contexts, stride=SEQ_LEN), :] = y[:, LANES:]
        return 0

    lax.fori_loop(0, MODES, mix, 0, unroll=4)

    for r in range(owners):
        for number in range(2):
            target = spec_refs[number * owners + r]

            def inverse(p, _, r=r, number=number, target=target):
                parts = []
                for k in range(pair):
                    row = (r * run + number * half + p * pair + k) * SEQ_LEN
                    parts.append(y_scr[pl.ds(pl.multiple_of(row, SEQ_LEN), SEQ_LEN), :])
                cols = jnp.concatenate(parts, axis=1)
                main = cols.astype(BF)
                rest = (cols - main.astype(F32)).astype(BF)
                res = dot(ti_ref[...], jnp.concatenate([main, main, rest], axis=0)).astype(BF)
                for k in range(pair):
                    target[p * pair + k] = res[:, k * LANES : (k + 1) * LANES]
                return 0

            lax.fori_loop(0, half // pair, inverse, 0)


def spectrum_call(queries, wt, tf, ti):
    owners = len(queries)
    run = queries[0].shape[0]
    contexts = owners * run
    out = jax.ShapeDtypeStruct((run // 2, SEQ_LEN, LANES), BF)
    res = pl.pallas_call(
        spectrum_kernel,
        out_shape=[out] * (2 * owners)
        + [jax.ShapeDtypeStruct((MODES, 2 * contexts, LANES), BF)],
        scratch_shapes=[
            pltpu.VMEM((contexts * SEQ_LEN, LANES), F32),
            pltpu.VMEM((contexts * SEQ_LEN, LANES), F32),
        ],
        compiler_params=pltpu.CompilerParams(vmem_limit_bytes=32 * MIB),
        cost_estimate=cost(15, 7e6),
        name="spectrum",
    )(wt, tf, ti, *queries)
    return res[:owners], res[owners : 2 * owners], res[2 * owners]


def query_grad_kernel(wt_ref, tit_ref, tft_ref, *refs):
    owners = (len(refs) - 4) // 3
    d_refs, dq_refs = refs[: 2 * owners], refs[2 * owners : 3 * owners]
    dy_ref, bias_ref, y_scr, x_scr = refs[3 * owners :]
    half = d_refs[0].shape[0]
    run = 2 * half
    contexts = owners * run
    pair = pair_width(half)
    low = lane_low(SEQ_LEN)
    zero = jnp.zeros((SEQ_LEN, LANES), F32)

    for number in range(2):
        for r in range(owners):
            source = d_refs[number * owners + r]

            def forward(p, _, number=number, r=r, source=source):
                cols = jnp.concatenate([source[p * pair + k] for k in range(pair)], axis=1)
                res = dot(tit_ref[...], jnp.concatenate([cols, cols], axis=0))
                for k in range(pair):
                    row = (r * run + number * half + p * pair + k) * SEQ_LEN
                    y_scr[pl.ds(pl.multiple_of(row, SEQ_LEN), SEQ_LEN), :] = res[
                        :, k * LANES : (k + 1) * LANES
                    ]
                return 0

            lax.fori_loop(0, half // pair, forward, 0)

    def mix(m, _):
        yr = y_scr[pl.ds(m, contexts, stride=SEQ_LEN), :].astype(BF)
        yi = y_scr[pl.ds(MODES + m, contexts, stride=SEQ_LEN), :].astype(BF)
        dy = jnp.concatenate([yr, yi], axis=1)
        dy_ref[m] = dy
        dx = dot(dy, mix_blocks(wt_ref, m, 1)[0])
        x_scr[pl.ds(m, contexts, stride=SEQ_LEN), :] = dx[:, :LANES]
        x_scr[pl.ds(MODES + m, contexts, stride=SEQ_LEN), :] = dx[:, LANES:]
        return 0

    lax.fori_loop(0, MODES, mix, 0, unroll=4)
    bias_ref[...] = jnp.zeros_like(bias_ref)

    for r in range(owners):

        def inverse(p, _, r=r):
            parts = []
            for k in range(pair):
                row = (r * run + p * pair + k) * SEQ_LEN
                one = x_scr[pl.ds(pl.multiple_of(row, SEQ_LEN), SEQ_LEN), :]
                parts.append(
                    jnp.concatenate([jnp.where(low, one, zero), jnp.where(low, zero, one)], axis=0)
                )
            cols = jnp.concatenate(parts, axis=1).astype(BF)
            res = dot(tft_ref[...], jnp.concatenate([cols, cols], axis=0)).astype(BF)
            total = jnp.zeros((8, LANES), F32)
            for k in range(pair):
                one = res[:, k * LANES : (k + 1) * LANES]
                dq_refs[r][p * pair + k] = one
                total = total + jnp.sum(one.astype(F32).reshape(SEQ_LEN // 8, 8, LANES), axis=0)
            bias_ref[...] += total
            return 0

        lax.fori_loop(0, run // pair, inverse, 0)


def query_grad_call(first, second, wt, tit, tft, waits):
    owners = len(first)
    run = 2 * first[0].shape[0]
    contexts = owners * run
    whole = pl.BlockSpec(memory_space=pltpu.VMEM)

    def body(*refs):
        at = 3 + 2 * owners
        query_grad_kernel(*refs[:at], *refs[at + len(waits) :])

    res = pl.pallas_call(
        body,
        in_specs=[whole] * (3 + 2 * owners) + [pl.BlockSpec(memory_space=pl.ANY)] * len(waits),
        out_shape=[jax.ShapeDtypeStruct((run, SEQ_LEN, LANES), BF)] * owners
        + [
            jax.ShapeDtypeStruct((MODES, contexts, 2 * LANES), BF),
            jax.ShapeDtypeStruct((8, LANES), F32),
        ],
        scratch_shapes=[
            pltpu.VMEM((contexts * SEQ_LEN, LANES), F32),
            pltpu.VMEM((contexts * SEQ_LEN, LANES), F32),
        ],
        compiler_params=pltpu.CompilerParams(vmem_limit_bytes=32 * MIB),
        cost_estimate=cost(11, 7e6),
        name="query_grads",
    )(wt, tit, tft, *first, *second, *waits)
    return res[:owners], res[owners], res[owners + 1]


def mode_grad_kernel(me_ref, dy_ref, xs_ref, *refs):
    outs = refs[-7:-3]
    dw_scr, low_scr, sems = refs[-3:]
    pieces, depth = 2 * outs[0].shape[0], outs[0].shape[1]
    total = HEAD_DIM * MODES
    low = lane_low(HEAD_DIM)
    me = me_ref[0]

    def mix(m, _):
        dy = dy_ref[m]
        yr, yi = dy[:, :LANES], dy[:, LANES:]
        right = jnp.concatenate(
            [jnp.concatenate([yr, yi], axis=0), jnp.concatenate([yi, -yr], axis=0)], axis=1
        )
        dw = dot(right, xs_ref[m], 0, 0)
        for c in range(2):
            first = 2 * c * HEAD_DIM
            part = jnp.where(
                low, dw[first : first + HEAD_DIM], dw[first + HEAD_DIM : first + 2 * HEAD_DIM]
            )
            dw_scr[pl.ds(c * total + m, HEAD_DIM, stride=MODES), :] = part
        return 0

    lax.fori_loop(0, MODES, mix, 0, unroll=4)
    for j in range(1, pieces, 2):
        for c in range(2):
            start = pl.multiple_of(c * total + (me ^ j) * depth, depth)
            low_scr[c, j // 2] = dw_scr[pl.ds(start, depth), :].astype(BF)
    copies = []
    for j in range(pieces):
        for c in range(2):
            start = pl.multiple_of(c * total + (me ^ j) * depth, depth)
            copies.append(
                pltpu.make_async_copy(
                    low_scr.at[c, j // 2] if j % 2 else dw_scr.at[pl.ds(start, depth), :],
                    outs[2 * c + (j + 1) % 2].at[j // 2],
                    sems.at[c, j],
                )
            )
    for copy in copies:
        copy.start()
    for copy in copies:
        copy.wait()


def mode_grad_call(me, dy, xs, pieces, waits):
    part = jax.ShapeDtypeStruct((pieces // 2, HEAD_DIM * MODES // pieces, LANES), F32)
    whole = pl.BlockSpec(memory_space=pltpu.VMEM)
    return pl.pallas_call(
        mode_grad_kernel,
        in_specs=[pl.BlockSpec(memory_space=pltpu.SMEM)]
        + [whole] * 2
        + [pl.BlockSpec(memory_space=pl.ANY)] * len(waits),
        out_specs=[pl.BlockSpec(memory_space=pl.ANY)] * 4,
        out_shape=[jax.ShapeDtypeStruct(part.shape, BF), part] * 2,
        scratch_shapes=[
            pltpu.VMEM((2 * HEAD_DIM * MODES, LANES), F32),
            pltpu.VMEM((2,) + part.shape, BF),
            pltpu.SemaphoreType.DMA((2, pieces)),
        ],
        compiler_params=pltpu.CompilerParams(vmem_limit_bytes=40 * MIB),
        cost_estimate=cost(9, 8e6),
        name="mode_grads",
    )(me, dy, xs, *waits)


SUM_SLOPE = (0, 10)
SUM_OFFSET = (5, 15)
SUM_LOSS = 20
SUM_BIAS = 21
SUM_ROWS = 24


def window_counts(first, last, rows, cols, width):
    lead = width - 1 - (width - 1) // 2
    reach = cols - rows + (lead + 1)
    here = jnp.where(cols < first, 0, jnp.where(cols >= last, width, jnp.clip(reach, 0, width)))
    before = jnp.where(
        cols <= first, 0, jnp.where(cols > last, width, jnp.clip(reach - 1, 0, width))
    )
    return (here - before).astype(F32)


def window_edges(starts, rows):
    s1, s2, s3 = starts
    first = jnp.where(rows >= s3, s3, jnp.where(rows >= s2, s2, jnp.where(rows >= s1, s1, 0)))
    last = jnp.where(
        rows < s1, s1 - 1, jnp.where(rows < s2, s2 - 1, jnp.where(rows < s3, s3 - 1, SEQ_LEN - 1))
    )
    return first, last


def fold(v):
    return jnp.sum(v.reshape(v.shape[0] // 8, 8, v.shape[1]), axis=0)


def local_kernel(*refs, chunk, hidden_width, heads, waits):
    refs = list(refs)

    def take(n):
        taken = refs[:n]
        del refs[:n]
        return taken

    starts_ref, prm_ref, me_ref, x_ref, tgt_ref, val_ref, bias_ref = take(7)
    spec_refs = take(heads)
    packed_refs = take(4)
    take(waits)
    dspec_refs = take(heads)
    act_ref, dhid_ref, low_ref, dfeed_ref, spec_out, dattn_ref, sums_ref = take(7)
    (
        u_scr,
        trend_scr,
        season_scr,
        av1_scr,
        share_scr,
        av2_scr,
        da_scr,
        part_scr,
        g_scr,
        slope_scr,
        a_scr,
        at_scr,
        weights,
        weight_sems,
    ) = refs
    step = pl.program_id(0)
    rows, d = x_ref.shape
    nctx = rows // SEQ_LEN
    out_width = dspec_refs[0].shape[1]
    up_rows = slice(0, hidden_width)
    down_rows = slice(hidden_width, 2 * hidden_width)
    out_rows = slice(2 * hidden_width, 2 * hidden_width + out_width)
    groups = d // LANES
    loops = SEQ_LEN // chunk

    @pl.when(step == 0)
    def _():
        count, shared, part, _ = packed_refs[0].shape
        copies = []
        for number, ref in enumerate(packed_refs):
            group, bit = number // 2, number % 2
            for k in range(count):
                for r in range(shared):
                    row = pl.multiple_of((me_ref[0] ^ (2 * k + bit)) * part, part)
                    copies.append(
                        pltpu.make_async_copy(
                            ref.at[k, r],
                            weights.at[(heads - group * shared - r) % heads, pl.ds(row, part), :],
                            weight_sems.at[number, k * shared + r],
                        )
                    )
        for copy in copies:
            copy.start()
        sums_ref[...] = jnp.zeros_like(sums_ref)
        for copy in copies:
            copy.wait()

    row_ids = lax.broadcasted_iota(jnp.int32, (SEQ_LEN, SEQ_LEN), 0)
    col_ids = lax.broadcasted_iota(jnp.int32, (SEQ_LEN, SEQ_LEN), 1)
    for c in range(nctx):
        starts = [starts_ref[step * nctx + c, k] for k in range(1, 4)]
        first, last = window_edges(starts, row_ids)
        first_t, last_t = window_edges(starts, col_ids)
        for w, width in enumerate(KERNEL_WIDTHS):
            counts = window_counts(first, last, row_ids, col_ids, width).astype(BF)
            a_scr[c, w * SEQ_LEN : (w + 1) * SEQ_LEN, :SEQ_LEN] = counts
            a_scr[c, w * SEQ_LEN : (w + 1) * SEQ_LEN, SEQ_LEN:] = counts
            at_scr[c, :, w * SEQ_LEN : (w + 1) * SEQ_LEN] = window_counts(
                first_t, last_t, col_ids, row_ids, width
            ).astype(BF)

    def averages(c, u, av):
        high = u.astype(BF)
        rest = (u - high.astype(F32)).astype(BF)
        av[c] = dot(a_scr[c], jnp.concatenate([high, rest], axis=0))

    spec = jnp.concatenate([ref[...] for ref in spec_refs], axis=1)
    for h in range(heads):
        spec_out[h] = spec_refs[h][...]
    out_all = jnp.concatenate([weights[h, out_rows] for h in range(heads)], axis=0)
    pre = x_ref[...].astype(F32) + (dot(spec, out_all) + bias_ref[...])
    u_scr[...] = pre
    for c in range(nctx):
        averages(c, pre[c * SEQ_LEN : (c + 1) * SEQ_LEN], av1_scr)

    def shares_of(u, avs, layer):
        logits = [
            u * (prm_ref[layer, 0, w] * LOG2E) + prm_ref[layer, 1, w] * LOG2E
            for w in range(KERNELS)
        ]
        top = logits[0]
        for v in logits[1:]:
            top = jnp.maximum(top, v)
        powers = [jnp.exp2(v - top) for v in logits]
        total = powers[0]
        for v in powers[1:]:
            total = total + v
        scale = 1.0 / total
        shares = [v * scale for v in powers]
        trend = shares[0] * avs[0]
        for s, a in zip(shares[1:], avs[1:]):
            trend = trend + s * a
        return shares, trend

    def read_averages(av, c, row, lanes):
        return [
            av[c, pl.ds(w * SEQ_LEN + row, chunk), lanes] * (1.0 / width)
            for w, width in enumerate(KERNEL_WIDTHS)
        ]

    def pull(shares, avs, trend, grad, u, layer, base, c, row, lanes, sums):
        rest = base
        slopes, offsets = [], []
        for w, width in enumerate(KERNEL_WIDTHS):
            d_avg = shares[w] * grad
            da_scr[c, pl.ds(w * SEQ_LEN + row, chunk), lanes] = (d_avg * (1.0 / width)).astype(BF)
            d_logit = d_avg * (avs[w] - trend)
            rest = rest + d_logit * prm_ref[layer, 0, w]
            slopes.append(sums[w] + fold(d_logit * u))
            offsets.append(sums[KERNELS + w] + fold(d_logit))
        return rest, slopes + offsets

    for c in range(nctx):
        for g in range(groups):
            lanes = slice(g * LANES, (g + 1) * LANES)

            def first_pass(r, _, c=c, lanes=lanes):
                row = pl.multiple_of(r * chunk, chunk)
                at = pl.ds(c * SEQ_LEN + row, chunk)
                u = u_scr[at, lanes]
                avs = read_averages(av1_scr, c, row, lanes)
                shares, trend = shares_of(u, avs, 0)
                for w in range(KERNELS):
                    share_scr[c, pl.ds(w * SEQ_LEN + row, chunk), lanes] = shares[w]
                season = u - trend
                trend_scr[at, lanes] = trend
                season_scr[at, lanes] = season
                low_ref[at, lanes] = season.astype(BF)
                return 0

            lax.fori_loop(0, loops, first_pass, 0)

    season_low = low_ref[...]
    feed = jnp.zeros((rows, d), F32)
    for h in range(heads):
        hid = dot(season_low, weights[h, up_rows], 1, 1)
        z = jnp.abs(hid) * (2.0**-0.5)
        t = 1.0 / (1.0 + ERF_P * z)
        e = jnp.exp2(hid * hid * (-0.5 * LOG2E))
        poly = ERF_A[4]
        for coef in ERF_A[3::-1]:
            poly = poly * t + coef
        tail = (0.5 * t) * poly * e
        phi = jnp.where(hid < 0, tail, 1.0 - tail)
        active = (hid * phi).astype(BF)
        slope_scr[h] = phi + hid * e * ((2.0 * math.pi) ** -0.5)
        act_ref[h] = active
        feed = feed + dot(active, weights[h, down_rows])

    pre = season_scr[...] + feed
    g_scr[...] = pre
    for c in range(nctx):
        averages(c, pre[c * SEQ_LEN : (c + 1) * SEQ_LEN], av2_scr)

    for c in range(nctx):
        for g in range(groups):
            lanes = slice(g * LANES, (g + 1) * LANES)

            def second_pass(r, sums, c=c, lanes=lanes):
                row = pl.multiple_of(r * chunk, chunk)
                at = pl.ds(c * SEQ_LEN + row, chunk)
                u = g_scr[at, lanes]
                avs = read_averages(av2_scr, c, row, lanes)
                shares, trend = shares_of(u, avs, 1)
                misfit = trend_scr[at, lanes] + trend - tgt_ref[at, lanes]
                weighted = val_ref[at, :] * misfit
                grad = 2.0 * weighted
                rest, new = pull(
                    shares, avs, trend, grad, u, 1, jnp.zeros_like(u), c, row, lanes, sums
                )
                part_scr[at, lanes] = rest
                g_scr[at, lanes] = grad
                return tuple(new) + (sums[2 * KERNELS] + fold(weighted * misfit),)

            zeros = tuple(jnp.zeros((8, LANES), F32) for _ in range(2 * KERNELS + 1))
            sums = lax.fori_loop(0, loops, second_pass, zeros)
            for k in range(KERNELS):
                sums_ref[SUM_SLOPE[1] + k, :, lanes] += sums[k]
                sums_ref[SUM_OFFSET[1] + k, :, lanes] += sums[KERNELS + k]
            sums_ref[SUM_LOSS, :, lanes] += sums[2 * KERNELS]

    for c in range(nctx):
        at = slice(c * SEQ_LEN, (c + 1) * SEQ_LEN)
        part_scr[at, :] += dot(at_scr[c], da_scr[c])

    d_pre = part_scr[...]
    d_feed = d_pre.astype(BF)
    dfeed_ref[...] = d_feed
    back = d_pre
    for h in range(heads):
        d_hid = (dot(d_feed, weights[h, down_rows], 1, 1) * slope_scr[h]).astype(BF)
        back = back + dot(d_hid, weights[h, up_rows])
        dhid_ref[h] = d_hid
    season_scr[...] = back

    for c in range(nctx):
        for g in range(groups):
            lanes = slice(g * LANES, (g + 1) * LANES)

            def third_pass(r, sums, c=c, lanes=lanes):
                row = pl.multiple_of(r * chunk, chunk)
                at = pl.ds(c * SEQ_LEN + row, chunk)
                u = u_scr[at, lanes]
                avs = read_averages(av1_scr, c, row, lanes)
                shares = [
                    share_scr[c, pl.ds(w * SEQ_LEN + row, chunk), lanes] for w in range(KERNELS)
                ]
                d_season = season_scr[at, lanes]
                rest, new = pull(
                    shares,
                    avs,
                    trend_scr[at, lanes],
                    g_scr[at, lanes] - d_season,
                    u,
                    0,
                    d_season,
                    c,
                    row,
                    lanes,
                    sums,
                )
                part_scr[at, lanes] = rest
                return tuple(new)

            zeros = tuple(jnp.zeros((8, LANES), F32) for _ in range(2 * KERNELS))
            sums = lax.fori_loop(0, loops, third_pass, zeros)
            for k in range(KERNELS):
                sums_ref[SUM_SLOPE[0] + k, :, lanes] += sums[k]
                sums_ref[SUM_OFFSET[0] + k, :, lanes] += sums[KERNELS + k]

    for c in range(nctx):
        at = slice(c * SEQ_LEN, (c + 1) * SEQ_LEN)
        part_scr[at, :] += dot(at_scr[c], da_scr[c])

    d_pre = part_scr[...]
    sums_ref[SUM_BIAS] += fold(d_pre)
    d_attn = d_pre.astype(BF)
    dattn_ref[...] = d_attn
    d_spec = dot(d_attn, out_all, 1, 1).astype(BF)
    for h in range(heads):
        dspec_refs[h][...] = d_spec[:, h * out_width : (h + 1) * out_width]


def up8(n):
    return -(-n // 8) * 8


def local_call(number, spec, waits, starts, prm, me, x, target, valid, bias, packed, hidden):
    rows_half = x.shape[0] // 2
    d = x.shape[1]
    heads = len(spec)
    width = spec[0].shape[1]
    nctx = 2 if rows_half % (2 * SEQ_LEN) == 0 else 1
    rows = nctx * SEQ_LEN
    steps = rows_half // rows
    smem = pl.BlockSpec(memory_space=pltpu.SMEM)
    whole = pl.BlockSpec(memory_space=pltpu.VMEM)
    anywhere = pl.BlockSpec(memory_space=pl.ANY)
    averages = (nctx, KERNELS * SEQ_LEN, d)
    count, shared, part, _ = packed[0].shape

    def row_block(columns, half=0):
        return pl.BlockSpec((rows, columns), lambda i: (half * steps + i, 0))

    def head_block(columns):
        return pl.BlockSpec((heads, rows, columns), lambda i: (0, i, 0))

    ctx_half = starts.shape[0] // 2
    res = pl.pallas_call(
        partial(local_kernel, chunk=16, hidden_width=hidden, heads=heads, waits=len(waits)),
        grid=(steps,),
        in_specs=[smem] * 3
        + [row_block(d, number), row_block(d, number), row_block(1, number), whole]
        + [row_block(width)] * heads
        + [anywhere] * (len(packed) + len(waits)),
        out_specs=[row_block(width)] * heads
        + [head_block(hidden), head_block(hidden), row_block(d), row_block(d)]
        + [head_block(width), row_block(d)]
        + [pl.BlockSpec((SUM_ROWS, 8, d), lambda i: (0, 0, 0))],
        out_shape=[jax.ShapeDtypeStruct((rows_half, width), BF)] * heads
        + [jax.ShapeDtypeStruct((heads, rows_half, hidden), BF)] * 2
        + [jax.ShapeDtypeStruct((rows_half, d), BF)] * 2
        + [
            jax.ShapeDtypeStruct((heads, rows_half, width), BF),
            jax.ShapeDtypeStruct((rows_half, d), BF),
            jax.ShapeDtypeStruct((SUM_ROWS, 8, d), F32),
        ],
        scratch_shapes=[
            pltpu.VMEM((rows, d), F32),
            pltpu.VMEM((rows, d), F32),
            pltpu.VMEM((rows, d), F32),
            pltpu.VMEM(averages, F32),
            pltpu.VMEM(averages, F32),
            pltpu.VMEM(averages, F32),
            pltpu.VMEM(averages, BF),
            pltpu.VMEM((rows, d), F32),
            pltpu.VMEM((rows, d), F32),
            pltpu.VMEM((heads, rows, hidden), F32),
            pltpu.VMEM((nctx, KERNELS * SEQ_LEN, 2 * SEQ_LEN), BF),
            pltpu.VMEM((nctx, SEQ_LEN, KERNELS * SEQ_LEN), BF),
            pltpu.VMEM((heads, len(packed) * count // 2 * part, d), BF),
            pltpu.SemaphoreType.DMA((len(packed), count * shared)),
        ],
        compiler_params=pltpu.CompilerParams(vmem_limit_bytes=56 * MIB),
        cost_estimate=cost(38, 24e6),
        name="local_layer",
    )(
        starts[number * ctx_half : (number + 1) * ctx_half],
        prm,
        me,
        x,
        target,
        valid,
        bias,
        *spec,
        *packed,
        *waits,
    )
    return res[:heads], res[heads:-1], res[-1]


def outer_kernel(me_ref, *refs, halves, outs, waits):
    scratch = refs[-1]
    ins = list(refs[: 2 * sum(halves)])
    targets = list(refs[2 * sum(halves) + waits : -1])
    for count, cuts in zip(halves, outs):
        total = None
        for _ in range(count):
            left, right = (r[0] if len(r.shape) == 3 else r[...] for r in ins[:2])
            del ins[:2]
            term = dot(left, right, 0, 0)
            total = term if total is None else total + term
        rows, columns = total.shape
        lanes = slice(0, columns)
        scratch[:rows, lanes] = total
        offset = 0
        for cut in cuts:
            send, keep = targets[:2]
            del targets[:2]
            pieces = 2 * send.shape[0]
            size = rows // pieces
            for j in range(pieces):
                target = send if j % 2 else keep
                start = (me_ref[0] ^ j) * size + offset
                if cut % 8 == 0:
                    part = scratch[pl.ds(pl.multiple_of(start, 8), cut), lanes]
                    target[j // 2, 0] = part.astype(target.dtype)
                else:
                    row = lax.broadcasted_iota(jnp.int32, (target.shape[2], 1), 0)
                    part = jnp.zeros((target.shape[2], columns), F32)
                    for i in range(cut):
                        part = jnp.where(row == i, scratch[pl.ds(start + i, 1), lanes], part)
                    target[j // 2, 0] = part.astype(target.dtype)
            offset += cut


def outer_call(me, products, outs, pieces, name, waits=()):
    heads = next(a.shape[0] for p in products for pair in p for a in pair if a.ndim == 3)
    operands = [a for p in products for pair in p for a in pair]

    def spec(a):
        if a.ndim == 3:
            return pl.BlockSpec((1,) + a.shape[1:], lambda h: (h, 0, 0))
        return pl.BlockSpec(a.shape, lambda h: (0, 0))

    shapes = []
    for p, cuts in zip(products, outs):
        for cut, kind in cuts:
            tail = (cut if cut % 8 == 0 else 16, p[0][1].shape[-1])
            shapes += [
                jax.ShapeDtypeStruct((pieces // 2, heads) + tail, t) for t in (kind, F32)
            ]
    rows = max(pair[0].shape[-1] for p in products for pair in p)
    columns = max(pair[1].shape[-1] for p in products for pair in p)
    res = pl.pallas_call(
        partial(
            outer_kernel,
            halves=[len(p) for p in products],
            outs=[[cut for cut, _ in cuts] for cuts in outs],
            waits=len(waits),
        ),
        grid=(heads,),
        in_specs=[pl.BlockSpec(memory_space=pltpu.SMEM)]
        + [spec(a) for a in operands]
        + [pl.BlockSpec(memory_space=pl.ANY)] * len(waits),
        out_specs=[
            pl.BlockSpec((s.shape[0], 1) + s.shape[2:], lambda h: (0, h, 0, 0)) for s in shapes
        ],
        out_shape=shapes,
        scratch_shapes=[pltpu.VMEM((rows, columns), F32)],
        compiler_params=pltpu.CompilerParams(vmem_limit_bytes=60 * MIB),
        cost_estimate=cost(8, 20e6),
        name=name,
    )(me, *operands, *waits)
    return [(res[2 * k], res[2 * k + 1]) for k in range(len(res) // 2)]


def adam_values(weight, gradient, first, second):
    m = BETA_ONE * first + (1.0 - BETA_ONE) * gradient
    v = BETA_TWO * second + (1.0 - BETA_TWO) * gradient * gradient
    first_hat = m * (1.0 / (1.0 - BETA_ONE**STEP))
    second_hat = v * (1.0 / (1.0 - BETA_TWO**STEP))
    return (
        weight - LEARN_RATE * (first_hat / (jnp.sqrt(second_hat) + EPSILON) + DECAY * weight),
        m,
        v,
    )


def adam_kernel(me_ref, scale_ref, *refs, views, leads, grads):
    scale = scale_ref[0]
    count = len(views)
    pairs = refs[: 2 * grads]
    states = refs[2 * grads : 2 * grads + 3 * count]
    outs = refs[2 * grads + 3 * count : 2 * grads + 6 * count]
    chosen = refs[2 * grads + 6 * count :]
    other = (pl.program_id(0) ^ me_ref[0]) & 1

    @pl.when(other == 0)
    def _():
        for k in range(grads):
            chosen[k][...] = pairs[2 * k][0]

    @pl.when(other == 1)
    def _():
        for k in range(grads):
            chosen[k][...] = pairs[2 * k + 1][0]

    for k, parts in enumerate(views):
        lead = leads[k]
        for which, source, place in parts:
            ins = [r.at[lead][place] for r in states[3 * k : 3 * k + 3]]
            g = chosen[which][source] * scale
            new = adam_values(ins[0], g, ins[1], ins[2])
            for r, value in zip(outs[3 * k : 3 * k + 3], new):
                r.at[lead][place] = value


def adam_call(me, scale, grads, views, states, axes):
    pieces = 2 * grads[0][0].shape[0]
    specs, out_specs, operands, shapes, leads = [], [], [], [], []
    for pair in grads:
        zeros = (0,) * (pair[0].ndim - 1)
        for grad in pair:
            specs.append(
                pl.BlockSpec(
                    (1,) + grad.shape[1:],
                    lambda i, me_ref, z=zeros: (lax.div(i ^ me_ref[0], 2),) + z,
                )
            )
            operands.append(grad)
    for group, axis in zip(states, axes):
        shape = group[0].shape
        size = shape[axis] // pieces
        direct = size % (LANES if axis == len(shape) - 1 else 8) == 0
        if not direct:
            shape = shape[:axis] + (pieces, size) + shape[axis + 1 :]
        block = shape[:axis] + (size if direct else 1,) + shape[axis + 1 :]
        leads.append((slice(None),) * axis + ((slice(None),) if direct else (0,)))
        for state in group:
            spec = pl.BlockSpec(
                block,
                lambda i, me_ref, a=axis, n=len(shape): (0,) * a + (i,) + (0,) * (n - a - 1),
            )
            specs.append(spec)
            out_specs.append(spec)
            operands.append(state.reshape(shape))
            shapes.append(jax.ShapeDtypeStruct(shape, F32))
    news = pl.pallas_call(
        partial(adam_kernel, views=views, leads=leads, grads=len(grads)),
        grid_spec=pltpu.PrefetchScalarGridSpec(
            num_scalar_prefetch=1,
            grid=(pieces,),
            in_specs=[pl.BlockSpec(memory_space=pltpu.SMEM)] + specs,
            out_specs=out_specs,
            scratch_shapes=[pltpu.VMEM(pair[0].shape[1:], F32) for pair in grads],
        ),
        out_shape=shapes,
        compiler_params=pltpu.CompilerParams(vmem_limit_bytes=60 * MIB),
        cost_estimate=cost(15, 48e6),
        name="adam",
    )(me, scale, *operands)
    return [n.reshape(states[k // 3][0].shape) for k, n in enumerate(news)]


def swap(value, axis, size, bit):
    return lax.ppermute(value, axis, [(i, i ^ (1 << bit)) for i in range(size)])


def split_add(items):
    specs, operands, shapes, out_specs = [], [], [], []
    half = items[0][0].shape[0] // 2
    splits = 4
    for kept, got, lowest in items:
        cut = kept.shape[2] % (16 * splits) == 0
        block = (1, kept.shape[1], kept.shape[2] // (splits if cut else 1), kept.shape[3])

        def at(index, cut=cut):
            return lambda i, s: (index(i), 0, s if cut else 0, 0)

        away = at((lambda i: 2 * i + 1) if lowest else (lambda i: half + i))
        stay = at((lambda i: 2 * i) if lowest else (lambda i: i))
        for index, kind in ((away, got.dtype), (stay, F32)):
            specs += [pl.BlockSpec(block, index)] * 2
            operands += [kept, got]
            out_specs.append(pl.BlockSpec(block, at(lambda i: i)))
            shapes.append(jax.ShapeDtypeStruct((half,) + kept.shape[1:], kind))

    def body(*refs):
        outs = refs[len(operands) :]
        for k, out in enumerate(outs):
            out[...] = (refs[2 * k][...] + refs[2 * k + 1][...].astype(F32)).astype(out.dtype)

    res = pl.pallas_call(
        body,
        grid=(half, splits),
        in_specs=specs,
        out_specs=out_specs,
        out_shape=shapes,
        compiler_params=pltpu.CompilerParams(vmem_limit_bytes=24 * MIB),
        cost_estimate=cost(3, 12e6),
        name="split_add",
    )(*operands)
    return [(res[2 * k], res[2 * k + 1]) for k in range(len(items))]


class Reduction:
    def __init__(self, pairs, orders, size):
        self.size = size
        self.orders = [list(order) for order in orders]
        self.lowest = [order == sorted(order) for order in orders]
        self.kept = [keep for _, keep in pairs]
        self.got = [swap(send, "dp", size, 0) for send, _ in pairs]

    def split(self):
        items = list(zip(self.kept, self.got, self.lowest))
        pairs = split_add(items)
        self.kept = [keep for _, keep in pairs]
        self.got = [
            swap(send, "dp", self.size, order.pop(0))
            for (send, _), order in zip(pairs, self.orders)
        ]

    def rest(self):
        while self.orders[0]:
            self.split()
        return [keep[0] + got[0].astype(F32) for keep, got in zip(self.kept, self.got)]


class Gathering:
    def __init__(self, pieces, orders, size):
        self.size = size
        self.now = list(pieces)
        self.shapes = [p.shape for p in pieces]
        self.orders = [list(order) for order in orders]
        self.have = [[] for _ in pieces]

    def start(self):
        self.other = [
            swap(now, "dp", self.size, order[0]) for now, order in zip(self.now, self.orders)
        ]

    def finish(self):
        for k, order in enumerate(self.orders):
            bit = order.pop(0)
            at = len([b for b in self.have[k] if b > bit])
            self.now[k] = jnp.stack([self.now[k], self.other[k]], axis=at)
            self.have[k] = sorted(self.have[k] + [bit], reverse=True)

    def double(self):
        self.start()
        self.finish()

    def across(self):
        while self.orders[0]:
            self.double()

    def pairs(self):
        self.across()
        own = [n.reshape((self.size // 2,) + s) for n, s in zip(self.now, self.shapes)]
        return [(n, swap(n, "dp", self.size, 0)) for n in own]


def together(*groups):
    flat, tree = jax.tree.flatten(groups)
    return jax.tree.unflatten(tree, lax.optimization_barrier(flat))


def sum_steps(value, sizes, steps):
    every = [(axis, size, bit) for axis, size in sizes for bit in range(size.bit_length() - 1)]
    for axis, size, bit in every[steps]:
        value = value + swap(value, axis, size, bit)
    return value


def split_low(table):
    high = lax.reduce_precision(table, 8, 7)
    return high.astype(BF), (table - high).astype(BF)


def spectral_tables(mode_index):
    heads = mode_index.shape[0]
    steps = jnp.arange(SEQ_LEN, dtype=jnp.int32)
    angles = (mode_index[:, :, None] * steps % SEQ_LEN).astype(F32) * (2.0 * math.pi / SEQ_LEN)
    ahead = jnp.concatenate([jnp.cos(angles), -jnp.sin(angles)], axis=1)
    if heads == 1:
        ahead = jnp.concatenate([ahead, jnp.zeros_like(ahead)], axis=0)
    ahead = ahead.reshape(2 * SEQ_LEN, SEQ_LEN)
    orders = jnp.arange(MODES, dtype=jnp.int32)
    angles = (steps[:, None] * orders % SEQ_LEN).astype(F32) * (2.0 * math.pi / SEQ_LEN)
    weights = jnp.where(orders == 0, 1.0, 2.0).astype(F32) / SEQ_LEN
    back = jnp.concatenate([jnp.cos(angles) * weights, -jnp.sin(angles) * weights], axis=1)
    tables = [jnp.concatenate(split_low(t), axis=1) for t in (ahead, back, back.T, ahead.T)]
    tables[1] = jnp.concatenate([tables[1], tables[1][:, :SEQ_LEN]], axis=1)
    return tables


def on_device(
    sizes,
    series,
    target,
    valid,
    window_id,
    mode_index,
    query_weight,
    query_first,
    query_second,
    out_weight,
    out_first,
    out_second,
    mode_weight,
    mode_first,
    mode_second,
    up_weight,
    up_first,
    up_second,
    down_weight,
    down_first,
    down_second,
    bias_pair,
    bias_first,
    bias_second,
    decomp_params,
    decomp_first,
    decomp_second,
):
    ndp, nhead = sizes
    bits = ndp.bit_length() - 1
    order_a = list(range(1, bits))
    order_b = order_a[::-1]
    dp = lax.axis_index("dp")
    head = lax.axis_index("head")
    me = dp.astype(jnp.int32).reshape(1)
    rows, d = series.shape
    own_heads = mode_index.shape[0]
    width = query_weight.shape[1]
    hidden = up_weight.shape[1]

    everyone = (("dp", ndp), ("head", nhead))
    place = jnp.concatenate([me, head.astype(jnp.int32).reshape(1)])

    def shift(v, r):
        return lax.ppermute(v, "head", [(i, (i + r) % nhead) for i in range(nhead)])

    def exchange(v):
        return lax.all_to_all(v, "head", 0, 0, tiled=True)

    def wide(v):
        pad = LANES - v.shape[-1]
        return jnp.pad(v, [(0, 0)] * (v.ndim - 1) + [(0, pad)]) if pad else v

    query_low = query_weight.astype(BF)
    query_parts = [query_low] + [shift(query_low, r) for r in range(1, nhead)]
    packed = jnp.concatenate(
        [w.astype(BF) for w in (up_weight.T, down_weight, out_weight)], axis=0
    )
    part = -(-packed.shape[0] // (16 * ndp)) * 16
    packed = jnp.pad(packed, ((0, part * ndp - packed.shape[0]), (0, 0)))
    packed = lax.dynamic_slice_in_dim(packed, dp * part, part, 0)
    packed = [packed] + [shift(packed, r) for r in range(1, nhead)]

    tf, ti, tit, tft = spectral_tables(mode_index)
    wt = mode_weight.reshape(2, own_heads * HEAD_DIM, HEAD_DIM * MODES).transpose(0, 2, 1)
    wt = wide(wt).reshape(2 * HEAD_DIM * MODES, LANES)

    def rows_of(v):
        return v[:, :, :width].reshape(-1, width)

    def contexts_of(v):
        return wide(v.reshape(-1, SEQ_LEN, width))

    def send(parts, way=1):
        return [parts[0]] + [shift(parts[r], way * r) for r in range(1, nhead)]

    starts = jnp.sum(window_id[:, None, :] < jnp.arange(5)[None, :, None], axis=2).astype(jnp.int32)
    valid_float = valid.astype(F32)
    valid_rows = valid_float[:, None]
    query_parts, wt, tf, ti, tit, tft, starts, valid_rows = together(
        query_parts, wt, tf, ti, tit, tft, starts, valid_rows
    )

    query_parts = [query_parts[-r % nhead] for r in range(nhead)]
    queries = query_call(place[1:], series, bias_pair[0], query_parts)
    queries = send(queries)
    queries[1], packed = together(queries[1], packed)
    packed = [jnp.stack(packed[: nhead // 2]), jnp.stack(packed[nhead // 2 :])]
    packed = Gathering(packed, [order_a, order_b], ndp)
    packed.start()
    queries, packed.other = together(queries, packed.other)
    packed.finish()
    packed.start()
    first, second, modes_in = spectrum_call([contexts_of(q) for q in queries], wt, tf, ti)
    first, second, packed.other = together(first, second, packed.other)
    packed.finish()
    packed = [half for pair in packed.pairs() for half in pair]
    first = send([rows_of(v) for v in first], -1)
    second = send([rows_of(v) for v in second], -1)

    half_call = partial(
        local_call,
        starts=starts,
        prm=decomp_params,
        me=me,
        x=series,
        target=target,
        valid=valid_rows,
        bias=bias_pair[1:],
        packed=packed,
        hidden=hidden,
    )
    d_first, kept_first, sums_first = half_call(0, first, [])
    d_first = send(d_first)
    d_second, kept_second, sums = half_call(1, second, [])
    d_second = send(d_second)
    sums = jnp.sum(sums + sums_first, axis=1)

    hidden_part, out_part = hidden // ndp, width // ndp
    both_halves = list(zip(kept_first, kept_second))
    active, d_hidden, season, d_feed, spectrum, d_attention = both_halves
    first_cut = hidden_part // 4 if hidden_part % 64 == 0 else 0
    down_cuts = [(c, F32) for c in (first_cut, hidden_part - first_cut) if c]
    layer = outer_call(
        me,
        [
            list(zip(season, d_hidden)),
            list(zip(active, d_feed)),
            list(zip(spectrum, d_attention)),
        ],
        [[(d // ndp, BF)], down_cuts, [(out_part, BF)]],
        ndp,
        "layer_grads",
        d_first[1:],
    )
    layer = Reduction(layer, ([order_a] * 2 + [order_b] * 2)[: len(layer)], ndp)
    layer.split()

    d_queries, d_modes, bias_part = query_grad_call(
        [contexts_of(v) for v in d_first],
        [contexts_of(v) for v in d_second],
        wt,
        tit,
        tft,
        layer.kept,
    )
    d_queries = send([rows_of(v) for v in d_queries], -1)
    layer.split()
    mode_parts = mode_grad_call(me, d_modes, modes_in, ndp, layer.kept)
    mode_parts = [m.reshape(ndp // 2, nhead, -1, LANES) for m in mode_parts]
    d_queries, mode_parts = together(d_queries, mode_parts)
    query = outer_call(
        me,
        [[(series, jnp.stack(d_queries))]],
        [[(d // ndp, BF)]],
        ndp,
        "query_weight_grads",
    )
    late = Reduction(
        [mode_parts[:2], mode_parts[2:], *query], [order_a, order_b, order_a], ndp
    )

    def over_heads(v, kind=F32):
        parts = send([v[r].astype(kind) for r in range(nhead)])
        return sum([p.astype(F32) for p in parts[1:]], v[0])

    lanes = HEAD_DIM * MODES // ndp
    up_piece, *down_pieces, out_piece = layer.rest()
    down_piece = over_heads(jnp.concatenate(down_pieces, axis=1))
    if hidden == d and out_part % 8 == 0:
        both_pieces = over_heads(jnp.concatenate([up_piece, out_piece], axis=1), BF)
        up_piece, out_piece = both_pieces[: d // ndp], both_pieces[d // ndp :]
    else:
        up_piece, out_piece = over_heads(up_piece, BF), over_heads(out_piece, BF)[:out_part]
    *mode_pieces, query_piece = late.rest()
    query_piece = over_heads(query_piece, BF)
    mode_pieces = [v.reshape(lanes, LANES).T[: own_heads * HEAD_DIM] for v in mode_pieces]
    mode_all = Gathering(mode_pieces, [order_b, order_a], ndp)
    mode_all.across()
    (up_piece, down_piece, out_piece, query_piece), mode_all.now = together(
        (up_piece, down_piece, out_piece, query_piece), mode_all.now
    )

    bias_zero = lax.dynamic_update_slice_in_dim(
        jnp.zeros((d,), F32), jnp.sum(bias_part, axis=0)[:width], head * width, 0
    )
    squares = sum(
        jnp.sum(p * p) for p in (query_piece, *mode_pieces, up_piece, down_piece, out_piece)
    )
    small = jnp.concatenate(
        [
            bias_zero,
            sums[SUM_BIAS],
            jnp.sum(sums[:SUM_BIAS], axis=1),
            jnp.stack([jnp.sum(valid_float), squares]),
        ]
    )
    small = jnp.pad(small, (0, -small.shape[0] % LANES)).reshape(-1, LANES)
    small_steps = (ndp * nhead).bit_length() - 1
    small = sum_steps(small, everyone, slice(0, 2))

    if HEAD_DIM * MODES // ndp == d and hidden == d and out_part % 8 == 0:
        ways = d // width
        per = d // ndp // ways
        query_flat = query_piece.reshape(ways, per, width).transpose(1, 0, 2).reshape(per, d)
        rest = [up_piece, jnp.concatenate([down_piece, out_piece, query_flat], axis=0)]
    else:
        rest = [up_piece, down_piece, out_piece, query_piece]
    rest_all = Gathering(rest, [order_b, order_a, order_b, order_a][: len(rest)], ndp)
    rest_all.double()
    small, rest_all.now, mode_all.now = together(small, rest_all.now, mode_all.now)
    small = sum_steps(small, everyone, slice(2, small_steps - 1))
    rest_all.across()
    grads = mode_all.pairs()
    small, rest_all.now, grads = together(small, rest_all.now, grads)
    small = sum_steps(small, everyone, slice(small_steps - 1, small_steps)).reshape(-1)
    grads += rest_all.pairs()
    loss_sum = small[2 * d + SUM_LOSS]
    valid_count = small[2 * d + SUM_LOSS + 1]
    inverse = 1.0 / valid_count
    bias_grad = small[: 2 * d].reshape(2, d) * inverse
    decomp_grad = small[2 * d : 2 * d + 4 * KERNELS].reshape(2, 2, KERNELS) * inverse
    grad_norm = jnp.sqrt(
        small[2 * d + SUM_LOSS + 2] * inverse * inverse
        + jnp.sum(bias_grad * bias_grad)
        + jnp.sum(decomp_grad * decomp_grad)
    )
    factor = jnp.minimum(1.0, CLIP_NORM / (grad_norm + 1e-06))

    everything = slice(None)

    def band(start, stop):
        return (slice(start, stop), everything)

    both = (everything, everything)
    mode_view = [
        (c, band(h * HEAD_DIM, (h + 1) * HEAD_DIM), (c, h) + both)
        for c in range(2)
        for h in range(own_heads)
    ]
    if len(rest) == 2:
        out_end = hidden_part + out_part
        views = [
            [
                (
                    3,
                    (slice(out_end, out_end + per), slice(n * width, (n + 1) * width)),
                    band(n * per, (n + 1) * per),
                )
                for n in range(ways)
            ],
            [(3, band(hidden_part, out_end), both)],
            mode_view,
            [(2, both, both)],
            [(3, band(0, hidden_part), both)],
        ]
    else:
        views = [[(5, both, both)], [(4, both, both)], mode_view, [(2, both, both)], [(3, both, both)]]

    states = (
        (query_weight, query_first, query_second),
        (out_weight, out_first, out_second),
        (mode_weight, mode_first, mode_second),
        (up_weight, up_first, up_second),
        (down_weight, down_first, down_second),
    )
    news = adam_call(me, (factor * inverse).reshape(1), grads, views, states, (0, 0, 3, 0, 0))
    news += adam_values(bias_pair, bias_grad * factor, bias_first, bias_second)
    news += adam_values(decomp_params, decomp_grad * factor, decomp_first, decomp_second)
    return (loss_sum, valid_count, grad_norm, *news)


def solution(mesh):
    rows = P(("dp", "head"), None)
    down = P("head", None)
    across = P(None, "head")
    modes = P(None, "head", None, None)
    weights = (across,) * 3 + (down,) * 3 + (modes,) * 3 + (across,) * 3 + (down,) * 3 + (P(),) * 6
    sizes = (mesh.shape["dp"], mesh.shape["head"])
    return jax.shard_map(
        partial(on_device, sizes),
        mesh=mesh,
        in_specs=(rows, rows, P(("dp", "head")), rows, down) + weights,
        out_specs=(P(), P(), P()) + weights,
        check_vma=False,
    )
```

```python
from functools import partial
import math

import jax
import jax.numpy as jnp
from jax import lax
from jax.experimental import pallas as pl
from jax.experimental.pallas import tpu as pltpu
from jax.sharding import PartitionSpec as P

MODES = 64
SEQ_LEN = 128
HEAD_DIM = 64
STEP = 10
KERNEL_WIDTHS = (7, 12, 14, 24, 48)
KERNELS = len(KERNEL_WIDTHS)
BETA_ONE = 0.9
BETA_TWO = 0.999
LEARN_RATE = 0.05
EPSILON = 1e-08
DECAY = 0.01
CLIP_NORM = 0.02
LOG2E = math.log2(math.e)
LANES = 128
BF = jnp.bfloat16
F32 = jnp.float32
MIB = 1 << 20
CHUNK = 128
UNROLL = 1

ERF_P = 0.3275911
ERF_A = (0.254829592, -0.284496736, 1.421413741, -1.453152027, 1.061405429)


def dot(a, b, ca=1, cb=0):
    return lax.dot_general(a, b, (((ca,), (cb,)), ((), ())), preferred_element_type=F32)


def cost(microseconds, moved):
    return pl.CostEstimate(
        flops=int(microseconds * 1.1e9), bytes_accessed=int(moved), transcendentals=0
    )


def query_kernel(head_ref, x_ref, b_ref, *refs):
    heads = len(refs) // 2
    x = x_ref[...]
    for r in range(heads):
        bias = b_ref[lax.rem(head_ref[0] + r, heads)]
        refs[heads + r][...] = (dot(x, refs[r][...]) + bias).astype(BF)


def query_call(head, x, bias_row, weights):
    rows, d = x.shape
    heads = len(weights)
    width = weights[0].shape[1]
    step = min(256, rows)
    return pl.pallas_call(
        query_kernel,
        grid=(rows // step,),
        in_specs=[
            pl.BlockSpec(memory_space=pltpu.SMEM),
            pl.BlockSpec((step, d), lambda i: (i, 0)),
            pl.BlockSpec((heads, 1, width), lambda i: (0, 0, 0)),
        ]
        + [pl.BlockSpec((d, width), lambda i: (0, 0)) for _ in weights],
        out_specs=[pl.BlockSpec((step, width), lambda i: (i, 0)) for _ in weights],
        out_shape=[jax.ShapeDtypeStruct((rows, width), BF) for _ in weights],
        compiler_params=pltpu.CompilerParams(vmem_limit_bytes=24 * MIB),
        cost_estimate=cost(2.5, 3e6),
        name="queries",
    )(head, x, bias_row.reshape(heads, 1, width), *weights)


def lane_low(rows):
    return lax.broadcasted_iota(jnp.int32, (rows, LANES), 1) < HEAD_DIM


def mix_blocks(wt_ref, m, count):
    low = lane_low(HEAD_DIM)
    zero = jnp.zeros((HEAD_DIM, LANES), F32)
    left = [
        wt_ref[pl.ds(c * HEAD_DIM * MODES + m, HEAD_DIM, stride=MODES), :] for c in range(2)
    ]
    blocks = []
    for _ in range(count):
        terms = [v.astype(BF).astype(F32) for v in left]
        left = [v - t for v, t in zip(left, terms)]
        real, imag = (
            jnp.concatenate([jnp.where(low, t, zero), jnp.where(low, zero, t)], axis=0)
            for t in terms
        )
        top = jnp.concatenate([real, -imag], axis=1)
        bottom = jnp.concatenate([imag, real], axis=1)
        blocks.append(jnp.concatenate([top, bottom], axis=0).astype(BF))
    return blocks


def pair_width(contexts):
    return 2 if contexts % 2 == 0 else 1


def spectrum_kernel(wt_ref, tf_ref, ti_ref, *refs):
    owners = (len(refs) - 3) // 3
    q_refs, spec_refs = refs[:owners], refs[owners : 3 * owners]
    xs_ref, x_scr, y_scr = refs[3 * owners :]
    run, width = q_refs[0].shape[0], q_refs[0].shape[2]
    half = run // 2
    contexts = owners * run
    pair = pair_width(half)
    low = lane_low(SEQ_LEN)

    for r in range(owners):

        def forward(p, _, r=r):
            cols = jnp.concatenate([q_refs[r][p * pair + k] for k in range(pair)], axis=1)
            res = dot(tf_ref[...], jnp.concatenate([cols, cols], axis=0))
            for k in range(pair):
                part = res[:, k * LANES : (k + 1) * LANES]
                row = (r * run + p * pair + k) * SEQ_LEN
                x_scr[pl.ds(pl.multiple_of(row, SEQ_LEN), SEQ_LEN), :] = jnp.where(
                    low, part[:SEQ_LEN], part[SEQ_LEN:]
                )
            return 0

        lax.fori_loop(0, run // pair, forward, 0)

    def mix(m, _):
        xr = x_scr[pl.ds(m, contexts, stride=SEQ_LEN), :].astype(BF)
        xi = x_scr[pl.ds(MODES + m, contexts, stride=SEQ_LEN), :].astype(BF)
        xs_ref[m] = jnp.concatenate([xr, xi], axis=0)
        x = jnp.concatenate([xr, xi], axis=1)
        main, rest = mix_blocks(wt_ref, m, 2)
        y = dot(x, main, 1, 1) + dot(x, rest, 1, 1)
        y_scr[pl.ds(m, contexts, stride=SEQ_LEN), :] = y[:, :LANES]
        y_scr[pl.ds(MODES + m, contexts, stride=SEQ_LEN), :] = y[:, LANES:]
        return 0

    lax.fori_loop(0, MODES, mix, 0, unroll=4)

    for r in range(owners):
        for number in range(2):
            target = spec_refs[number * owners + r]

            def inverse(p, _, r=r, number=number, target=target):
                parts = []
                for k in range(pair):
                    row = (r * run + number * half + p * pair + k) * SEQ_LEN
                    parts.append(y_scr[pl.ds(pl.multiple_of(row, SEQ_LEN), SEQ_LEN), :])
                cols = jnp.concatenate(parts, axis=1)
                main = cols.astype(BF)
                rest = (cols - main.astype(F32)).astype(BF)
                res = dot(ti_ref[...], jnp.concatenate([main, main, rest], axis=0)).astype(BF)
                for k in range(pair):
                    target[p * pair + k] = res[:, k * LANES : (k + 1) * LANES]
                return 0

            lax.fori_loop(0, half // pair, inverse, 0)


def spectrum_call(queries, wt, tf, ti):
    owners = len(queries)
    run = queries[0].shape[0]
    contexts = owners * run
    out = jax.ShapeDtypeStruct((run // 2, SEQ_LEN, LANES), BF)
    res = pl.pallas_call(
        spectrum_kernel,
        out_shape=[out] * (2 * owners)
        + [jax.ShapeDtypeStruct((MODES, 2 * contexts, LANES), BF)],
        scratch_shapes=[
            pltpu.VMEM((contexts * SEQ_LEN, LANES), F32),
            pltpu.VMEM((contexts * SEQ_LEN, LANES), F32),
        ],
        compiler_params=pltpu.CompilerParams(vmem_limit_bytes=32 * MIB),
        cost_estimate=cost(15, 7e6),
        name="spectrum",
    )(wt, tf, ti, *queries)
    return res[:owners], res[owners : 2 * owners], res[2 * owners]


def query_grad_kernel(wt_ref, tit_ref, tft_ref, *refs):
    owners = (len(refs) - 4) // 3
    d_refs, dq_refs = refs[: 2 * owners], refs[2 * owners : 3 * owners]
    dy_ref, bias_ref, y_scr, x_scr = refs[3 * owners :]
    half = d_refs[0].shape[0]
    run = 2 * half
    contexts = owners * run
    pair = pair_width(half)
    low = lane_low(SEQ_LEN)
    zero = jnp.zeros((SEQ_LEN, LANES), F32)

    for number in range(2):
        for r in range(owners):
            source = d_refs[number * owners + r]

            def forward(p, _, number=number, r=r, source=source):
                cols = jnp.concatenate([source[p * pair + k] for k in range(pair)], axis=1)
                res = dot(tit_ref[...], jnp.concatenate([cols, cols], axis=0))
                for k in range(pair):
                    row = (r * run + number * half + p * pair + k) * SEQ_LEN
                    y_scr[pl.ds(pl.multiple_of(row, SEQ_LEN), SEQ_LEN), :] = res[
                        :, k * LANES : (k + 1) * LANES
                    ]
                return 0

            lax.fori_loop(0, half // pair, forward, 0)

    def mix(m, _):
        yr = y_scr[pl.ds(m, contexts, stride=SEQ_LEN), :].astype(BF)
        yi = y_scr[pl.ds(MODES + m, contexts, stride=SEQ_LEN), :].astype(BF)
        dy = jnp.concatenate([yr, yi], axis=1)
        dy_ref[m] = dy
        dx = dot(dy, mix_blocks(wt_ref, m, 1)[0])
        x_scr[pl.ds(m, contexts, stride=SEQ_LEN), :] = dx[:, :LANES]
        x_scr[pl.ds(MODES + m, contexts, stride=SEQ_LEN), :] = dx[:, LANES:]
        return 0

    lax.fori_loop(0, MODES, mix, 0, unroll=4)
    bias_ref[...] = jnp.zeros_like(bias_ref)

    for r in range(owners):

        def inverse(p, _, r=r):
            parts = []
            for k in range(pair):
                row = (r * run + p * pair + k) * SEQ_LEN
                one = x_scr[pl.ds(pl.multiple_of(row, SEQ_LEN), SEQ_LEN), :]
                parts.append(
                    jnp.concatenate([jnp.where(low, one, zero), jnp.where(low, zero, one)], axis=0)
                )
            cols = jnp.concatenate(parts, axis=1).astype(BF)
            res = dot(tft_ref[...], jnp.concatenate([cols, cols], axis=0)).astype(BF)
            total = jnp.zeros((8, LANES), F32)
            for k in range(pair):
                one = res[:, k * LANES : (k + 1) * LANES]
                dq_refs[r][p * pair + k] = one
                total = total + jnp.sum(one.astype(F32).reshape(SEQ_LEN // 8, 8, LANES), axis=0)
            bias_ref[...] += total
            return 0

        lax.fori_loop(0, run // pair, inverse, 0)


def query_grad_call(first, second, wt, tit, tft, waits):
    owners = len(first)
    run = 2 * first[0].shape[0]
    contexts = owners * run
    whole = pl.BlockSpec(memory_space=pltpu.VMEM)

    def body(*refs):
        at = 3 + 2 * owners
        query_grad_kernel(*refs[:at], *refs[at + len(waits) :])

    res = pl.pallas_call(
        body,
        in_specs=[whole] * (3 + 2 * owners) + [pl.BlockSpec(memory_space=pl.ANY)] * len(waits),
        out_shape=[jax.ShapeDtypeStruct((run, SEQ_LEN, LANES), BF)] * owners
        + [
            jax.ShapeDtypeStruct((MODES, contexts, 2 * LANES), BF),
            jax.ShapeDtypeStruct((8, LANES), F32),
        ],
        scratch_shapes=[
            pltpu.VMEM((contexts * SEQ_LEN, LANES), F32),
            pltpu.VMEM((contexts * SEQ_LEN, LANES), F32),
        ],
        compiler_params=pltpu.CompilerParams(vmem_limit_bytes=32 * MIB),
        cost_estimate=cost(11, 7e6),
        name="query_grads",
    )(wt, tit, tft, *first, *second, *waits)
    return res[:owners], res[owners], res[owners + 1]


def mode_grad_kernel(me_ref, dy_ref, xs_ref, *refs):
    outs = refs[-6:-2]
    dw_scr, sems = refs[-2:]
    pieces, depth = 2 * outs[0].shape[0], outs[0].shape[1]
    total = HEAD_DIM * MODES
    low = lane_low(HEAD_DIM)
    me = me_ref[0]

    def mix(m, _):
        dy = dy_ref[m]
        yr, yi = dy[:, :LANES], dy[:, LANES:]
        right = jnp.concatenate(
            [jnp.concatenate([yr, yi], axis=0), jnp.concatenate([yi, -yr], axis=0)], axis=1
        )
        dw = dot(right, xs_ref[m], 0, 0)
        for c in range(2):
            first = 2 * c * HEAD_DIM
            part = jnp.where(
                low, dw[first : first + HEAD_DIM], dw[first + HEAD_DIM : first + 2 * HEAD_DIM]
            )
            dw_scr[pl.ds(c * total + m, HEAD_DIM, stride=MODES), :] = part
        return 0

    lax.fori_loop(0, MODES, mix, 0, unroll=4)
    copies = []
    for j in range(pieces):
        for c in range(2):
            start = pl.multiple_of(c * total + (me ^ j) * depth, depth)
            copies.append(
                pltpu.make_async_copy(
                    dw_scr.at[pl.ds(start, depth), :],
                    outs[2 * c + (j + 1) % 2].at[j // 2],
                    sems.at[c, j],
                )
            )
    for copy in copies:
        copy.start()
    for copy in copies:
        copy.wait()


def mode_grad_call(me, dy, xs, pieces, waits):
    part = jax.ShapeDtypeStruct((pieces // 2, HEAD_DIM * MODES // pieces, LANES), F32)
    whole = pl.BlockSpec(memory_space=pltpu.VMEM)
    return pl.pallas_call(
        mode_grad_kernel,
        in_specs=[pl.BlockSpec(memory_space=pltpu.SMEM)]
        + [whole] * 2
        + [pl.BlockSpec(memory_space=pl.ANY)] * len(waits),
        out_specs=[pl.BlockSpec(memory_space=pl.ANY)] * 4,
        out_shape=[part] * 4,
        scratch_shapes=[
            pltpu.VMEM((2 * HEAD_DIM * MODES, LANES), F32),
            pltpu.SemaphoreType.DMA((2, pieces)),
        ],
        compiler_params=pltpu.CompilerParams(vmem_limit_bytes=40 * MIB),
        cost_estimate=cost(9, 8e6),
        name="mode_grads",
    )(me, dy, xs, *waits)


SUM_SLOPE = (0, 10)
SUM_OFFSET = (5, 15)
SUM_LOSS = 20
SUM_BIAS = 21
SUM_ROWS = 24


def window_counts(first, last, rows, cols, width):
    lead = width - 1 - (width - 1) // 2
    reach = cols - rows + (lead + 1)
    here = jnp.where(cols < first, 0, jnp.where(cols >= last, width, jnp.clip(reach, 0, width)))
    before = jnp.where(
        cols <= first, 0, jnp.where(cols > last, width, jnp.clip(reach - 1, 0, width))
    )
    return (here - before).astype(F32)


def window_edges(starts, rows):
    s1, s2, s3 = starts
    first = jnp.where(rows >= s3, s3, jnp.where(rows >= s2, s2, jnp.where(rows >= s1, s1, 0)))
    last = jnp.where(
        rows < s1, s1 - 1, jnp.where(rows < s2, s2 - 1, jnp.where(rows < s3, s3 - 1, SEQ_LEN - 1))
    )
    return first, last


def fold(v):
    return jnp.sum(v.reshape(v.shape[0] // 8, 8, v.shape[1]), axis=0)


def local_kernel(*refs, chunk, hidden_width, heads, waits):
    refs = list(refs)

    def take(n):
        taken = refs[:n]
        del refs[:n]
        return taken

    starts_ref, prm_ref, me_ref, x_ref, tgt_ref, val_ref, bias_ref = take(7)
    spec_refs = take(heads)
    packed_refs = take(4)
    take(waits)
    dspec_refs = take(heads)
    act_ref, dhid_ref, low_ref, dfeed_ref, spec_out, dattn_ref, sums_ref = take(7)
    (
        u_scr,
        trend_scr,
        season_scr,
        av1_scr,
        share_scr,
        av2_scr,
        da_scr,
        part_scr,
        g_scr,
        slope_scr,
        a_scr,
        at_scr,
        weights,
        weight_sems,
    ) = refs
    step = pl.program_id(0)
    rows, d = x_ref.shape
    nctx = rows // SEQ_LEN
    out_width = dspec_refs[0].shape[1]
    up_rows = slice(0, hidden_width)
    down_rows = slice(hidden_width, 2 * hidden_width)
    out_rows = slice(2 * hidden_width, 2 * hidden_width + out_width)
    groups = d // LANES
    loops = SEQ_LEN // chunk

    def weight_copies():
        count, shared, part, _ = packed_refs[0].shape
        for number, ref in enumerate(packed_refs):
            group, bit = number // 2, number % 2
            for k in range(count):
                for r in range(shared):
                    row = pl.multiple_of((me_ref[0] ^ (2 * k + bit)) * part, part)
                    yield pltpu.make_async_copy(
                        ref.at[k, r],
                        weights.at[(heads - group * shared - r) % heads, pl.ds(row, part), :],
                        weight_sems.at[number, k * shared + r],
                    )

    @pl.when(step == 0)
    def _():
        for copy in weight_copies():
            copy.start()
        sums_ref[...] = jnp.zeros_like(sums_ref)

    def repeat(body, start):
        if loops == 1:
            return body(0, start)
        return lax.fori_loop(0, loops, body, start, unroll=UNROLL)

    row_ids = lax.broadcasted_iota(jnp.int32, (SEQ_LEN, SEQ_LEN), 0)
    col_ids = lax.broadcasted_iota(jnp.int32, (SEQ_LEN, SEQ_LEN), 1)
    for c in range(nctx):
        starts = [starts_ref[step * nctx + c, k] for k in range(1, 4)]
        first, last = window_edges(starts, row_ids)
        first_t, last_t = window_edges(starts, col_ids)
        for w, width in enumerate(KERNEL_WIDTHS):
            counts = window_counts(first, last, row_ids, col_ids, width).astype(BF)
            a_scr[c, w * SEQ_LEN : (w + 1) * SEQ_LEN, :SEQ_LEN] = counts
            a_scr[c, w * SEQ_LEN : (w + 1) * SEQ_LEN, SEQ_LEN:] = counts
            at_scr[c, :, w * SEQ_LEN : (w + 1) * SEQ_LEN] = window_counts(
                first_t, last_t, col_ids, row_ids, width
            ).astype(BF)

    @pl.when(step == 0)
    def _():
        for copy in weight_copies():
            copy.wait()

    def averages(c, u, av):
        high = u.astype(BF)
        rest = (u - high.astype(F32)).astype(BF)
        av[c] = dot(a_scr[c], jnp.concatenate([high, rest], axis=0))

    spec = jnp.concatenate([ref[...] for ref in spec_refs], axis=1)
    for h in range(heads):
        spec_out[h] = spec_refs[h][...]
    out_all = jnp.concatenate([weights[h, out_rows] for h in range(heads)], axis=0)
    pre = x_ref[...].astype(F32) + (dot(spec, out_all) + bias_ref[...])
    u_scr[...] = pre
    for c in range(nctx):
        averages(c, pre[c * SEQ_LEN : (c + 1) * SEQ_LEN], av1_scr)

    def shares_of(u, avs, layer):
        logits = [
            u * (prm_ref[layer, 0, w] * LOG2E) + prm_ref[layer, 1, w] * LOG2E
            for w in range(KERNELS)
        ]
        top = logits[0]
        for v in logits[1:]:
            top = jnp.maximum(top, v)
        powers = [jnp.exp2(v - top) for v in logits]
        total = powers[0]
        for v in powers[1:]:
            total = total + v
        scale = 1.0 / total
        shares = [v * scale for v in powers]
        trend = shares[0] * avs[0]
        for s, a in zip(shares[1:], avs[1:]):
            trend = trend + s * a
        return shares, trend

    def read_averages(av, c, row, lanes):
        return [
            av[c, pl.ds(w * SEQ_LEN + row, chunk), lanes] * (1.0 / width)
            for w, width in enumerate(KERNEL_WIDTHS)
        ]

    def pull(shares, avs, trend, grad, u, layer, base, c, row, lanes, sums):
        rest = base
        slopes, offsets = [], []
        for w, width in enumerate(KERNEL_WIDTHS):
            d_avg = shares[w] * grad
            da_scr[c, pl.ds(w * SEQ_LEN + row, chunk), lanes] = (d_avg * (1.0 / width)).astype(BF)
            d_logit = d_avg * (avs[w] - trend)
            rest = rest + d_logit * prm_ref[layer, 0, w]
            slopes.append(sums[w] + fold(d_logit * u))
            offsets.append(sums[KERNELS + w] + fold(d_logit))
        return rest, slopes + offsets

    for c in range(nctx):
        for g in range(groups):
            lanes = slice(g * LANES, (g + 1) * LANES)

            def first_pass(r, _, c=c, lanes=lanes):
                row = r * chunk if loops == 1 else pl.multiple_of(r * chunk, chunk)
                at = pl.ds(c * SEQ_LEN + row, chunk)
                u = u_scr[at, lanes]
                avs = read_averages(av1_scr, c, row, lanes)
                shares, trend = shares_of(u, avs, 0)
                for w in range(KERNELS):
                    share_scr[c, pl.ds(w * SEQ_LEN + row, chunk), lanes] = shares[w]
                season = u - trend
                trend_scr[at, lanes] = trend
                season_scr[at, lanes] = season
                low_ref[at, lanes] = season.astype(BF)
                return 0

            repeat(first_pass, 0)

    season_low = low_ref[...]
    feed = jnp.zeros((rows, d), F32)
    for h in range(heads):
        hid = dot(season_low, weights[h, up_rows], 1, 1)
        z = jnp.abs(hid) * (2.0**-0.5)
        t = 1.0 / (1.0 + ERF_P * z)
        e = jnp.exp2(hid * hid * (-0.5 * LOG2E))
        poly = ERF_A[4]
        for coef in ERF_A[3::-1]:
            poly = poly * t + coef
        tail = (0.5 * t) * poly * e
        phi = jnp.where(hid < 0, tail, 1.0 - tail)
        active = (hid * phi).astype(BF)
        slope_scr[h] = phi + hid * e * ((2.0 * math.pi) ** -0.5)
        act_ref[h] = active
        feed = feed + dot(active, weights[h, down_rows])

    pre = season_scr[...] + feed
    g_scr[...] = pre
    for c in range(nctx):
        averages(c, pre[c * SEQ_LEN : (c + 1) * SEQ_LEN], av2_scr)

    for c in range(nctx):
        for g in range(groups):
            lanes = slice(g * LANES, (g + 1) * LANES)

            def second_pass(r, sums, c=c, lanes=lanes):
                row = r * chunk if loops == 1 else pl.multiple_of(r * chunk, chunk)
                at = pl.ds(c * SEQ_LEN + row, chunk)
                u = g_scr[at, lanes]
                avs = read_averages(av2_scr, c, row, lanes)
                shares, trend = shares_of(u, avs, 1)
                misfit = trend_scr[at, lanes] + trend - tgt_ref[at, lanes]
                weighted = val_ref[at, :] * misfit
                grad = 2.0 * weighted
                rest, new = pull(
                    shares, avs, trend, grad, u, 1, jnp.zeros_like(u), c, row, lanes, sums
                )
                part_scr[at, lanes] = rest
                g_scr[at, lanes] = grad
                return tuple(new) + (sums[2 * KERNELS] + fold(weighted * misfit),)

            zeros = tuple(jnp.zeros((8, LANES), F32) for _ in range(2 * KERNELS + 1))
            sums = repeat(second_pass, zeros)
            for k in range(KERNELS):
                sums_ref[SUM_SLOPE[1] + k, :, lanes] += sums[k]
                sums_ref[SUM_OFFSET[1] + k, :, lanes] += sums[KERNELS + k]
            sums_ref[SUM_LOSS, :, lanes] += sums[2 * KERNELS]

    for c in range(nctx):
        at = slice(c * SEQ_LEN, (c + 1) * SEQ_LEN)
        part_scr[at, :] += dot(at_scr[c], da_scr[c])

    d_pre = part_scr[...]
    d_feed = d_pre.astype(BF)
    dfeed_ref[...] = d_feed
    back = d_pre
    for h in range(heads):
        d_hid = (dot(d_feed, weights[h, down_rows], 1, 1) * slope_scr[h]).astype(BF)
        back = back + dot(d_hid, weights[h, up_rows])
        dhid_ref[h] = d_hid
    season_scr[...] = back

    for c in range(nctx):
        for g in range(groups):
            lanes = slice(g * LANES, (g + 1) * LANES)

            def third_pass(r, sums, c=c, lanes=lanes):
                row = r * chunk if loops == 1 else pl.multiple_of(r * chunk, chunk)
                at = pl.ds(c * SEQ_LEN + row, chunk)
                u = u_scr[at, lanes]
                avs = read_averages(av1_scr, c, row, lanes)
                shares = [
                    share_scr[c, pl.ds(w * SEQ_LEN + row, chunk), lanes] for w in range(KERNELS)
                ]
                d_season = season_scr[at, lanes]
                rest, new = pull(
                    shares,
                    avs,
                    trend_scr[at, lanes],
                    g_scr[at, lanes] - d_season,
                    u,
                    0,
                    d_season,
                    c,
                    row,
                    lanes,
                    sums,
                )
                part_scr[at, lanes] = rest
                return tuple(new)

            zeros = tuple(jnp.zeros((8, LANES), F32) for _ in range(2 * KERNELS))
            sums = repeat(third_pass, zeros)
            for k in range(KERNELS):
                sums_ref[SUM_SLOPE[0] + k, :, lanes] += sums[k]
                sums_ref[SUM_OFFSET[0] + k, :, lanes] += sums[KERNELS + k]

    for c in range(nctx):
        at = slice(c * SEQ_LEN, (c + 1) * SEQ_LEN)
        part_scr[at, :] += dot(at_scr[c], da_scr[c])

    d_pre = part_scr[...]
    sums_ref[SUM_BIAS] += fold(d_pre)
    d_attn = d_pre.astype(BF)
    dattn_ref[...] = d_attn
    d_spec = dot(d_attn, out_all, 1, 1).astype(BF)
    for h in range(heads):
        dspec_refs[h][...] = d_spec[:, h * out_width : (h + 1) * out_width]


def up8(n):
    return -(-n // 8) * 8


def local_call(number, spec, waits, starts, prm, me, x, target, valid, bias, packed, hidden):
    rows_half = x.shape[0] // 2
    d = x.shape[1]
    heads = len(spec)
    width = spec[0].shape[1]
    nctx = 2 if rows_half % (2 * SEQ_LEN) == 0 else 1
    rows = nctx * SEQ_LEN
    steps = rows_half // rows
    smem = pl.BlockSpec(memory_space=pltpu.SMEM)
    whole = pl.BlockSpec(memory_space=pltpu.VMEM)
    anywhere = pl.BlockSpec(memory_space=pl.ANY)
    averages = (nctx, KERNELS * SEQ_LEN, d)
    count, shared, part, _ = packed[0].shape

    def row_block(columns, half=0):
        return pl.BlockSpec((rows, columns), lambda i: (half * steps + i, 0))

    def head_block(columns):
        return pl.BlockSpec((heads, rows, columns), lambda i: (0, i, 0))

    ctx_half = starts.shape[0] // 2
    res = pl.pallas_call(
        partial(local_kernel, chunk=CHUNK, hidden_width=hidden, heads=heads, waits=len(waits)),
        grid=(steps,),
        in_specs=[smem] * 3
        + [row_block(d, number), row_block(d, number), row_block(1, number), whole]
        + [row_block(width)] * heads
        + [anywhere] * (len(packed) + len(waits)),
        out_specs=[row_block(width)] * heads
        + [head_block(hidden), head_block(hidden), row_block(d), row_block(d)]
        + [head_block(width), row_block(d)]
        + [pl.BlockSpec((SUM_ROWS, 8, d), lambda i: (0, 0, 0))],
        out_shape=[jax.ShapeDtypeStruct((rows_half, width), BF)] * heads
        + [jax.ShapeDtypeStruct((heads, rows_half, hidden), BF)] * 2
        + [jax.ShapeDtypeStruct((rows_half, d), BF)] * 2
        + [
            jax.ShapeDtypeStruct((heads, rows_half, width), BF),
            jax.ShapeDtypeStruct((rows_half, d), BF),
            jax.ShapeDtypeStruct((SUM_ROWS, 8, d), F32),
        ],
        scratch_shapes=[
            pltpu.VMEM((rows, d), F32),
            pltpu.VMEM((rows, d), F32),
            pltpu.VMEM((rows, d), F32),
            pltpu.VMEM(averages, F32),
            pltpu.VMEM(averages, F32),
            pltpu.VMEM(averages, F32),
            pltpu.VMEM(averages, BF),
            pltpu.VMEM((rows, d), F32),
            pltpu.VMEM((rows, d), F32),
            pltpu.VMEM((heads, rows, hidden), F32),
            pltpu.VMEM((nctx, KERNELS * SEQ_LEN, 2 * SEQ_LEN), BF),
            pltpu.VMEM((nctx, SEQ_LEN, KERNELS * SEQ_LEN), BF),
            pltpu.VMEM((heads, len(packed) * count // 2 * part, d), BF),
            pltpu.SemaphoreType.DMA((len(packed), count * shared)),
        ],
        compiler_params=pltpu.CompilerParams(vmem_limit_bytes=56 * MIB),
        cost_estimate=cost(26, 24e6),
        name="local_layer",
    )(
        starts[number * ctx_half : (number + 1) * ctx_half],
        prm,
        me,
        x,
        target,
        valid,
        bias,
        *spec,
        *packed,
        *waits,
    )
    return res[:heads], res[heads:-1], res[-1]


def outer_kernel(me_ref, *refs, halves, outs, waits):
    scratch = refs[-1]
    ins = list(refs[: 2 * sum(halves)])
    targets = list(refs[2 * sum(halves) + waits : -1])
    for count, cuts in zip(halves, outs):
        total = None
        for _ in range(count):
            left, right = (r[0] if len(r.shape) == 3 else r[...] for r in ins[:2])
            del ins[:2]
            term = dot(left, right, 0, 0)
            total = term if total is None else total + term
        rows, columns = total.shape
        lanes = slice(0, columns)
        scratch[:rows, lanes] = total
        offset = 0
        for cut in cuts:
            send, keep = targets[:2]
            del targets[:2]
            pieces = 2 * send.shape[0]
            size = rows // pieces
            for j in range(pieces):
                target = send if j % 2 else keep
                start = (me_ref[0] ^ j) * size + offset
                if cut % 8 == 0:
                    part = scratch[pl.ds(pl.multiple_of(start, 8), cut), lanes]
                    target[j // 2, 0] = part.astype(target.dtype)
                else:
                    row = lax.broadcasted_iota(jnp.int32, (target.shape[2], 1), 0)
                    part = jnp.zeros((target.shape[2], columns), F32)
                    for i in range(cut):
                        part = jnp.where(row == i, scratch[pl.ds(start + i, 1), lanes], part)
                    target[j // 2, 0] = part.astype(target.dtype)
            offset += cut


def outer_call(me, products, outs, pieces, name, waits=()):
    heads = next(a.shape[0] for p in products for pair in p for a in pair if a.ndim == 3)
    operands = [a for p in products for pair in p for a in pair]

    def spec(a):
        if a.ndim == 3:
            return pl.BlockSpec((1,) + a.shape[1:], lambda h: (h, 0, 0))
        return pl.BlockSpec(a.shape, lambda h: (0, 0))

    shapes = []
    for p, cuts in zip(products, outs):
        for cut, kind in cuts:
            tail = (cut if cut % 8 == 0 else 16, p[0][1].shape[-1])
            shapes += [
                jax.ShapeDtypeStruct((pieces // 2, heads) + tail, t) for t in (kind, F32)
            ]
    rows = max(pair[0].shape[-1] for p in products for pair in p)
    columns = max(pair[1].shape[-1] for p in products for pair in p)
    res = pl.pallas_call(
        partial(
            outer_kernel,
            halves=[len(p) for p in products],
            outs=[[cut for cut, _ in cuts] for cuts in outs],
            waits=len(waits),
        ),
        grid=(heads,),
        in_specs=[pl.BlockSpec(memory_space=pltpu.SMEM)]
        + [spec(a) for a in operands]
        + [pl.BlockSpec(memory_space=pl.ANY)] * len(waits),
        out_specs=[
            pl.BlockSpec((s.shape[0], 1) + s.shape[2:], lambda h: (0, h, 0, 0)) for s in shapes
        ],
        out_shape=shapes,
        scratch_shapes=[pltpu.VMEM((rows, columns), F32)],
        compiler_params=pltpu.CompilerParams(vmem_limit_bytes=60 * MIB),
        cost_estimate=cost(0.3, 1e5),
        name=name,
    )(me, *operands, *waits)
    return [(res[2 * k], res[2 * k + 1]) for k in range(len(res) // 2)]


def adam_values(weight, gradient, first, second):
    m = BETA_ONE * first + (1.0 - BETA_ONE) * gradient
    v = BETA_TWO * second + (1.0 - BETA_TWO) * gradient * gradient
    first_hat = m * (1.0 / (1.0 - BETA_ONE**STEP))
    second_hat = v * (1.0 / (1.0 - BETA_TWO**STEP))
    return (
        weight - LEARN_RATE * (first_hat / (jnp.sqrt(second_hat) + EPSILON) + DECAY * weight),
        m,
        v,
    )


def adam_kernel(me_ref, scale_ref, *refs, views, leads, grads):
    scale = scale_ref[0]
    count = len(views)
    pairs = refs[: 2 * grads]
    states = refs[2 * grads : 2 * grads + 3 * count]
    outs = refs[2 * grads + 3 * count : 2 * grads + 6 * count]
    chosen = refs[2 * grads + 6 * count :]
    other = (pl.program_id(0) ^ me_ref[0]) & 1

    @pl.when(other == 0)
    def _():
        for k in range(grads):
            chosen[k][...] = pairs[2 * k][0]

    @pl.when(other == 1)
    def _():
        for k in range(grads):
            chosen[k][...] = pairs[2 * k + 1][0]

    for k, parts in enumerate(views):
        lead = leads[k]
        for which, source, place in parts:
            ins = [r.at[lead][place] for r in states[3 * k : 3 * k + 3]]
            g = chosen[which][source] * scale
            new = adam_values(ins[0], g, ins[1], ins[2])
            for r, value in zip(outs[3 * k : 3 * k + 3], new):
                r.at[lead][place] = value


def adam_call(me, scale, grads, views, states, axes):
    pieces = 2 * grads[0][0].shape[0]
    specs, out_specs, operands, shapes, leads = [], [], [], [], []
    for pair in grads:
        zeros = (0,) * (pair[0].ndim - 1)
        for grad in pair:
            specs.append(
                pl.BlockSpec(
                    (1,) + grad.shape[1:],
                    lambda i, me_ref, z=zeros: (lax.div(i ^ me_ref[0], 2),) + z,
                )
            )
            operands.append(grad)
    for group, axis in zip(states, axes):
        shape = group[0].shape
        size = shape[axis] // pieces
        direct = size % (LANES if axis == len(shape) - 1 else 8) == 0
        if not direct:
            shape = shape[:axis] + (pieces, size) + shape[axis + 1 :]
        block = shape[:axis] + (size if direct else 1,) + shape[axis + 1 :]
        leads.append((slice(None),) * axis + ((slice(None),) if direct else (0,)))
        for state in group:
            spec = pl.BlockSpec(
                block,
                lambda i, me_ref, a=axis, n=len(shape): (0,) * a + (i,) + (0,) * (n - a - 1),
            )
            specs.append(spec)
            out_specs.append(spec)
            operands.append(state.reshape(shape))
            shapes.append(jax.ShapeDtypeStruct(shape, F32))
    news = pl.pallas_call(
        partial(adam_kernel, views=views, leads=leads, grads=len(grads)),
        grid_spec=pltpu.PrefetchScalarGridSpec(
            num_scalar_prefetch=1,
            grid=(pieces,),
            in_specs=[pl.BlockSpec(memory_space=pltpu.SMEM)] + specs,
            out_specs=out_specs,
            scratch_shapes=[pltpu.VMEM(pair[0].shape[1:], F32) for pair in grads],
        ),
        out_shape=shapes,
        compiler_params=pltpu.CompilerParams(vmem_limit_bytes=60 * MIB),
        cost_estimate=cost(15, 48e6),
        name="adam",
    )(me, scale, *operands)
    return [n.reshape(states[k // 3][0].shape) for k, n in enumerate(news)]


def swap(value, axis, size, bit):
    return lax.ppermute(value, axis, [(i, i ^ (1 << bit)) for i in range(size)])


def split_add(items):
    specs, operands, shapes, out_specs = [], [], [], []
    half = items[0][0].shape[0] // 2
    splits = 4
    for kept, got, lowest in items:
        cut = kept.shape[2] % (16 * splits) == 0
        block = (1, kept.shape[1], kept.shape[2] // (splits if cut else 1), kept.shape[3])

        def at(index, cut=cut):
            return lambda i, s: (index(i), 0, s if cut else 0, 0)

        away = at((lambda i: 2 * i + 1) if lowest else (lambda i: half + i))
        stay = at((lambda i: 2 * i) if lowest else (lambda i: i))
        for index, kind in ((away, got.dtype), (stay, F32)):
            specs += [pl.BlockSpec(block, index)] * 2
            operands += [kept, got]
            out_specs.append(pl.BlockSpec(block, at(lambda i: i)))
            shapes.append(jax.ShapeDtypeStruct((half,) + kept.shape[1:], kind))

    def body(*refs):
        outs = refs[len(operands) :]
        for k, out in enumerate(outs):
            out[...] = (refs[2 * k][...] + refs[2 * k + 1][...].astype(F32)).astype(out.dtype)

    res = pl.pallas_call(
        body,
        grid=(half, splits),
        in_specs=specs,
        out_specs=out_specs,
        out_shape=shapes,
        compiler_params=pltpu.CompilerParams(vmem_limit_bytes=24 * MIB),
        cost_estimate=cost(0.3, 1e5),
        name="split_add",
    )(*operands)
    return [(res[2 * k], res[2 * k + 1]) for k in range(len(items))]


class Reduction:
    def __init__(self, pairs, orders, size):
        self.size = size
        self.orders = [list(order) for order in orders]
        self.lowest = [order == sorted(order) for order in orders]
        self.kept = [keep for _, keep in pairs]
        self.got = [swap(send, "dp", size, 0) for send, _ in pairs]

    def split(self):
        items = list(zip(self.kept, self.got, self.lowest))
        pairs = split_add(items)
        self.kept = [keep for _, keep in pairs]
        self.got = [
            swap(send, "dp", self.size, order.pop(0))
            for (send, _), order in zip(pairs, self.orders)
        ]

    def rest(self):
        while self.orders[0]:
            self.split()
        return [keep[0] + got[0].astype(F32) for keep, got in zip(self.kept, self.got)]


class Gathering:
    def __init__(self, pieces, orders, size):
        self.size = size
        self.now = list(pieces)
        self.shapes = [p.shape for p in pieces]
        self.orders = [list(order) for order in orders]
        self.have = [[] for _ in pieces]

    def start(self):
        self.other = [
            swap(now, "dp", self.size, order[0]) for now, order in zip(self.now, self.orders)
        ]

    def finish(self):
        for k, order in enumerate(self.orders):
            bit = order.pop(0)
            at = len([b for b in self.have[k] if b > bit])
            self.now[k] = jnp.stack([self.now[k], self.other[k]], axis=at)
            self.have[k] = sorted(self.have[k] + [bit], reverse=True)

    def double(self):
        self.start()
        self.finish()

    def across(self):
        while self.orders[0]:
            self.double()

    def pairs(self):
        self.across()
        own = [n.reshape((self.size // 2,) + s) for n, s in zip(self.now, self.shapes)]
        return [(n, swap(n, "dp", self.size, 0)) for n in own]


def together(*groups):
    flat, tree = jax.tree.flatten(groups)
    return jax.tree.unflatten(tree, lax.optimization_barrier(flat))


def sum_steps(value, sizes, steps):
    every = [(axis, size, bit) for axis, size in sizes for bit in range(size.bit_length() - 1)]
    for axis, size, bit in every[steps]:
        value = value + swap(value, axis, size, bit)
    return value


def split_low(table):
    high = lax.reduce_precision(table, 8, 7)
    return high.astype(BF), (table - high).astype(BF)


def spectral_tables(mode_index):
    heads = mode_index.shape[0]
    steps = jnp.arange(SEQ_LEN, dtype=jnp.int32)
    angles = (mode_index[:, :, None] * steps % SEQ_LEN).astype(F32) * (2.0 * math.pi / SEQ_LEN)
    ahead = jnp.concatenate([jnp.cos(angles), -jnp.sin(angles)], axis=1)
    if heads == 1:
        ahead = jnp.concatenate([ahead, jnp.zeros_like(ahead)], axis=0)
    ahead = ahead.reshape(2 * SEQ_LEN, SEQ_LEN)
    orders = jnp.arange(MODES, dtype=jnp.int32)
    angles = (steps[:, None] * orders % SEQ_LEN).astype(F32) * (2.0 * math.pi / SEQ_LEN)
    weights = jnp.where(orders == 0, 1.0, 2.0).astype(F32) / SEQ_LEN
    back = jnp.concatenate([jnp.cos(angles) * weights, -jnp.sin(angles) * weights], axis=1)
    tables = [jnp.concatenate(split_low(t), axis=1) for t in (ahead, back, back.T, ahead.T)]
    tables[1] = jnp.concatenate([tables[1], tables[1][:, :SEQ_LEN]], axis=1)
    return tables


def on_device(
    sizes,
    series,
    target,
    valid,
    window_id,
    mode_index,
    query_weight,
    query_first,
    query_second,
    out_weight,
    out_first,
    out_second,
    mode_weight,
    mode_first,
    mode_second,
    up_weight,
    up_first,
    up_second,
    down_weight,
    down_first,
    down_second,
    bias_pair,
    bias_first,
    bias_second,
    decomp_params,
    decomp_first,
    decomp_second,
):
    ndp, nhead = sizes
    bits = ndp.bit_length() - 1
    order_a = list(range(1, bits))
    order_b = order_a[::-1]
    dp = lax.axis_index("dp")
    head = lax.axis_index("head")
    me = dp.astype(jnp.int32).reshape(1)
    rows, d = series.shape
    own_heads = mode_index.shape[0]
    width = query_weight.shape[1]
    hidden = up_weight.shape[1]

    everyone = (("dp", ndp), ("head", nhead))
    place = jnp.concatenate([me, head.astype(jnp.int32).reshape(1)])

    def shift(v, r):
        return lax.ppermute(v, "head", [(i, (i + r) % nhead) for i in range(nhead)])

    def exchange(v):
        return lax.all_to_all(v, "head", 0, 0, tiled=True)

    def wide(v):
        pad = LANES - v.shape[-1]
        return jnp.pad(v, [(0, 0)] * (v.ndim - 1) + [(0, pad)]) if pad else v

    query_low = query_weight.astype(BF)
    query_parts = [query_low] + [shift(query_low, r) for r in range(1, nhead)]
    packed = jnp.concatenate(
        [w.astype(BF) for w in (up_weight.T, down_weight, out_weight)], axis=0
    )
    part = -(-packed.shape[0] // (16 * ndp)) * 16
    packed = jnp.pad(packed, ((0, part * ndp - packed.shape[0]), (0, 0)))
    packed = lax.dynamic_slice_in_dim(packed, dp * part, part, 0)
    packed = [packed] + [shift(packed, r) for r in range(1, nhead)]

    tf, ti, tit, tft = spectral_tables(mode_index)
    wt = mode_weight.reshape(2, own_heads * HEAD_DIM, HEAD_DIM * MODES).transpose(0, 2, 1)
    wt = wide(wt).reshape(2 * HEAD_DIM * MODES, LANES)

    def rows_of(v):
        return v[:, :, :width].reshape(-1, width)

    def contexts_of(v):
        return wide(v.reshape(-1, SEQ_LEN, width))

    def send(parts, way=1):
        return [parts[0]] + [shift(parts[r], way * r) for r in range(1, nhead)]

    starts = jnp.sum(window_id[:, None, :] < jnp.arange(5)[None, :, None], axis=2).astype(jnp.int32)
    valid_float = valid.astype(F32)
    valid_rows = valid_float[:, None]
    query_parts, wt, tf, ti, tit, tft, starts, valid_rows = together(
        query_parts, wt, tf, ti, tit, tft, starts, valid_rows
    )

    query_parts = [query_parts[-r % nhead] for r in range(nhead)]
    queries = query_call(place[1:], series, bias_pair[0], query_parts)
    queries = send(queries)
    queries[1], packed = together(queries[1], packed)
    packed = [jnp.stack(packed[: nhead // 2]), jnp.stack(packed[nhead // 2 :])]
    packed = Gathering(packed, [order_a, order_b], ndp)
    packed.start()
    queries, packed.other = together(queries, packed.other)
    packed.finish()
    packed.start()
    first, second, modes_in = spectrum_call([contexts_of(q) for q in queries], wt, tf, ti)
    first, second, packed.other = together(first, second, packed.other)
    packed.finish()
    packed = [half for pair in packed.pairs() for half in pair]
    first = send([rows_of(v) for v in first], -1)
    first, second = together(first, second)
    second = send([rows_of(v) for v in second], -1)

    half_call = partial(
        local_call,
        starts=starts,
        prm=decomp_params,
        me=me,
        x=series,
        target=target,
        valid=valid_rows,
        bias=bias_pair[1:],
        packed=packed,
        hidden=hidden,
    )
    d_first, kept_first, sums_first = half_call(0, first, [])
    d_first = send(d_first)
    d_second, kept_second, sums = half_call(1, second, [])
    d_second = send(d_second)
    sums = jnp.sum(sums + sums_first, axis=1)

    hidden_part, out_part = hidden // ndp, width // ndp
    both_halves = list(zip(kept_first, kept_second))
    active, d_hidden, season, d_feed, spectrum, d_attention = both_halves
    first_cut = hidden_part // 4 if hidden_part % 64 == 0 else 0
    down_cuts = [(c, F32) for c in (first_cut, hidden_part - first_cut) if c]
    layer = outer_call(
        me,
        [
            list(zip(season, d_hidden)),
            list(zip(active, d_feed)),
            list(zip(spectrum, d_attention)),
        ],
        [[(d // ndp, BF)], down_cuts, [(out_part, F32)]],
        ndp,
        "layer_grads",
        d_first[1:],
    )
    layer = Reduction(layer, ([order_a] * 2 + [order_b] * 2)[: len(layer)], ndp)
    layer.split()

    d_queries, d_modes, bias_part = query_grad_call(
        [contexts_of(v) for v in d_first],
        [contexts_of(v) for v in d_second],
        wt,
        tit,
        tft,
        layer.kept,
    )
    d_queries = send([rows_of(v) for v in d_queries], -1)
    layer.split()
    mode_parts = mode_grad_call(me, d_modes, modes_in, ndp, layer.kept)
    mode_parts = [m.reshape(ndp // 2, nhead, -1, LANES) for m in mode_parts]
    d_queries, mode_parts = together(d_queries, mode_parts)
    query = outer_call(
        me,
        [[(series, jnp.stack(d_queries))]],
        [[(d // ndp, BF)]],
        ndp,
        "query_weight_grads",
    )
    query = Reduction(query, [order_a], ndp)
    query.split()
    modes = Reduction([mode_parts[:2], mode_parts[2:]], [order_a, order_b], ndp)
    query.got, modes.got = together(query.got, modes.got)
    modes.split()

    def over_heads(v, kind=F32):
        parts = send([v[r].astype(kind) for r in range(nhead)])
        return sum([p.astype(F32) for p in parts[1:]], v[0])

    lanes = HEAD_DIM * MODES // ndp
    up_piece, *down_pieces, out_piece = layer.rest()
    down_piece = over_heads(jnp.concatenate([*down_pieces, out_piece], axis=1))
    down_piece, out_piece = down_piece[:hidden_part], down_piece[hidden_part:][:out_part]
    up_piece = over_heads(up_piece, BF)
    (query_piece,) = [over_heads(v, BF) for v in query.rest()]
    mode_pieces = modes.rest()
    mode_pieces = [v.reshape(lanes, LANES).T[: own_heads * HEAD_DIM] for v in mode_pieces]
    mode_all = Gathering(mode_pieces, [order_b, order_a], ndp)
    mode_all.across()
    (up_piece, down_piece, out_piece, query_piece), mode_all.now = together(
        (up_piece, down_piece, out_piece, query_piece), mode_all.now
    )

    bias_zero = lax.dynamic_update_slice_in_dim(
        jnp.zeros((d,), F32), jnp.sum(bias_part, axis=0)[:width], head * width, 0
    )
    squares = sum(
        jnp.sum(p * p) for p in (query_piece, *mode_pieces, up_piece, down_piece, out_piece)
    )
    small = jnp.concatenate(
        [
            bias_zero,
            sums[SUM_BIAS],
            jnp.sum(sums[:SUM_BIAS], axis=1),
            jnp.stack([jnp.sum(valid_float), squares]),
        ]
    )
    small = jnp.pad(small, (0, -small.shape[0] % LANES)).reshape(-1, LANES)
    small_steps = (ndp * nhead).bit_length() - 1
    small = sum_steps(small, everyone, slice(0, 2))

    if HEAD_DIM * MODES // ndp == d and hidden == d and out_part % 8 == 0:
        ways = d // width
        per = d // ndp // ways
        query_flat = query_piece.reshape(ways, per, width).transpose(1, 0, 2).reshape(per, d)
        rest = [up_piece, jnp.concatenate([down_piece, out_piece, query_flat], axis=0)]
    else:
        rest = [up_piece, down_piece, out_piece, query_piece]
    rest_all = Gathering(rest, [order_b, order_a, order_b, order_a][: len(rest)], ndp)
    rest_all.double()
    small, rest_all.now, mode_all.now = together(small, rest_all.now, mode_all.now)
    small = sum_steps(small, everyone, slice(2, small_steps - 1))
    rest_all.across()
    grads = mode_all.pairs()
    small, rest_all.now, grads = together(small, rest_all.now, grads)
    small = sum_steps(small, everyone, slice(small_steps - 1, small_steps)).reshape(-1)
    grads += rest_all.pairs()
    loss_sum = small[2 * d + SUM_LOSS]
    valid_count = small[2 * d + SUM_LOSS + 1]
    inverse = 1.0 / valid_count
    bias_grad = small[: 2 * d].reshape(2, d) * inverse
    decomp_grad = small[2 * d : 2 * d + 4 * KERNELS].reshape(2, 2, KERNELS) * inverse
    grad_norm = jnp.sqrt(
        small[2 * d + SUM_LOSS + 2] * inverse * inverse
        + jnp.sum(bias_grad * bias_grad)
        + jnp.sum(decomp_grad * decomp_grad)
    )
    factor = jnp.minimum(1.0, CLIP_NORM / (grad_norm + 1e-06))

    everything = slice(None)

    def band(start, stop):
        return (slice(start, stop), everything)

    both = (everything, everything)
    mode_view = [
        (c, band(h * HEAD_DIM, (h + 1) * HEAD_DIM), (c, h) + both)
        for c in range(2)
        for h in range(own_heads)
    ]
    if len(rest) == 2:
        out_end = hidden_part + out_part
        views = [
            [
                (
                    3,
                    (slice(out_end, out_end + per), slice(n * width, (n + 1) * width)),
                    band(n * per, (n + 1) * per),
                )
                for n in range(ways)
            ],
            [(3, band(hidden_part, out_end), both)],
            mode_view,
            [(2, both, both)],
            [(3, band(0, hidden_part), both)],
        ]
    else:
        views = [[(5, both, both)], [(4, both, both)], mode_view, [(2, both, both)], [(3, both, both)]]

    states = (
        (query_weight, query_first, query_second),
        (out_weight, out_first, out_second),
        (mode_weight, mode_first, mode_second),
        (up_weight, up_first, up_second),
        (down_weight, down_first, down_second),
    )
    news = adam_call(me, (factor * inverse).reshape(1), grads, views, states, (0, 0, 3, 0, 0))
    news += adam_values(bias_pair, bias_grad * factor, bias_first, bias_second)
    news += adam_values(decomp_params, decomp_grad * factor, decomp_first, decomp_second)
    return (loss_sum, valid_count, grad_norm, *news)


def solution(mesh):
    rows = P(("dp", "head"), None)
    down = P("head", None)
    across = P(None, "head")
    modes = P(None, "head", None, None)
    weights = (across,) * 3 + (down,) * 3 + (modes,) * 3 + (across,) * 3 + (down,) * 3 + (P(),) * 6
    sizes = (mesh.shape["dp"], mesh.shape["head"])
    return jax.shard_map(
        partial(on_device, sizes),
        mesh=mesh,
        in_specs=(rows, rows, P(("dp", "head")), rows, down) + weights,
        out_specs=(P(), P(), P()) + weights,
        check_vma=False,
    )
```

```python
from functools import partial
import math

import jax
import jax.numpy as jnp
from jax import lax
from jax.experimental import pallas as pl
from jax.experimental.pallas import tpu as pltpu
from jax.sharding import PartitionSpec as P

MODES = 64
SEQ_LEN = 128
HEAD_DIM = 64
STEP = 10
KERNEL_WIDTHS = (7, 12, 14, 24, 48)
KERNELS = len(KERNEL_WIDTHS)
BETA_ONE = 0.9
BETA_TWO = 0.999
LEARN_RATE = 0.05
EPSILON = 1e-08
DECAY = 0.01
CLIP_NORM = 0.02
LOG2E = math.log2(math.e)
LANES = 128
BF = jnp.bfloat16
F32 = jnp.float32
MIB = 1 << 20
CHUNK = 128
UNROLL = 1

ERF_P = 0.3275911
ERF_A = (0.254829592, -0.284496736, 1.421413741, -1.453152027, 1.061405429)


def dot(a, b, ca=1, cb=0):
    return lax.dot_general(a, b, (((ca,), (cb,)), ((), ())), preferred_element_type=F32)


def cost(microseconds, moved):
    return pl.CostEstimate(
        flops=int(microseconds * 1.1e9), bytes_accessed=int(moved), transcendentals=0
    )


def query_kernel(head_ref, x_ref, b_ref, *refs):
    heads = len(refs) // 2
    x = x_ref[...]
    for r in range(heads):
        bias = b_ref[lax.rem(head_ref[0] + r, heads)]
        refs[heads + r][...] = (dot(x, refs[r][...]) + bias).astype(BF)


def query_call(head, x, bias_row, weights):
    rows, d = x.shape
    heads = len(weights)
    width = weights[0].shape[1]
    step = min(256, rows)
    return pl.pallas_call(
        query_kernel,
        grid=(rows // step,),
        in_specs=[
            pl.BlockSpec(memory_space=pltpu.SMEM),
            pl.BlockSpec((step, d), lambda i: (i, 0)),
            pl.BlockSpec((heads, 1, width), lambda i: (0, 0, 0)),
        ]
        + [pl.BlockSpec((d, width), lambda i: (0, 0)) for _ in weights],
        out_specs=[pl.BlockSpec((step, width), lambda i: (i, 0)) for _ in weights],
        out_shape=[jax.ShapeDtypeStruct((rows, width), BF) for _ in weights],
        compiler_params=pltpu.CompilerParams(vmem_limit_bytes=24 * MIB),
        cost_estimate=cost(2.5, 3e6),
        name="queries",
    )(head, x, bias_row.reshape(heads, 1, width), *weights)


def lane_low(rows):
    return lax.broadcasted_iota(jnp.int32, (rows, LANES), 1) < HEAD_DIM


def mix_blocks(wt_ref, m, count):
    low = lane_low(HEAD_DIM)
    zero = jnp.zeros((HEAD_DIM, LANES), F32)
    left = [
        wt_ref[pl.ds(c * HEAD_DIM * MODES + m, HEAD_DIM, stride=MODES), :] for c in range(2)
    ]
    blocks = []
    for _ in range(count):
        terms = [v.astype(BF).astype(F32) for v in left]
        left = [v - t for v, t in zip(left, terms)]
        real, imag = (
            jnp.concatenate([jnp.where(low, t, zero), jnp.where(low, zero, t)], axis=0)
            for t in terms
        )
        top = jnp.concatenate([real, -imag], axis=1)
        bottom = jnp.concatenate([imag, real], axis=1)
        blocks.append(jnp.concatenate([top, bottom], axis=0).astype(BF))
    return blocks


def pair_width(contexts):
    return 2 if contexts % 2 == 0 else 1


def spectrum_kernel(wt_ref, tf_ref, ti_ref, *refs):
    owners = (len(refs) - 3) // 3
    q_refs, spec_refs = refs[:owners], refs[owners : 3 * owners]
    xs_ref, x_scr, y_scr = refs[3 * owners :]
    run, width = q_refs[0].shape[0], q_refs[0].shape[2]
    half = run // 2
    contexts = owners * run
    pair = pair_width(half)
    low = lane_low(SEQ_LEN)

    for r in range(owners):

        def forward(p, _, r=r):
            cols = jnp.concatenate([q_refs[r][p * pair + k] for k in range(pair)], axis=1)
            res = dot(tf_ref[...], jnp.concatenate([cols, cols], axis=0))
            for k in range(pair):
                part = res[:, k * LANES : (k + 1) * LANES]
                row = (r * run + p * pair + k) * SEQ_LEN
                x_scr[pl.ds(pl.multiple_of(row, SEQ_LEN), SEQ_LEN), :] = jnp.where(
                    low, part[:SEQ_LEN], part[SEQ_LEN:]
                )
            return 0

        lax.fori_loop(0, run // pair, forward, 0, unroll=True)

    def mix(m, _):
        xr = x_scr[pl.ds(m, contexts, stride=SEQ_LEN), :].astype(BF)
        xi = x_scr[pl.ds(MODES + m, contexts, stride=SEQ_LEN), :].astype(BF)
        xs_ref[m] = jnp.concatenate([xr, xi], axis=0)
        x = jnp.concatenate([xr, xi], axis=1)
        main, rest = mix_blocks(wt_ref, m, 2)
        y = dot(x, main, 1, 1) + dot(x, rest, 1, 1)
        y_scr[pl.ds(m, contexts, stride=SEQ_LEN), :] = y[:, :LANES]
        y_scr[pl.ds(MODES + m, contexts, stride=SEQ_LEN), :] = y[:, LANES:]
        return 0

    lax.fori_loop(0, MODES, mix, 0, unroll=16)

    for r in range(owners):
        for number in range(2):
            target = spec_refs[number * owners + r]

            def inverse(p, _, r=r, number=number, target=target):
                parts = []
                for k in range(pair):
                    row = (r * run + number * half + p * pair + k) * SEQ_LEN
                    parts.append(y_scr[pl.ds(pl.multiple_of(row, SEQ_LEN), SEQ_LEN), :])
                cols = jnp.concatenate(parts, axis=1)
                main = cols.astype(BF)
                rest = (cols - main.astype(F32)).astype(BF)
                res = dot(ti_ref[...], jnp.concatenate([main, main, rest], axis=0)).astype(BF)
                for k in range(pair):
                    target[p * pair + k] = res[:, k * LANES : (k + 1) * LANES]
                return 0

            lax.fori_loop(0, half // pair, inverse, 0, unroll=True)


def spectrum_call(queries, wt, tf, ti):
    owners = len(queries)
    run = queries[0].shape[0]
    contexts = owners * run
    out = jax.ShapeDtypeStruct((run // 2, SEQ_LEN, LANES), BF)
    res = pl.pallas_call(
        spectrum_kernel,
        out_shape=[out] * (2 * owners)
        + [jax.ShapeDtypeStruct((MODES, 2 * contexts, LANES), BF)],
        scratch_shapes=[
            pltpu.VMEM((contexts * SEQ_LEN, LANES), F32),
            pltpu.VMEM((contexts * SEQ_LEN, LANES), F32),
        ],
        compiler_params=pltpu.CompilerParams(vmem_limit_bytes=32 * MIB),
        cost_estimate=cost(15, 7e6),
        name="spectrum",
    )(wt, tf, ti, *queries)
    return res[:owners], res[owners : 2 * owners], res[2 * owners]


def query_grad_kernel(wt_ref, tit_ref, tft_ref, *refs):
    owners = (len(refs) - 4) // 3
    d_refs, dq_refs = refs[: 2 * owners], refs[2 * owners : 3 * owners]
    dy_ref, bias_ref, y_scr, x_scr = refs[3 * owners :]
    half = d_refs[0].shape[0]
    run = 2 * half
    contexts = owners * run
    pair = pair_width(half)
    low = lane_low(SEQ_LEN)
    zero = jnp.zeros((SEQ_LEN, LANES), F32)

    for number in range(2):
        for r in range(owners):
            source = d_refs[number * owners + r]

            def forward(p, _, number=number, r=r, source=source):
                cols = jnp.concatenate([source[p * pair + k] for k in range(pair)], axis=1)
                res = dot(tit_ref[...], jnp.concatenate([cols, cols], axis=0))
                for k in range(pair):
                    row = (r * run + number * half + p * pair + k) * SEQ_LEN
                    y_scr[pl.ds(pl.multiple_of(row, SEQ_LEN), SEQ_LEN), :] = res[
                        :, k * LANES : (k + 1) * LANES
                    ]
                return 0

            lax.fori_loop(0, half // pair, forward, 0, unroll=True)

    def mix(m, _):
        yr = y_scr[pl.ds(m, contexts, stride=SEQ_LEN), :].astype(BF)
        yi = y_scr[pl.ds(MODES + m, contexts, stride=SEQ_LEN), :].astype(BF)
        dy = jnp.concatenate([yr, yi], axis=1)
        dy_ref[m] = dy
        dx = dot(dy, mix_blocks(wt_ref, m, 1)[0])
        x_scr[pl.ds(m, contexts, stride=SEQ_LEN), :] = dx[:, :LANES]
        x_scr[pl.ds(MODES + m, contexts, stride=SEQ_LEN), :] = dx[:, LANES:]
        return 0

    lax.fori_loop(0, MODES, mix, 0, unroll=16)
    bias_ref[...] = jnp.zeros_like(bias_ref)

    for r in range(owners):

        def inverse(p, _, r=r):
            parts = []
            for k in range(pair):
                row = (r * run + p * pair + k) * SEQ_LEN
                one = x_scr[pl.ds(pl.multiple_of(row, SEQ_LEN), SEQ_LEN), :]
                parts.append(
                    jnp.concatenate([jnp.where(low, one, zero), jnp.where(low, zero, one)], axis=0)
                )
            cols = jnp.concatenate(parts, axis=1).astype(BF)
            res = dot(tft_ref[...], jnp.concatenate([cols, cols], axis=0)).astype(BF)
            total = jnp.zeros((8, LANES), F32)
            for k in range(pair):
                one = res[:, k * LANES : (k + 1) * LANES]
                dq_refs[r][p * pair + k] = one
                total = total + jnp.sum(one.astype(F32).reshape(SEQ_LEN // 8, 8, LANES), axis=0)
            bias_ref[...] += total
            return 0

        lax.fori_loop(0, run // pair, inverse, 0, unroll=True)


def query_grad_call(first, second, wt, tit, tft, waits):
    owners = len(first)
    run = 2 * first[0].shape[0]
    contexts = owners * run
    whole = pl.BlockSpec(memory_space=pltpu.VMEM)

    def body(*refs):
        at = 3 + 2 * owners
        query_grad_kernel(*refs[:at], *refs[at + len(waits) :])

    res = pl.pallas_call(
        body,
        in_specs=[whole] * (3 + 2 * owners) + [pl.BlockSpec(memory_space=pl.ANY)] * len(waits),
        out_shape=[jax.ShapeDtypeStruct((run, SEQ_LEN, LANES), BF)] * owners
        + [
            jax.ShapeDtypeStruct((MODES, contexts, 2 * LANES), BF),
            jax.ShapeDtypeStruct((8, LANES), F32),
        ],
        scratch_shapes=[
            pltpu.VMEM((contexts * SEQ_LEN, LANES), F32),
            pltpu.VMEM((contexts * SEQ_LEN, LANES), F32),
        ],
        compiler_params=pltpu.CompilerParams(vmem_limit_bytes=32 * MIB),
        cost_estimate=cost(11, 7e6),
        name="query_grads",
    )(wt, tit, tft, *first, *second, *waits)
    return res[:owners], res[owners], res[owners + 1]


def mode_grad_kernel(me_ref, dy_ref, xs_ref, *refs):
    outs = refs[-6:-2]
    dw_scr, sems = refs[-2:]
    pieces, depth = 2 * outs[0].shape[0], outs[0].shape[1]
    total = HEAD_DIM * MODES
    low = lane_low(HEAD_DIM)
    me = me_ref[0]

    def mix(m, _):
        dy = dy_ref[m]
        yr, yi = dy[:, :LANES], dy[:, LANES:]
        right = jnp.concatenate(
            [jnp.concatenate([yr, yi], axis=0), jnp.concatenate([yi, -yr], axis=0)], axis=1
        )
        dw = dot(right, xs_ref[m], 0, 0)
        for c in range(2):
            first = 2 * c * HEAD_DIM
            part = jnp.where(
                low, dw[first : first + HEAD_DIM], dw[first + HEAD_DIM : first + 2 * HEAD_DIM]
            )
            dw_scr[pl.ds(c * total + m, HEAD_DIM, stride=MODES), :] = part
        return 0

    lax.fori_loop(0, MODES, mix, 0, unroll=16)
    copies = []
    for j in range(pieces):
        for c in range(2):
            start = pl.multiple_of(c * total + (me ^ j) * depth, depth)
            copies.append(
                pltpu.make_async_copy(
                    dw_scr.at[pl.ds(start, depth), :],
                    outs[2 * c + (j + 1) % 2].at[j // 2],
                    sems.at[c, j],
                )
            )
    for copy in copies:
        copy.start()
    for copy in copies:
        copy.wait()


def mode_grad_call(me, dy, xs, pieces, waits):
    part = jax.ShapeDtypeStruct((pieces // 2, HEAD_DIM * MODES // pieces, LANES), F32)
    whole = pl.BlockSpec(memory_space=pltpu.VMEM)
    return pl.pallas_call(
        mode_grad_kernel,
        in_specs=[pl.BlockSpec(memory_space=pltpu.SMEM)]
        + [whole] * 2
        + [pl.BlockSpec(memory_space=pl.ANY)] * len(waits),
        out_specs=[pl.BlockSpec(memory_space=pl.ANY)] * 4,
        out_shape=[part] * 4,
        scratch_shapes=[
            pltpu.VMEM((2 * HEAD_DIM * MODES, LANES), F32),
            pltpu.SemaphoreType.DMA((2, pieces)),
        ],
        compiler_params=pltpu.CompilerParams(vmem_limit_bytes=40 * MIB),
        cost_estimate=cost(9, 8e6),
        name="mode_grads",
    )(me, dy, xs, *waits)


SUM_SLOPE = (0, 10)
SUM_OFFSET = (5, 15)
SUM_LOSS = 20
SUM_BIAS = 21
SUM_ROWS = 24


def window_counts(first, last, rows, cols, width):
    lead = width - 1 - (width - 1) // 2
    reach = cols - rows + (lead + 1)
    here = jnp.where(cols < first, 0, jnp.where(cols >= last, width, jnp.clip(reach, 0, width)))
    before = jnp.where(
        cols <= first, 0, jnp.where(cols > last, width, jnp.clip(reach - 1, 0, width))
    )
    return (here - before).astype(F32)


def window_edges(starts, rows):
    s1, s2, s3 = starts
    first = jnp.where(rows >= s3, s3, jnp.where(rows >= s2, s2, jnp.where(rows >= s1, s1, 0)))
    last = jnp.where(
        rows < s1, s1 - 1, jnp.where(rows < s2, s2 - 1, jnp.where(rows < s3, s3 - 1, SEQ_LEN - 1))
    )
    return first, last


def fold(v):
    return jnp.sum(v.reshape(v.shape[0] // 8, 8, v.shape[1]), axis=0)


def local_kernel(*refs, chunk, hidden_width, heads, waits):
    refs = list(refs)

    def take(n):
        taken = refs[:n]
        del refs[:n]
        return taken

    starts_ref, prm_ref, me_ref, x_ref, tgt_ref, val_ref, bias_ref = take(7)
    spec_refs = take(heads)
    packed_refs = take(4)
    take(waits)
    dspec_refs = take(heads)
    act_ref, dhid_ref, low_ref, dfeed_ref, spec_out, dattn_ref, sums_ref = take(7)
    (
        u_scr,
        trend_scr,
        season_scr,
        av1_scr,
        share_scr,
        av2_scr,
        da_scr,
        part_scr,
        g_scr,
        slope_scr,
        a_scr,
        at_scr,
        weights,
        weight_sems,
    ) = refs
    step = pl.program_id(0)
    rows, d = x_ref.shape
    nctx = rows // SEQ_LEN
    out_width = dspec_refs[0].shape[1]
    up_rows = slice(0, hidden_width)
    down_rows = slice(hidden_width, 2 * hidden_width)
    out_rows = slice(2 * hidden_width, 2 * hidden_width + out_width)
    groups = d // LANES
    loops = SEQ_LEN // chunk

    def weight_copies():
        count, shared, part, _ = packed_refs[0].shape
        for number, ref in enumerate(packed_refs):
            group, bit = number // 2, number % 2
            for k in range(count):
                for r in range(shared):
                    row = pl.multiple_of((me_ref[0] ^ (2 * k + bit)) * part, part)
                    yield pltpu.make_async_copy(
                        ref.at[k, r],
                        weights.at[(heads - group * shared - r) % heads, pl.ds(row, part), :],
                        weight_sems.at[number, k * shared + r],
                    )

    @pl.when(step == 0)
    def _():
        for copy in weight_copies():
            copy.start()
        sums_ref[...] = jnp.zeros_like(sums_ref)

    def repeat(body, start):
        if loops == 1:
            return body(0, start)
        return lax.fori_loop(0, loops, body, start, unroll=UNROLL)

    row_ids = lax.broadcasted_iota(jnp.int32, (SEQ_LEN, SEQ_LEN), 0)
    col_ids = lax.broadcasted_iota(jnp.int32, (SEQ_LEN, SEQ_LEN), 1)
    for c in range(nctx):
        starts = [starts_ref[step * nctx + c, k] for k in range(1, 4)]
        first, last = window_edges(starts, row_ids)
        first_t, last_t = window_edges(starts, col_ids)
        for w, width in enumerate(KERNEL_WIDTHS):
            counts = window_counts(first, last, row_ids, col_ids, width).astype(BF)
            a_scr[c, w * SEQ_LEN : (w + 1) * SEQ_LEN, :SEQ_LEN] = counts
            a_scr[c, w * SEQ_LEN : (w + 1) * SEQ_LEN, SEQ_LEN:] = counts
            at_scr[c, :, w * SEQ_LEN : (w + 1) * SEQ_LEN] = window_counts(
                first_t, last_t, col_ids, row_ids, width
            ).astype(BF)

    @pl.when(step == 0)
    def _():
        for copy in weight_copies():
            copy.wait()

    def averages(c, u, av):
        high = u.astype(BF)
        rest = (u - high.astype(F32)).astype(BF)
        av[c] = dot(a_scr[c], jnp.concatenate([high, rest], axis=0))

    spec = jnp.concatenate([ref[...] for ref in spec_refs], axis=1)
    for h in range(heads):
        spec_out[h] = spec_refs[h][...]
    out_all = jnp.concatenate([weights[h, out_rows] for h in range(heads)], axis=0)
    pre = x_ref[...].astype(F32) + (dot(spec, out_all) + bias_ref[...])
    u_scr[...] = pre
    for c in range(nctx):
        averages(c, pre[c * SEQ_LEN : (c + 1) * SEQ_LEN], av1_scr)

    def shares_of(u, avs, layer):
        logits = [
            u * (prm_ref[layer, 0, w] * LOG2E) + prm_ref[layer, 1, w] * LOG2E
            for w in range(KERNELS)
        ]
        top = logits[0]
        for v in logits[1:]:
            top = jnp.maximum(top, v)
        powers = [jnp.exp2(v - top) for v in logits]
        total = powers[0]
        for v in powers[1:]:
            total = total + v
        scale = 1.0 / total
        shares = [v * scale for v in powers]
        trend = shares[0] * avs[0]
        for s, a in zip(shares[1:], avs[1:]):
            trend = trend + s * a
        return shares, trend

    def read_averages(av, c, row, lanes):
        return [
            av[c, pl.ds(w * SEQ_LEN + row, chunk), lanes] * (1.0 / width)
            for w, width in enumerate(KERNEL_WIDTHS)
        ]

    def pull(shares, avs, trend, grad, u, layer, base, c, row, lanes, sums):
        rest = base
        slopes, offsets = [], []
        for w, width in enumerate(KERNEL_WIDTHS):
            d_avg = shares[w] * grad
            da_scr[c, pl.ds(w * SEQ_LEN + row, chunk), lanes] = (d_avg * (1.0 / width)).astype(BF)
            d_logit = d_avg * (avs[w] - trend)
            rest = rest + d_logit * prm_ref[layer, 0, w]
            slopes.append(sums[w] + fold(d_logit * u))
            offsets.append(sums[KERNELS + w] + fold(d_logit))
        return rest, slopes + offsets

    for c in range(nctx):
        for g in range(groups):
            lanes = slice(g * LANES, (g + 1) * LANES)

            def first_pass(r, _, c=c, lanes=lanes):
                row = r * chunk if loops == 1 else pl.multiple_of(r * chunk, chunk)
                at = pl.ds(c * SEQ_LEN + row, chunk)
                u = u_scr[at, lanes]
                avs = read_averages(av1_scr, c, row, lanes)
                shares, trend = shares_of(u, avs, 0)
                for w in range(KERNELS):
                    share_scr[c, pl.ds(w * SEQ_LEN + row, chunk), lanes] = shares[w]
                season = u - trend
                trend_scr[at, lanes] = trend
                season_scr[at, lanes] = season
                low_ref[at, lanes] = season.astype(BF)
                return 0

            repeat(first_pass, 0)

    season_low = low_ref[...]
    feed = jnp.zeros((rows, d), F32)
    for h in range(heads):
        hid = dot(season_low, weights[h, up_rows], 1, 1)
        z = jnp.abs(hid) * (2.0**-0.5)
        t = 1.0 / (1.0 + ERF_P * z)
        e = jnp.exp2(hid * hid * (-0.5 * LOG2E))
        poly = ERF_A[4]
        for coef in ERF_A[3::-1]:
            poly = poly * t + coef
        tail = (0.5 * t) * poly * e
        phi = jnp.where(hid < 0, tail, 1.0 - tail)
        active = (hid * phi).astype(BF)
        slope_scr[h] = phi + hid * e * ((2.0 * math.pi) ** -0.5)
        act_ref[h] = active
        feed = feed + dot(active, weights[h, down_rows])

    pre = season_scr[...] + feed
    g_scr[...] = pre
    for c in range(nctx):
        averages(c, pre[c * SEQ_LEN : (c + 1) * SEQ_LEN], av2_scr)

    for c in range(nctx):
        for g in range(groups):
            lanes = slice(g * LANES, (g + 1) * LANES)

            def second_pass(r, sums, c=c, lanes=lanes):
                row = r * chunk if loops == 1 else pl.multiple_of(r * chunk, chunk)
                at = pl.ds(c * SEQ_LEN + row, chunk)
                u = g_scr[at, lanes]
                avs = read_averages(av2_scr, c, row, lanes)
                shares, trend = shares_of(u, avs, 1)
                misfit = trend_scr[at, lanes] + trend - tgt_ref[at, lanes]
                weighted = val_ref[at, :] * misfit
                grad = 2.0 * weighted
                rest, new = pull(
                    shares, avs, trend, grad, u, 1, jnp.zeros_like(u), c, row, lanes, sums
                )
                part_scr[at, lanes] = rest
                g_scr[at, lanes] = grad
                return tuple(new) + (sums[2 * KERNELS] + fold(weighted * misfit),)

            zeros = tuple(jnp.zeros((8, LANES), F32) for _ in range(2 * KERNELS + 1))
            sums = repeat(second_pass, zeros)
            for k in range(KERNELS):
                sums_ref[SUM_SLOPE[1] + k, :, lanes] += sums[k]
                sums_ref[SUM_OFFSET[1] + k, :, lanes] += sums[KERNELS + k]
            sums_ref[SUM_LOSS, :, lanes] += sums[2 * KERNELS]

    for c in range(nctx):
        at = slice(c * SEQ_LEN, (c + 1) * SEQ_LEN)
        part_scr[at, :] += dot(at_scr[c], da_scr[c])

    d_pre = part_scr[...]
    d_feed = d_pre.astype(BF)
    dfeed_ref[...] = d_feed
    back = d_pre
    for h in range(heads):
        d_hid = (dot(d_feed, weights[h, down_rows], 1, 1) * slope_scr[h]).astype(BF)
        back = back + dot(d_hid, weights[h, up_rows])
        dhid_ref[h] = d_hid
    season_scr[...] = back

    for c in range(nctx):
        for g in range(groups):
            lanes = slice(g * LANES, (g + 1) * LANES)

            def third_pass(r, sums, c=c, lanes=lanes):
                row = r * chunk if loops == 1 else pl.multiple_of(r * chunk, chunk)
                at = pl.ds(c * SEQ_LEN + row, chunk)
                u = u_scr[at, lanes]
                avs = read_averages(av1_scr, c, row, lanes)
                shares = [
                    share_scr[c, pl.ds(w * SEQ_LEN + row, chunk), lanes] for w in range(KERNELS)
                ]
                d_season = season_scr[at, lanes]
                rest, new = pull(
                    shares,
                    avs,
                    trend_scr[at, lanes],
                    g_scr[at, lanes] - d_season,
                    u,
                    0,
                    d_season,
                    c,
                    row,
                    lanes,
                    sums,
                )
                part_scr[at, lanes] = rest
                return tuple(new)

            zeros = tuple(jnp.zeros((8, LANES), F32) for _ in range(2 * KERNELS))
            sums = repeat(third_pass, zeros)
            for k in range(KERNELS):
                sums_ref[SUM_SLOPE[0] + k, :, lanes] += sums[k]
                sums_ref[SUM_OFFSET[0] + k, :, lanes] += sums[KERNELS + k]

    for c in range(nctx):
        at = slice(c * SEQ_LEN, (c + 1) * SEQ_LEN)
        part_scr[at, :] += dot(at_scr[c], da_scr[c])

    d_pre = part_scr[...]
    sums_ref[SUM_BIAS] += fold(d_pre)
    d_attn = d_pre.astype(BF)
    dattn_ref[...] = d_attn
    d_spec = dot(d_attn, out_all, 1, 1).astype(BF)
    for h in range(heads):
        dspec_refs[h][...] = d_spec[:, h * out_width : (h + 1) * out_width]


def up8(n):
    return -(-n // 8) * 8


def local_call(number, spec, waits, starts, prm, me, x, target, valid, bias, packed, hidden):
    rows_half = x.shape[0] // 2
    d = x.shape[1]
    heads = len(spec)
    width = spec[0].shape[1]
    nctx = 2 if rows_half % (2 * SEQ_LEN) == 0 else 1
    rows = nctx * SEQ_LEN
    steps = rows_half // rows
    smem = pl.BlockSpec(memory_space=pltpu.SMEM)
    whole = pl.BlockSpec(memory_space=pltpu.VMEM)
    anywhere = pl.BlockSpec(memory_space=pl.ANY)
    averages = (nctx, KERNELS * SEQ_LEN, d)
    count, shared, part, _ = packed[0].shape

    def row_block(columns, half=0):
        return pl.BlockSpec((rows, columns), lambda i: (half * steps + i, 0))

    def head_block(columns):
        return pl.BlockSpec((heads, rows, columns), lambda i: (0, i, 0))

    ctx_half = starts.shape[0] // 2
    res = pl.pallas_call(
        partial(local_kernel, chunk=CHUNK, hidden_width=hidden, heads=heads, waits=len(waits)),
        grid=(steps,),
        in_specs=[smem] * 3
        + [row_block(d, number), row_block(d, number), row_block(1, number), whole]
        + [row_block(width)] * heads
        + [anywhere] * (len(packed) + len(waits)),
        out_specs=[row_block(width)] * heads
        + [head_block(hidden), head_block(hidden), row_block(d), row_block(d)]
        + [head_block(width), row_block(d)]
        + [pl.BlockSpec((SUM_ROWS, 8, d), lambda i: (0, 0, 0))],
        out_shape=[jax.ShapeDtypeStruct((rows_half, width), BF)] * heads
        + [jax.ShapeDtypeStruct((heads, rows_half, hidden), BF)] * 2
        + [jax.ShapeDtypeStruct((rows_half, d), BF)] * 2
        + [
            jax.ShapeDtypeStruct((heads, rows_half, width), BF),
            jax.ShapeDtypeStruct((rows_half, d), BF),
            jax.ShapeDtypeStruct((SUM_ROWS, 8, d), F32),
        ],
        scratch_shapes=[
            pltpu.VMEM((rows, d), F32),
            pltpu.VMEM((rows, d), F32),
            pltpu.VMEM((rows, d), F32),
            pltpu.VMEM(averages, F32),
            pltpu.VMEM(averages, F32),
            pltpu.VMEM(averages, F32),
            pltpu.VMEM(averages, BF),
            pltpu.VMEM((rows, d), F32),
            pltpu.VMEM((rows, d), F32),
            pltpu.VMEM((heads, rows, hidden), F32),
            pltpu.VMEM((nctx, KERNELS * SEQ_LEN, 2 * SEQ_LEN), BF),
            pltpu.VMEM((nctx, SEQ_LEN, KERNELS * SEQ_LEN), BF),
            pltpu.VMEM((heads, len(packed) * count // 2 * part, d), BF),
            pltpu.SemaphoreType.DMA((len(packed), count * shared)),
        ],
        compiler_params=pltpu.CompilerParams(vmem_limit_bytes=56 * MIB),
        cost_estimate=cost(5, 4e6),
        name="local_layer",
    )(
        starts[number * ctx_half : (number + 1) * ctx_half],
        prm,
        me,
        x,
        target,
        valid,
        bias,
        *spec,
        *packed,
        *waits,
    )
    return res[:heads], res[heads:-1], res[-1]


def outer_kernel(me_ref, *refs, halves, outs, waits):
    scratch = refs[-1]
    ins = list(refs[: 2 * sum(halves)])
    targets = list(refs[2 * sum(halves) + waits : -1])
    for count, cuts in zip(halves, outs):
        total = None
        for _ in range(count):
            left, right = (r[0] if len(r.shape) == 3 else r[...] for r in ins[:2])
            del ins[:2]
            term = dot(left, right, 0, 0)
            total = term if total is None else total + term
        rows, columns = total.shape
        lanes = slice(0, columns)
        scratch[:rows, lanes] = total
        offset = 0
        for cut in cuts:
            send, keep = targets[:2]
            del targets[:2]
            pieces = 2 * send.shape[0]
            size = rows // pieces
            for j in range(pieces):
                target = send if j % 2 else keep
                start = (me_ref[0] ^ j) * size + offset
                if cut % 8 == 0:
                    part = scratch[pl.ds(pl.multiple_of(start, 8), cut), lanes]
                    target[j // 2, 0] = part.astype(target.dtype)
                else:
                    row = lax.broadcasted_iota(jnp.int32, (target.shape[2], 1), 0)
                    part = jnp.zeros((target.shape[2], columns), F32)
                    for i in range(cut):
                        part = jnp.where(row == i, scratch[pl.ds(start + i, 1), lanes], part)
                    target[j // 2, 0] = part.astype(target.dtype)
            offset += cut


def outer_call(me, products, outs, pieces, name, waits=()):
    heads = next(a.shape[0] for p in products for pair in p for a in pair if a.ndim == 3)
    operands = [a for p in products for pair in p for a in pair]

    def spec(a):
        if a.ndim == 3:
            return pl.BlockSpec((1,) + a.shape[1:], lambda h: (h, 0, 0))
        return pl.BlockSpec(a.shape, lambda h: (0, 0))

    shapes = []
    for p, cuts in zip(products, outs):
        for cut, kind in cuts:
            tail = (cut if cut % 8 == 0 else 16, p[0][1].shape[-1])
            shapes += [
                jax.ShapeDtypeStruct((pieces // 2, heads) + tail, t) for t in (kind, F32)
            ]
    rows = max(pair[0].shape[-1] for p in products for pair in p)
    columns = max(pair[1].shape[-1] for p in products for pair in p)
    res = pl.pallas_call(
        partial(
            outer_kernel,
            halves=[len(p) for p in products],
            outs=[[cut for cut, _ in cuts] for cuts in outs],
            waits=len(waits),
        ),
        grid=(heads,),
        in_specs=[pl.BlockSpec(memory_space=pltpu.SMEM)]
        + [spec(a) for a in operands]
        + [pl.BlockSpec(memory_space=pl.ANY)] * len(waits),
        out_specs=[
            pl.BlockSpec((s.shape[0], 1) + s.shape[2:], lambda h: (0, h, 0, 0)) for s in shapes
        ],
        out_shape=shapes,
        scratch_shapes=[pltpu.VMEM((rows, columns), F32)],
        compiler_params=pltpu.CompilerParams(vmem_limit_bytes=60 * MIB),
        cost_estimate=cost(0.3, 1e5),
        name=name,
    )(me, *operands, *waits)
    return [(res[2 * k], res[2 * k + 1]) for k in range(len(res) // 2)]


def adam_values(weight, gradient, first, second):
    m = BETA_ONE * first + (1.0 - BETA_ONE) * gradient
    v = BETA_TWO * second + (1.0 - BETA_TWO) * gradient * gradient
    first_hat = m * (1.0 / (1.0 - BETA_ONE**STEP))
    second_hat = v * (1.0 / (1.0 - BETA_TWO**STEP))
    return (
        weight - LEARN_RATE * (first_hat / (jnp.sqrt(second_hat) + EPSILON) + DECAY * weight),
        m,
        v,
    )


def adam_kernel(me_ref, scale_ref, *refs, views, leads, grads):
    scale = scale_ref[0]
    count = len(views)
    pairs = refs[: 2 * grads]
    states = refs[2 * grads : 2 * grads + 3 * count]
    outs = refs[2 * grads + 3 * count : 2 * grads + 6 * count]
    chosen = refs[2 * grads + 6 * count :]
    other = (pl.program_id(0) ^ me_ref[0]) & 1

    @pl.when(other == 0)
    def _():
        for k in range(grads):
            chosen[k][...] = pairs[2 * k][0]

    @pl.when(other == 1)
    def _():
        for k in range(grads):
            chosen[k][...] = pairs[2 * k + 1][0]

    for k, parts in enumerate(views):
        lead = leads[k]
        for which, source, place in parts:
            ins = [r.at[lead][place] for r in states[3 * k : 3 * k + 3]]
            g = chosen[which][source] * scale
            new = adam_values(ins[0], g, ins[1], ins[2])
            for r, value in zip(outs[3 * k : 3 * k + 3], new):
                r.at[lead][place] = value


def adam_call(me, scale, grads, views, states, axes):
    pieces = 2 * grads[0][0].shape[0]
    specs, out_specs, operands, shapes, leads = [], [], [], [], []
    for pair in grads:
        zeros = (0,) * (pair[0].ndim - 1)
        for grad in pair:
            specs.append(
                pl.BlockSpec(
                    (1,) + grad.shape[1:],
                    lambda i, me_ref, z=zeros: (lax.div(i ^ me_ref[0], 2),) + z,
                )
            )
            operands.append(grad)
    for group, axis in zip(states, axes):
        shape = group[0].shape
        size = shape[axis] // pieces
        direct = size % (LANES if axis == len(shape) - 1 else 8) == 0
        if not direct:
            shape = shape[:axis] + (pieces, size) + shape[axis + 1 :]
        block = shape[:axis] + (size if direct else 1,) + shape[axis + 1 :]
        leads.append((slice(None),) * axis + ((slice(None),) if direct else (0,)))
        for state in group:
            spec = pl.BlockSpec(
                block,
                lambda i, me_ref, a=axis, n=len(shape): (0,) * a + (i,) + (0,) * (n - a - 1),
            )
            specs.append(spec)
            out_specs.append(spec)
            operands.append(state.reshape(shape))
            shapes.append(jax.ShapeDtypeStruct(shape, F32))
    news = pl.pallas_call(
        partial(adam_kernel, views=views, leads=leads, grads=len(grads)),
        grid_spec=pltpu.PrefetchScalarGridSpec(
            num_scalar_prefetch=1,
            grid=(pieces,),
            in_specs=[pl.BlockSpec(memory_space=pltpu.SMEM)] + specs,
            out_specs=out_specs,
            scratch_shapes=[pltpu.VMEM(pair[0].shape[1:], F32) for pair in grads],
        ),
        out_shape=shapes,
        compiler_params=pltpu.CompilerParams(vmem_limit_bytes=60 * MIB),
        cost_estimate=cost(15, 48e6),
        name="adam",
    )(me, scale, *operands)
    return [n.reshape(states[k // 3][0].shape) for k, n in enumerate(news)]


def swap(value, axis, size, bit):
    return lax.ppermute(value, axis, [(i, i ^ (1 << bit)) for i in range(size)])


def split_add(items):
    specs, operands, shapes, out_specs = [], [], [], []
    half = items[0][0].shape[0] // 2
    splits = 4
    for kept, got, lowest in items:
        cut = kept.shape[2] % (16 * splits) == 0
        block = (1, kept.shape[1], kept.shape[2] // (splits if cut else 1), kept.shape[3])

        def at(index, cut=cut):
            return lambda i, s: (index(i), 0, s if cut else 0, 0)

        away = at((lambda i: 2 * i + 1) if lowest else (lambda i: half + i))
        stay = at((lambda i: 2 * i) if lowest else (lambda i: i))
        for index, kind in ((away, got.dtype), (stay, F32)):
            specs += [pl.BlockSpec(block, index)] * 2
            operands += [kept, got]
            out_specs.append(pl.BlockSpec(block, at(lambda i: i)))
            shapes.append(jax.ShapeDtypeStruct((half,) + kept.shape[1:], kind))

    def body(*refs):
        outs = refs[len(operands) :]
        for k, out in enumerate(outs):
            out[...] = (refs[2 * k][...] + refs[2 * k + 1][...].astype(F32)).astype(out.dtype)

    res = pl.pallas_call(
        body,
        grid=(half, splits),
        in_specs=specs,
        out_specs=out_specs,
        out_shape=shapes,
        compiler_params=pltpu.CompilerParams(vmem_limit_bytes=24 * MIB),
        cost_estimate=cost(0.3, 1e5),
        name="split_add",
    )(*operands)
    return [(res[2 * k], res[2 * k + 1]) for k in range(len(items))]


class Reduction:
    def __init__(self, pairs, orders, size):
        self.size = size
        self.orders = [list(order) for order in orders]
        self.lowest = [order == sorted(order) for order in orders]
        self.kept = [keep for _, keep in pairs]
        self.got = [swap(send, "dp", size, 0) for send, _ in pairs]

    def split(self):
        items = list(zip(self.kept, self.got, self.lowest))
        pairs = split_add(items)
        self.kept = [keep for _, keep in pairs]
        self.got = [
            swap(send, "dp", self.size, order.pop(0))
            for (send, _), order in zip(pairs, self.orders)
        ]

    def rest(self):
        while self.orders[0]:
            self.split()
        return [keep[0] + got[0].astype(F32) for keep, got in zip(self.kept, self.got)]


class Gathering:
    def __init__(self, pieces, orders, size):
        self.size = size
        self.now = list(pieces)
        self.shapes = [p.shape for p in pieces]
        self.orders = [list(order) for order in orders]
        self.have = [[] for _ in pieces]

    def start(self):
        self.other = [
            swap(now, "dp", self.size, order[0]) for now, order in zip(self.now, self.orders)
        ]

    def finish(self):
        for k, order in enumerate(self.orders):
            bit = order.pop(0)
            at = len([b for b in self.have[k] if b > bit])
            self.now[k] = jnp.stack([self.now[k], self.other[k]], axis=at)
            self.have[k] = sorted(self.have[k] + [bit], reverse=True)

    def double(self):
        self.start()
        self.finish()

    def across(self):
        while self.orders[0]:
            self.double()

    def pairs(self):
        self.across()
        own = [n.reshape((self.size // 2,) + s) for n, s in zip(self.now, self.shapes)]
        return [(n, swap(n, "dp", self.size, 0)) for n in own]


def together(*groups):
    flat, tree = jax.tree.flatten(groups)
    return jax.tree.unflatten(tree, lax.optimization_barrier(flat))


def sum_steps(value, sizes, steps):
    every = [(axis, size, bit) for axis, size in sizes for bit in range(size.bit_length() - 1)]
    for axis, size, bit in every[steps]:
        value = value + swap(value, axis, size, bit)
    return value


def split_low(table):
    high = lax.reduce_precision(table, 8, 7)
    return high.astype(BF), (table - high).astype(BF)


def spectral_tables(mode_index):
    heads = mode_index.shape[0]
    steps = jnp.arange(SEQ_LEN, dtype=jnp.int32)
    angles = (mode_index[:, :, None] * steps % SEQ_LEN).astype(F32) * (2.0 * math.pi / SEQ_LEN)
    ahead = jnp.concatenate([jnp.cos(angles), -jnp.sin(angles)], axis=1)
    if heads == 1:
        ahead = jnp.concatenate([ahead, jnp.zeros_like(ahead)], axis=0)
    ahead = ahead.reshape(2 * SEQ_LEN, SEQ_LEN)
    orders = jnp.arange(MODES, dtype=jnp.int32)
    angles = (steps[:, None] * orders % SEQ_LEN).astype(F32) * (2.0 * math.pi / SEQ_LEN)
    weights = jnp.where(orders == 0, 1.0, 2.0).astype(F32) / SEQ_LEN
    back = jnp.concatenate([jnp.cos(angles) * weights, -jnp.sin(angles) * weights], axis=1)
    tables = [jnp.concatenate(split_low(t), axis=1) for t in (ahead, back, back.T, ahead.T)]
    tables[1] = jnp.concatenate([tables[1], tables[1][:, :SEQ_LEN]], axis=1)
    return tables


def on_device(
    sizes,
    series,
    target,
    valid,
    window_id,
    mode_index,
    query_weight,
    query_first,
    query_second,
    out_weight,
    out_first,
    out_second,
    mode_weight,
    mode_first,
    mode_second,
    up_weight,
    up_first,
    up_second,
    down_weight,
    down_first,
    down_second,
    bias_pair,
    bias_first,
    bias_second,
    decomp_params,
    decomp_first,
    decomp_second,
):
    ndp, nhead = sizes
    bits = ndp.bit_length() - 1
    order_a = list(range(1, bits))
    order_b = order_a[::-1]
    dp = lax.axis_index("dp")
    head = lax.axis_index("head")
    me = dp.astype(jnp.int32).reshape(1)
    rows, d = series.shape
    own_heads = mode_index.shape[0]
    width = query_weight.shape[1]
    hidden = up_weight.shape[1]

    everyone = (("dp", ndp), ("head", nhead))
    place = jnp.concatenate([me, head.astype(jnp.int32).reshape(1)])

    def shift(v, r):
        return lax.ppermute(v, "head", [(i, (i + r) % nhead) for i in range(nhead)])

    def exchange(v):
        return lax.all_to_all(v, "head", 0, 0, tiled=True)

    def wide(v):
        pad = LANES - v.shape[-1]
        return jnp.pad(v, [(0, 0)] * (v.ndim - 1) + [(0, pad)]) if pad else v

    query_low = query_weight.astype(BF)
    query_parts = [query_low] + [shift(query_low, r) for r in range(1, nhead)]
    packed = jnp.concatenate(
        [w.astype(BF) for w in (up_weight.T, down_weight, out_weight)], axis=0
    )
    part = -(-packed.shape[0] // (16 * ndp)) * 16
    packed = jnp.pad(packed, ((0, part * ndp - packed.shape[0]), (0, 0)))
    packed = lax.dynamic_slice_in_dim(packed, dp * part, part, 0)
    packed = [packed] + [shift(packed, r) for r in range(1, nhead)]

    tf, ti, tit, tft = spectral_tables(mode_index)
    wt = mode_weight.reshape(2, own_heads * HEAD_DIM, HEAD_DIM * MODES).transpose(0, 2, 1)
    wt = wide(wt).reshape(2 * HEAD_DIM * MODES, LANES)

    def rows_of(v):
        return v[:, :, :width].reshape(-1, width)

    def contexts_of(v):
        return wide(v.reshape(-1, SEQ_LEN, width))

    def send(parts, way=1):
        return [parts[0]] + [shift(parts[r], way * r) for r in range(1, nhead)]

    starts = jnp.sum(window_id[:, None, :] < jnp.arange(5)[None, :, None], axis=2).astype(jnp.int32)
    valid_float = valid.astype(F32)
    valid_rows = valid_float[:, None]
    query_parts, wt, tf, ti, tit, tft, starts, valid_rows = together(
        query_parts, wt, tf, ti, tit, tft, starts, valid_rows
    )

    query_parts = [query_parts[-r % nhead] for r in range(nhead)]
    queries = query_call(place[1:], series, bias_pair[0], query_parts)
    queries = send(queries)
    queries[1], packed = together(queries[1], packed)
    packed = [jnp.stack(packed[: nhead // 2]), jnp.stack(packed[nhead // 2 :])]
    packed = Gathering(packed, [order_a, order_b], ndp)
    packed.start()
    queries, packed.other = together(queries, packed.other)
    packed.finish()
    packed.start()
    first, second, modes_in = spectrum_call([contexts_of(q) for q in queries], wt, tf, ti)
    first, second, packed.other = together(first, second, packed.other)
    packed.finish()
    packed = [half for pair in packed.pairs() for half in pair]
    first = send([rows_of(v) for v in first], -1)
    first, second = together(first, second)
    second = send([rows_of(v) for v in second], -1)

    half_call = partial(
        local_call,
        starts=starts,
        prm=decomp_params,
        me=me,
        x=series,
        target=target,
        valid=valid_rows,
        bias=bias_pair[1:],
        packed=packed,
        hidden=hidden,
    )
    d_first, kept_first, sums_first = half_call(0, first, [])
    d_first = send(d_first)
    d_second, kept_second, sums = half_call(1, second, [])
    d_second = send(d_second)
    sums = jnp.sum(sums + sums_first, axis=1)

    hidden_part, out_part = hidden // ndp, width // ndp
    both_halves = list(zip(kept_first, kept_second))
    active, d_hidden, season, d_feed, spectrum, d_attention = both_halves
    first_cut = hidden_part // 4 if hidden_part % 64 == 0 else 0
    down_cuts = [(c, F32) for c in (first_cut, hidden_part - first_cut) if c]
    layer = outer_call(
        me,
        [
            list(zip(season, d_hidden)),
            list(zip(active, d_feed)),
            list(zip(spectrum, d_attention)),
        ],
        [[(d // ndp, BF)], down_cuts, [(out_part, F32)]],
        ndp,
        "layer_grads",
        d_first[1:],
    )
    layer = Reduction(layer, ([order_a] * 2 + [order_b] * 2)[: len(layer)], ndp)
    layer.split()

    d_queries, d_modes, bias_part = query_grad_call(
        [contexts_of(v) for v in d_first],
        [contexts_of(v) for v in d_second],
        wt,
        tit,
        tft,
        layer.kept,
    )
    d_queries = send([rows_of(v) for v in d_queries], -1)
    layer.split()
    mode_parts = mode_grad_call(me, d_modes, modes_in, ndp, layer.kept)
    mode_parts = [m.reshape(ndp // 2, nhead, -1, LANES) for m in mode_parts]
    d_queries, mode_parts = together(d_queries, mode_parts)
    query = outer_call(
        me,
        [[(series, jnp.stack(d_queries))]],
        [[(d // ndp, BF)]],
        ndp,
        "query_weight_grads",
    )
    query = Reduction(query, [order_a], ndp)
    query.split()
    modes = Reduction([mode_parts[:2], mode_parts[2:]], [order_a, order_b], ndp)
    query.got, modes.got = together(query.got, modes.got)
    modes.split()

    def over_heads(v, kind=F32):
        parts = send([v[r].astype(kind) for r in range(nhead)])
        return sum([p.astype(F32) for p in parts[1:]], v[0])

    lanes = HEAD_DIM * MODES // ndp
    up_piece, *down_pieces, out_piece = layer.rest()
    down_piece = over_heads(jnp.concatenate([*down_pieces, out_piece], axis=1))
    down_piece, out_piece = down_piece[:hidden_part], down_piece[hidden_part:][:out_part]
    up_piece = over_heads(up_piece, BF)
    (query_piece,) = [over_heads(v, BF) for v in query.rest()]
    mode_pieces = modes.rest()
    mode_pieces = [v.reshape(lanes, LANES).T[: own_heads * HEAD_DIM] for v in mode_pieces]
    mode_all = Gathering(mode_pieces, [order_b, order_a], ndp)
    mode_all.across()
    (up_piece, down_piece, out_piece, query_piece), mode_all.now = together(
        (up_piece, down_piece, out_piece, query_piece), mode_all.now
    )

    bias_zero = lax.dynamic_update_slice_in_dim(
        jnp.zeros((d,), F32), jnp.sum(bias_part, axis=0)[:width], head * width, 0
    )
    squares = sum(
        jnp.sum(p * p) for p in (query_piece, *mode_pieces, up_piece, down_piece, out_piece)
    )
    small = jnp.concatenate(
        [
            bias_zero,
            sums[SUM_BIAS],
            jnp.sum(sums[:SUM_BIAS], axis=1),
            jnp.stack([jnp.sum(valid_float), squares]),
        ]
    )
    small = jnp.pad(small, (0, -small.shape[0] % LANES)).reshape(-1, LANES)
    small_steps = (ndp * nhead).bit_length() - 1
    small = sum_steps(small, everyone, slice(0, 2))

    if HEAD_DIM * MODES // ndp == d and hidden == d and out_part % 8 == 0:
        ways = d // width
        per = d // ndp // ways
        query_flat = query_piece.reshape(ways, per, width).transpose(1, 0, 2).reshape(per, d)
        rest = [up_piece, jnp.concatenate([down_piece, out_piece, query_flat], axis=0)]
    else:
        rest = [up_piece, down_piece, out_piece, query_piece]
    rest_all = Gathering(rest, [order_b, order_a, order_b, order_a][: len(rest)], ndp)
    rest_all.double()
    small, rest_all.now, mode_all.now = together(small, rest_all.now, mode_all.now)
    small = sum_steps(small, everyone, slice(2, small_steps - 1))
    rest_all.across()
    grads = mode_all.pairs()
    small, rest_all.now, grads = together(small, rest_all.now, grads)
    small = sum_steps(small, everyone, slice(small_steps - 1, small_steps)).reshape(-1)
    grads += rest_all.pairs()
    loss_sum = small[2 * d + SUM_LOSS]
    valid_count = small[2 * d + SUM_LOSS + 1]
    inverse = 1.0 / valid_count
    bias_grad = small[: 2 * d].reshape(2, d) * inverse
    decomp_grad = small[2 * d : 2 * d + 4 * KERNELS].reshape(2, 2, KERNELS) * inverse
    grad_norm = jnp.sqrt(
        small[2 * d + SUM_LOSS + 2] * inverse * inverse
        + jnp.sum(bias_grad * bias_grad)
        + jnp.sum(decomp_grad * decomp_grad)
    )
    factor = jnp.minimum(1.0, CLIP_NORM / (grad_norm + 1e-06))

    everything = slice(None)

    def band(start, stop):
        return (slice(start, stop), everything)

    both = (everything, everything)
    mode_view = [
        (c, band(h * HEAD_DIM, (h + 1) * HEAD_DIM), (c, h) + both)
        for c in range(2)
        for h in range(own_heads)
    ]
    if len(rest) == 2:
        out_end = hidden_part + out_part
        views = [
            [
                (
                    3,
                    (slice(out_end, out_end + per), slice(n * width, (n + 1) * width)),
                    band(n * per, (n + 1) * per),
                )
                for n in range(ways)
            ],
            [(3, band(hidden_part, out_end), both)],
            mode_view,
            [(2, both, both)],
            [(3, band(0, hidden_part), both)],
        ]
    else:
        views = [[(5, both, both)], [(4, both, both)], mode_view, [(2, both, both)], [(3, both, both)]]

    states = (
        (query_weight, query_first, query_second),
        (out_weight, out_first, out_second),
        (mode_weight, mode_first, mode_second),
        (up_weight, up_first, up_second),
        (down_weight, down_first, down_second),
    )
    news = adam_call(me, (factor * inverse).reshape(1), grads, views, states, (0, 0, 3, 0, 0))
    news += adam_values(bias_pair, bias_grad * factor, bias_first, bias_second)
    news += adam_values(decomp_params, decomp_grad * factor, decomp_first, decomp_second)
    return (loss_sum, valid_count, grad_norm, *news)


def solution(mesh):
    rows = P(("dp", "head"), None)
    down = P("head", None)
    across = P(None, "head")
    modes = P(None, "head", None, None)
    weights = (across,) * 3 + (down,) * 3 + (modes,) * 3 + (across,) * 3 + (down,) * 3 + (P(),) * 6
    sizes = (mesh.shape["dp"], mesh.shape["head"])
    return jax.shard_map(
        partial(on_device, sizes),
        mesh=mesh,
        in_specs=(rows, rows, P(("dp", "head")), rows, down) + weights,
        out_specs=(P(), P(), P()) + weights,
        check_vma=False,
    )
```
